32 devices in a mesh: grp: 2 (over y), seq: 4 (over x, core), sub: 4 (over z).
Axes of the slice: x: 2, y: 2, z: 4, core: 2. Of those that a mesh axis runs over, the one named last changes fastest.
Arguments:
- events: bfloat16 [4096, 1024], P(('grp', 'seq', 'sub')), parts along dimension 0, may hold values from -36 to 36
- offsets: int32 [4096], P(('grp', 'seq', 'sub')), parts along dimension 0, may hold values from 0 to 2047
- cotangent: bfloat16 [4096, 1024], P(('grp', 'seq', 'sub')), parts along dimension 0, may hold values from -6 to 6
- query_weight: bfloat16 [1024, 1024], P('sub'), may hold values from -0.1875 to 0.1875
- key_weight: bfloat16 [1024, 1024], P('sub'), may hold values from -0.1875 to 0.1875
- value_weight: bfloat16 [1024, 1024], P('sub'), may hold values from -0.1875 to 0.1875
- omega: bfloat16 [8, 128, 256], replicated, may hold values from -0.5 to 0.5
Outputs:
- grad_events: bfloat16 [4096, 1024], P(('grp', 'seq', 'sub')), parts along dimension 0
The draws below stay inside these ranges and needn't reach their ends.
There are 2 independent parts, one for each index of `grp`. The reference program is written for one: setup_inputs(seed, part) draws one part's arguments, and reference() takes and returns one part's arrays. A program takes and returns all parts, laid end to end along the dimension named above; an argument that names none is the same for every part. Nothing has to cross between parts.
All inputs are finite; a program needn't handle non-finite values.
Results may differ from the reference program's by a relative error of at most 0.012.
Values may be sent and summed in bfloat16 or wider, within the bound.
No kernel may reach another device: no remote copies, remote signals or barrier semaphores. Data moves between devices by JAX's collectives and lax.ppermute only.
A program may use at most 64 MiB of HBM per device.

```python
import math
import jax
import jax.numpy as jnp
from jax import lax

D = 1024
H = 8
M = 256
TOK_DEV = 128
HD = 128
TOKENS = 2048
N_SUB = 4


def draw_events(key, part):
    block_count = TOKENS // TOK_DEV
    ranks = jax.random.permutation(jax.random.fold_in(key, 11), block_count).astype(jnp.float32)
    scales = 0.5 * jnp.exp(ranks / max(block_count - 1, 1) * jnp.log(12.0))
    noise_key = jax.random.fold_in(key, 12)
    noise = jnp.clip(jax.random.normal(noise_key, (block_count, TOK_DEV, D), jnp.float32), -6.0, 6.0)
    values = noise * scales[:, None, None]
    return values.reshape(TOKENS, D).astype(jnp.bfloat16)


def plant(array, stream_key, smallest, top_value):
    longest = array.shape.index(max(array.shape))
    spots = []
    for shift in (0, 1):
        where = [jax.random.randint(jax.random.fold_in(stream_key, axis), (), 0, length) for axis, length in enumerate(array.shape)]
        where[longest] = (where[longest] + shift) % array.shape[longest]
        spots.append(tuple(where))
    return array.at[spots[0]].set(smallest).at[spots[1]].set(top_value)


def levels(rng, extent, split, least, high):
    def one(axis_at, blocks):
        draws = jax.random.uniform(jax.random.fold_in(jax.random.fold_in(rng, 6), axis_at), (blocks,), jnp.float32, least / len(split), high / len(split))
        return jnp.repeat(jnp.exp(draws), extent[axis_at] // blocks).reshape((-1,) + (1,) * (len(extent) - axis_at - 1))

    factor_of = one(*split[0])
    for cut in split[1:]:
        factor_of = factor_of * one(*cut)
    return factor_of


def bell_draw(rng, extent, spread, reach, pieces=(), held_as=jnp.bfloat16):
    entries = spread * jax.random.normal(rng, extent, jnp.float32)
    if pieces:
        entries = entries * levels(rng, extent, pieces, -0.22, 0.18)
    return jnp.clip(entries, -reach, reach).astype(held_as)


def setup_inputs(seed: int = 0, part: int = 0) -> dict:
    keys = jax.random.split(jax.random.key(seed), 8)
    own_keys = jax.random.split(jax.random.fold_in(keys[7], part), 8)
    return {
        "events": draw_events(jax.random.fold_in(jax.random.fold_in(keys[7], part), 71), part),
        "offsets": plant(jax.random.randint(own_keys[1], (TOKENS,), 0, 2048), jax.random.fold_in(own_keys[1], 1), 0, 2047).astype(jnp.int32),
        "cotangent": bell_draw(own_keys[2], (TOKENS, D), 1.0, 6.0, ((0, 16),)),
        "query_weight": bell_draw(keys[3], (D, D), D ** -0.5, 0.1875, ((0, 4),)),
        "key_weight": bell_draw(keys[4], (D, D), D ** -0.5, 0.1875, ((0, 4),)),
        "value_weight": bell_draw(keys[5], (D, D), D ** -0.5, 0.1875, ((0, 4),)),
        "omega": bell_draw(keys[6], (H, HD, M), HD ** -0.5, 0.5),
    }


def encode(events, offsets):
    half_width = events.shape[1] // 2
    indices = jnp.arange(half_width, dtype=jnp.float32)
    frequency = jnp.exp(indices * (-2.0 * math.log(10000.0) / events.shape[1]))
    angles = offsets.astype(jnp.float32)[:, None] * frequency[None, :]
    encoding = jnp.concatenate([jnp.sin(angles), jnp.cos(angles)], axis=1)
    return (events.astype(jnp.float32) + encoding).astype(jnp.bfloat16)

def project(inputs, weight):
    return jnp.dot(inputs, weight, preferred_element_type=jnp.float32).astype(jnp.bfloat16)

def reference(events, offsets, cotangent, query_weight, key_weight, value_weight, omega):
    widened_rows = jnp.float32
    inputs = encode(events, offsets)
    queries = project(inputs, query_weight)
    key_act = project(inputs, key_weight)
    value_act = project(inputs, value_weight)
    block_rows = TOK_DEV * N_SUB
    block_count = TOKENS // block_rows
    omega_wide = omega.astype(widened_rows)
    loss_scale = math.sqrt(TOKENS)

    def as_blocks(matrix):
        return matrix.reshape(block_count, block_rows, H, D // H)

    def featurize(acts):
        pre_act = jnp.einsum('thd,hdm->thm', acts.astype(widened_rows), omega_wide)
        return (pre_act, jax.nn.softplus(pre_act).astype(jnp.bfloat16))

    def add_keys(running_state, block_pair):
        key_blk, value_block = block_pair
        _, key_feature_map = featurize(key_blk)
        key_widened = key_feature_map.astype(widened_rows)
        state_digest = running_state[0] + jnp.einsum('reb,rec->ebc', key_widened, value_block.astype(widened_rows))
        return ((state_digest, running_state[1] + lax.optimization_barrier(jnp.sum(key_widened, axis=0))), None)
    starting = (jnp.zeros((H, M, D // H), widened_rows), jnp.zeros((H, M), widened_rows))
    (state_digest, key_total), _ = lax.scan(add_keys, starting, (as_blocks(key_act), as_blocks(value_act)))
    digest_halves = state_digest.astype(jnp.bfloat16)
    total_half = key_total.astype(jnp.bfloat16)

    def query_side(query_blk, upstream_blk):
        query_pre, query_feature_map = featurize(query_blk)
        query_widened = query_feature_map.astype(widened_rows)
        numerator = jnp.einsum('xls,lsk->xlk', query_widened, digest_halves.astype(widened_rows))
        denom = jnp.einsum('thm,hm->th', query_widened, total_half.astype(widened_rows))
        attended = numerator / denom[..., None]
        upstream = upstream_blk.astype(widened_rows) * loss_scale
        scaled_grad = upstream / denom[..., None]
        norm_grad = -lax.optimization_barrier(jnp.sum(scaled_grad * attended, axis=-1))
        return (query_pre, query_feature_map, scaled_grad.astype(jnp.bfloat16), norm_grad, norm_grad.astype(jnp.bfloat16))

    def add_queries(running_state, block_pair):
        _, query_feature_map, scaled_halves, _, norm_half = query_side(block_pair[0], block_pair[1])
        query_widened = query_feature_map.astype(widened_rows)
        gradient_summed = running_state[0] + jnp.einsum('reb,rec->ebc', query_widened, scaled_halves.astype(widened_rows))
        total_sum = running_state[1] + jnp.einsum('thm,th->hm', query_widened, norm_half.astype(widened_rows))
        return ((gradient_summed, total_sum), None)
    query_blocks = as_blocks(queries)
    upstream_blocks = as_blocks(cotangent)
    (summary_grad, overall_gradient), _ = lax.scan(add_queries, starting, (query_blocks, upstream_blocks))
    gradient_halves = summary_grad.astype(jnp.bfloat16).astype(widened_rows)

    def gradients(block_set):
        query_blk, key_blk, value_block, upstream_blk = block_set
        query_pre, _, scaled_halves, norm_grad, _ = query_side(query_blk, upstream_blk)
        key_pre, key_feature_map = featurize(key_blk)
        query_feature_gradient = jnp.einsum('pfy,fly->pfl', scaled_halves.astype(widened_rows), digest_halves.astype(widened_rows))
        query_feature_gradient = query_feature_gradient + norm_grad[..., None] * total_half.astype(widened_rows)[None]
        key_feature_gradient = jnp.einsum('pfy,fly->pfl', value_block.astype(widened_rows), gradient_halves) + overall_gradient[None]
        value_gradient = jnp.einsum('xls,lsk->xlk', key_feature_map.astype(widened_rows), gradient_halves).astype(jnp.bfloat16)
        query_pre_grad = (query_feature_gradient * jax.nn.sigmoid(query_pre)).astype(jnp.bfloat16)
        key_pre_grad = (key_feature_gradient * jax.nn.sigmoid(key_pre)).astype(jnp.bfloat16)
        query_grad = jnp.einsum('thm,hdm->thd', query_pre_grad.astype(widened_rows), omega_wide).astype(jnp.bfloat16)
        key_grad = jnp.einsum('thm,hdm->thd', key_pre_grad.astype(widened_rows), omega_wide).astype(jnp.bfloat16)
        return (query_grad, key_grad, value_gradient)
    query_grad, key_grad, value_gradient = lax.map(gradients, (query_blocks, as_blocks(key_act), as_blocks(value_act), upstream_blocks))
    total = jnp.dot(query_grad.reshape(TOKENS, D), query_weight.T, preferred_element_type=jnp.float32)
    total = total + jnp.dot(key_grad.reshape(TOKENS, D), key_weight.T, preferred_element_type=jnp.float32)
    total = total + jnp.dot(value_gradient.reshape(TOKENS, D), value_weight.T, preferred_element_type=jnp.float32)
    return total.astype(jnp.bfloat16)
```

```python
import functools
import math

import jax
import jax.numpy as jnp
from jax import lax
from jax.experimental import pallas as pl
from jax.experimental.pallas import tpu as pltpu
from jax.sharding import PartitionSpec as P

F32 = jnp.float32
BF16 = jnp.bfloat16


def encode(events, offsets):
    half_width = events.shape[1] // 2
    indices = jnp.arange(half_width, dtype=F32)
    frequency = jnp.exp(indices * (-2.0 * math.log(10000.0) / events.shape[1]))
    angles = offsets.astype(F32)[:, None] * frequency[None, :]
    encoding = jnp.concatenate([jnp.sin(angles), jnp.cos(angles)], axis=1)
    return (events.astype(F32) + encoding).astype(BF16)


def dot(a, b, ca=1, cb=0):
    return lax.dot_general(a, b, (((ca,), (cb,)), ((), ())), preferred_element_type=F32)


def soft_and_sigmoid(u):
    e = jnp.exp(-jnp.abs(u))
    series = e * (1.0 + e * (-0.5 + e * (1.0 / 3.0)))
    soft = jnp.maximum(u, 0.0) + jnp.where(e < 1e-3, series, jnp.log(1.0 + e))
    r = 1.0 / (1.0 + e)
    return soft, jnp.where(u >= 0.0, r, e * r)


def place_rows(full, parts):
    z = lax.axis_index("sub")
    rows = parts[0].shape[0]
    for k, part in enumerate(parts):
        full[pl.ds(pl.multiple_of((z ^ k) * rows, rows), rows), :] = part[...]


def call(body, outs, args, flops):
    nbytes = sum(a.size * a.dtype.itemsize for a in args)
    return pl.pallas_call(
        body,
        out_shape=[jax.ShapeDtypeStruct(s, d) for s, d in outs],
        compiler_params=pltpu.CompilerParams(vmem_limit_bytes=48 * 1024 * 1024),
        cost_estimate=pl.CostEstimate(flops=flops, bytes_accessed=nbytes, transcendentals=0),
    )(*args)


def features(xs, w_full, om, hp, feat, sig, total):
    hd, m = om.shape[1], om.shape[2]
    rows = xs[0].shape[0]
    sums = [jnp.zeros((1, m), F32) for _ in range(hp)]
    for i, x in enumerate(xs):
        act = dot(x[...], w_full[...]).astype(BF16)
        for h in range(hp):
            pre = dot(act[:, h * hd : (h + 1) * hd], om[h])
            soft, s = soft_and_sigmoid(pre)
            soft = soft.astype(BF16)
            at = (slice(i * rows, (i + 1) * rows), slice(h * m, (h + 1) * m))
            feat[at] = soft
            sig[at] = s
            if total is not None:
                sums[h] = sums[h] + jnp.sum(soft.astype(F32), axis=0, keepdims=True)
    if total is not None:
        for h in range(hp):
            total[:, h * m : (h + 1) * m] = sums[h]


def key_kernel(g, n, hp, *refs):
    xs, ws, om = refs[:g], refs[g : g + n], refs[g + n]
    w_full, feat, sig, total = refs[g + n + 1 :]
    place_rows(w_full, ws)
    features(xs, w_full, om, hp, feat, sig, total)


def query_kernel(g, n, hp, *refs):
    xs, ws, om = refs[:g], refs[g : g + n], refs[g + n]
    w_full, feat, sig = refs[g + n + 1 :]
    place_rows(w_full, ws)
    features(xs, w_full, om, hp, feat, sig, None)


def value_kernel(g, n, hp, *refs):
    xs, ws, feat = refs[:g], refs[g : g + n], refs[g + n]
    w_full, val, own, send = refs[g + n + 1 :]
    place_rows(w_full, ws)
    rows = xs[0].shape[0]
    for i, x in enumerate(xs):
        val[i * rows : (i + 1) * rows, :] = dot(x[...], w_full[...]).astype(BF16)
    m, hd = feat.shape[1] // hp, val.shape[1] // hp
    for h in range(hp):
        s = dot(feat[:, h * m : (h + 1) * m], val[:, h * hd : (h + 1) * hd], 0, 0)
        own[h * m : (h + 1) * m, :] = s
        send[h * m : (h + 1) * m, :] = s.astype(BF16)


def summed(parts):
    out = parts[0][...]
    for part in parts[1:]:
        out = out + part[...].astype(F32)
    return out


def scale_kernel(g, p, hp, loss_scale, *refs):
    tots, cots, feat = refs[:p], refs[p : p + g], refs[p + g]
    total_half, scaled_half, twice, own, send = refs[p + g + 1 :]
    total_half[...] = summed(tots).astype(BF16)
    m, hd = feat.shape[1] // hp, scaled_half.shape[1] // hp
    rows = cots[0].shape[0]
    for h in range(hp):
        spread = jnp.broadcast_to(total_half[:, h * m : (h + 1) * m].astype(F32), (hd, m)).astype(BF16)
        for i in range(g):
            tok = slice(i * rows, (i + 1) * rows)
            col = slice(h * hd, (h + 1) * hd)
            denom = dot(feat[tok, h * m : (h + 1) * m], spread, 1, 1)
            scaled = cots[i][:, col].astype(F32) * loss_scale / denom
            scaled_half[tok, col] = scaled.astype(BF16)
            twice[tok, col] = scaled / denom
        s = dot(feat[:, h * m : (h + 1) * m], scaled_half[:, h * hd : (h + 1) * hd], 0, 0)
        own[h * m : (h + 1) * m, :] = s
        send[h * m : (h + 1) * m, :] = s.astype(BF16)


def norm_kernel(p, hp, *refs):
    parts, feat, twice = refs[:p], refs[p], refs[p + 1]
    summary_half, norm, total = refs[p + 2 :]
    summary_half[...] = summed(parts).astype(BF16)
    m, hd = feat.shape[1] // hp, twice.shape[1] // hp
    for h in range(hp):
        qf = feat[:, h * m : (h + 1) * m]
        numer = dot(qf, summary_half[h * m : (h + 1) * m, :])
        ng = -jnp.sum(twice[:, h * hd : (h + 1) * hd] * numer, axis=1, keepdims=True)
        norm[:, h : h + 1] = ng
        half = ng.astype(BF16).astype(F32)
        total[:, h * m : (h + 1) * m] = jnp.sum(qf.astype(F32) * half, axis=0, keepdims=True)


def query_grad_kernel(hp, scaled_half, summary_half, norm, total_half, sig, om, out):
    hd, m = om.shape[1], om.shape[2]
    for h in range(hp):
        fg = dot(scaled_half[:, h * hd : (h + 1) * hd], summary_half[h * m : (h + 1) * m, :], 1, 1)
        fg = fg + norm[:, h : h + 1] * total_half[:, h * m : (h + 1) * m].astype(F32)
        pg = (fg * sig[:, h * m : (h + 1) * m]).astype(BF16)
        out[:, h * hd : (h + 1) * hd] = dot(pg, om[h], 1, 1).astype(BF16)


def final_kernel(g, p, hp, *refs):
    parts, tots = refs[:p], refs[p : 2 * p]
    val, feat, sig, om, qg, wq, wk, wv = refs[2 * p : 2 * p + 8]
    odd, even, kg, vg = refs[2 * p + 8 :]
    hd, m = om.shape[1], om.shape[2]
    grad_half = summed(parts).astype(BF16)
    total = summed(tots)
    for h in range(hp):
        gh = grad_half[h * m : (h + 1) * m, :]
        col = slice(h * hd, (h + 1) * hd)
        fg = dot(val[:, col], gh, 1, 1) + total[:, h * m : (h + 1) * m]
        vg[:, col] = dot(feat[:, h * m : (h + 1) * m], gh).astype(BF16)
        pg = (fg * sig[:, h * m : (h + 1) * m]).astype(BF16)
        kg[:, col] = dot(pg, om[h], 1, 1).astype(BF16)
    rows = val.shape[0] // g
    for i in range(g):
        tok = slice(i * rows, (i + 1) * rows)
        out = dot(qg[tok, :], wq[...], 1, 1)
        out = out + dot(kg[tok, :], wk[...], 1, 1)
        out = out + dot(vg[tok, :], wv[...], 1, 1)
        at = slice((i // 2) * rows, (i // 2 + 1) * rows)
        if i % 2:
            odd[at, :] = out.astype(BF16)
        else:
            even[at, :] = out


def local(events, offsets, cotangent, query_weight, key_weight, value_weight, omega):
    heads, hd, m = omega.shape
    n_seq, n_sub = lax.axis_size("seq"), lax.axis_size("sub")
    rows, width = events.shape
    loss_scale = math.sqrt(rows * n_seq * n_sub)
    g = math.gcd(heads, n_seq)
    r = n_seq // g
    hp = heads // g
    p = r * n_sub
    t = g * rows
    cols = hp * hd
    s = lax.axis_index("seq")
    mine = s % g

    def over_seq(x, k):
        return lax.ppermute(x, "seq", [(i, i ^ k) for i in range(n_seq)])

    def over_sub(x, k):
        return lax.ppermute(x, "sub", [(i, i ^ k) for i in range(n_sub)])

    def to_all(own, send):
        parts = [own]
        for j in range(r):
            for k in range(n_sub):
                if j or k:
                    perm = [
                        (a * n_sub + b, (a ^ (j * g)) * n_sub + (b ^ k))
                        for a in range(n_seq)
                        for b in range(n_sub)
                    ]
                    parts.append(lax.ppermute(send, ("seq", "sub"), perm))
        return parts

    def columns(w):
        return lax.dynamic_slice_in_dim(w, mine * cols, cols, 1)

    def weight_rows(w):
        w = columns(w)
        return [w] + [over_sub(w, k) for k in range(1, n_sub)]

    wk, wv, wq = weight_rows(key_weight), weight_rows(value_weight), weight_rows(query_weight)
    x0 = encode(events, offsets)
    xs = [x0] * g
    for k in range(2, g, 2):
        xs[k] = over_seq(x0, k)
    for k in range(1, g, 2):
        xs[k] = over_seq(xs[k ^ 1], 1)
    cots = [columns(cotangent)]
    for k in range(1, g):
        cots.append(over_seq(lax.dynamic_slice_in_dim(cotangent, (mine ^ k) * cols, cols, 1), k))
    om = lax.dynamic_slice_in_dim(omega, mine * hp, hp, 0)

    flop = 2 * t * width * cols
    wk_full, key_feat, key_sig, key_total = call(
        functools.partial(key_kernel, g, n_sub, hp),
        [((width, cols), BF16), ((t, hp * m), BF16), ((t, hp * m), F32), ((1, hp * m), F32)],
        [*xs, *wk, om],
        8 * flop,
    )
    tots = to_all(key_total, key_total)
    wv_full, val, own, send = call(
        functools.partial(value_kernel, g, n_sub, hp),
        [((width, cols), BF16), ((t, cols), BF16), ((hp * m, hd), F32), ((hp * m, hd), BF16)],
        [*xs, *wv, key_feat],
        4 * flop,
    )
    summary = to_all(own, send)
    wq_full, query_feat, query_sig = call(
        functools.partial(query_kernel, g, n_sub, hp),
        [((width, cols), BF16), ((t, hp * m), BF16), ((t, hp * m), F32)],
        [*xs, *wq, om],
        8 * flop,
    )
    total_half, scaled_half, twice, own, send = call(
        functools.partial(scale_kernel, g, p, hp, loss_scale),
        [((1, hp * m), BF16), ((t, cols), BF16), ((t, cols), F32), ((hp * m, hd), F32), ((hp * m, hd), BF16)],
        [*tots, *cots, query_feat],
        4 * flop,
    )
    summary_grad = to_all(own, send)
    summary_half, norm, total_part = call(
        functools.partial(norm_kernel, p, hp),
        [((hp * m, hd), BF16), ((t, hp), F32), ((1, hp * m), F32)],
        [*summary, query_feat, twice],
        4 * flop,
    )
    total_grad = to_all(total_part, total_part)
    (query_grad,) = call(
        functools.partial(query_grad_kernel, hp),
        [((t, cols), BF16)],
        [scaled_half, summary_half, norm, total_half, query_sig, om],
        4 * flop,
    )
    odd, even, _, _ = call(
        functools.partial(final_kernel, g, p, hp),
        [((t // 2, width), BF16), ((t // 2, width), F32), ((t, cols), BF16), ((t, cols), BF16)],
        [*summary_grad, *total_grad, val, key_feat, key_sig, om, query_grad, wq_full, wk_full, wv_full],
        8 * flop,
    )
    got = over_seq(odd, 1)
    both = even + got.astype(F32)
    out = both[:rows]
    for k in range(2, g, 2):
        at = (k // 2) * rows
        out = out + over_seq(both[at : at + rows].astype(BF16), k).astype(F32)
    return out.astype(BF16)


def solution(mesh):
    in_specs = (
        P(("grp", "seq", "sub"), None),
        P(("grp", "seq", "sub")),
        P(("grp", "seq", "sub"), None),
        P("sub", None),
        P("sub", None),
        P("sub", None),
        P(),
    )
    out_specs = P(("grp", "seq", "sub"), None)
    return jax.shard_map(local, mesh=mesh, in_specs=in_specs, out_specs=out_specs, check_vma=False)
```

```python
import functools
import math

import jax
import jax.numpy as jnp
from jax import lax
from jax.experimental import pallas as pl
from jax.experimental.pallas import tpu as pltpu
from jax.sharding import PartitionSpec as P

F32 = jnp.float32
BF16 = jnp.bfloat16
ANY = pl.BlockSpec(memory_space=pl.ANY)


def dot(a, b, ca=1, cb=0):
    return lax.dot_general(a, b, (((ca,), (cb,)), ((), ())), preferred_element_type=F32)


def soft_and_sigmoid(u):
    e = jnp.exp(-jnp.abs(u))
    series = e * (1.0 + e * (-0.5 + e * (1.0 / 3.0)))
    soft = jnp.maximum(u, 0.0) + jnp.where(e < 1e-3, series, jnp.log(1.0 + e))
    r = 1.0 / (1.0 + e)
    return soft, jnp.where(u >= 0.0, r, e * r)


def call(body, outs, args, flops, **kw):
    nbytes = sum(a.size * a.dtype.itemsize for a in args)
    return pl.pallas_call(
        body,
        out_shape=[jax.ShapeDtypeStruct(s, d) for s, d in outs],
        compiler_params=pltpu.CompilerParams(vmem_limit_bytes=24 * 1024 * 1024),
        cost_estimate=pl.CostEstimate(flops=flops, bytes_accessed=nbytes, transcendentals=0),
        **kw,
    )(*args)


def weight_kernel(g, cols, wk, wv, wq, kv, q, sems):
    at = pl.ds(pl.multiple_of((lax.axis_index("seq") % g) * cols, cols), cols)
    copies = [
        pltpu.make_async_copy(wk.at[:, at], kv.at[:, :cols], sems.at[0]),
        pltpu.make_async_copy(wv.at[:, at], kv.at[:, cols:], sems.at[1]),
        pltpu.make_async_copy(wq.at[:, at], q, sems.at[2]),
    ]
    for c in copies:
        c.start()
    for c in copies:
        c.wait()


def input_kernel(g, pair, events, sines, cosines, cot, *outs):
    width = events.shape[1]
    half = width // 2
    mine = (lax.axis_index("seq") % g) // 2
    left = (events[:, :half].astype(F32) + sines[...]).astype(BF16)
    right = (events[:, half:].astype(F32) + cosines[...]).astype(BF16)
    for k, out in enumerate(outs):
        out[:, :half] = left
        out[:, half:width] = right
        out[:, width:] = cot[:, pl.ds(pl.multiple_of((mine ^ k) * pair, pair), pair)]


def place_rows(full, parts):
    z = lax.axis_index("sub")
    rows = parts[0].shape[0]
    for k, part in enumerate(parts):
        full[pl.ds(pl.multiple_of((z ^ k) * rows, rows), rows), :] = part[...]


def features(act, om, h, i, feat, sig):
    hd, m = om.shape[1], om.shape[2]
    rows = act.shape[0]
    soft, s = soft_and_sigmoid(dot(act[:, h * hd : (h + 1) * hd], om[h]))
    soft = soft.astype(BF16)
    at = (slice(i * rows, (i + 1) * rows), slice(h * m, (h + 1) * m))
    feat[at] = soft
    sig[at] = s
    return soft


def put_total(own, send, base, extra, total):
    hd = own.shape[1]
    n = total.shape[1] // hd
    for j in range(n):
        piece = total[:, j * hd : (j + 1) * hd]
        high = piece.astype(BF16)
        own[base + j : base + j + 1, :] = piece
        send[base + j : base + j + 1, :] = high
        own[base + extra + j : base + extra + j + 1, :] = jnp.zeros_like(piece)
        send[base + extra + j : base + extra + j + 1, :] = (piece - high.astype(F32)).astype(BF16)


def get_total(tail, extra, h, m):
    hd = tail.shape[1]
    n = m // hd
    rows = [
        tail[h * n + j : h * n + j + 1, :] + tail[extra + h * n + j : extra + h * n + j + 1, :]
        for j in range(n)
    ]
    return jnp.concatenate(rows, axis=1)


def summed(parts, lo, hi):
    out = parts[0][lo:hi, :]
    for part in parts[1:]:
        out = out + part[lo:hi, :].astype(F32)
    return out


def key_value_kernel(g, n, hp, width, *refs):
    xs, ws, om = refs[:g], refs[g : g + n], refs[g + n]
    w_full, feat, sig, val, own, send = refs[g + n + 1 :]
    hd, m = om.shape[1], om.shape[2]
    cols = hp * hd
    place_rows(w_full, ws)
    rows = xs[0].shape[0]
    sums = [jnp.zeros((1, m), F32) for _ in range(hp)]
    for i, x in enumerate(xs):
        act = dot(x[:, :width], w_full[...]).astype(BF16)
        val[i * rows : (i + 1) * rows, :] = act[:, cols:]
        for h in range(hp):
            soft = features(act, om, h, i, feat, sig)
            sums[h] = sums[h] + jnp.sum(soft.astype(F32), axis=0, keepdims=True)
    base = hp * m
    own[base:, :] = jnp.zeros_like(own[base:, :])
    send[base:, :] = jnp.zeros_like(send[base:, :])
    for h in range(hp):
        s = dot(feat[:, h * m : (h + 1) * m], val[:, h * hd : (h + 1) * hd], 0, 0)
        own[h * m : (h + 1) * m, :] = s
        send[h * m : (h + 1) * m, :] = s.astype(BF16)
    put_total(own, send, base, hp * m // hd, jnp.concatenate(sums, axis=1))


def query_kernel(g, n, hp, width, *refs):
    xs, ws, om = refs[:g], refs[g : g + n], refs[g + n]
    w_full, feat, sig = refs[g + n + 1 :]
    place_rows(w_full, ws)
    for i, x in enumerate(xs):
        act = dot(x[:, :width], w_full[...]).astype(BF16)
        for h in range(hp):
            features(act, om, h, i, feat, sig)


def query_side_kernel(g, p, hp, m, width, loss_scale, *refs):
    parts, xs, feat = refs[:p], refs[p : p + g], refs[p + g]
    total_half, summary_half, scaled_half, norm, own, send = refs[p + g + 1 :]
    hd = summary_half.shape[1]
    cols = hp * hd
    base = hp * m
    extra = base // hd
    summary_half[...] = summed(parts, 0, base).astype(BF16)
    tail = summed(parts, base, parts[0].shape[0])
    core = lax.axis_index("seq") % 2
    rows = xs[0].shape[0]
    own[base:, :] = jnp.zeros_like(own[base:, :])
    send[base:, :] = jnp.zeros_like(send[base:, :])
    sums = []
    for h in range(hp):
        row = get_total(tail, extra, h, m).astype(BF16)
        total_half[:, h * m : (h + 1) * m] = row
        spread = jnp.broadcast_to(row.astype(F32), (hd, m)).astype(BF16)
        acc = jnp.zeros((1, m), F32)
        for i in range(g):
            tok = slice(i * rows, (i + 1) * rows)
            qf = feat[tok, h * m : (h + 1) * m]
            at = pl.multiple_of(width + core * cols + h * hd, hd)
            denom = dot(qf, spread, 1, 1)
            numer = dot(qf, summary_half[h * m : (h + 1) * m, :])
            scaled = xs[i][:, pl.ds(at, hd)].astype(F32) * loss_scale / denom
            scaled_half[tok, h * hd : (h + 1) * hd] = scaled.astype(BF16)
            ng = -jnp.sum(scaled * (numer / denom), axis=1, keepdims=True)
            norm[tok, h : h + 1] = ng
            acc = acc + jnp.sum(qf.astype(F32) * ng.astype(BF16).astype(F32), axis=0, keepdims=True)
        s = dot(feat[:, h * m : (h + 1) * m], scaled_half[:, h * hd : (h + 1) * hd], 0, 0)
        own[h * m : (h + 1) * m, :] = s
        send[h * m : (h + 1) * m, :] = s.astype(BF16)
        sums.append(acc)
    put_total(own, send, base, extra, jnp.concatenate(sums, axis=1))


def query_grad_kernel(hp, scaled_half, summary_half, norm, total_half, sig, om, out):
    hd, m = om.shape[1], om.shape[2]
    for h in range(hp):
        fg = dot(scaled_half[:, h * hd : (h + 1) * hd], summary_half[h * m : (h + 1) * m, :], 1, 1)
        fg = fg + norm[:, h : h + 1] * total_half[:, h * m : (h + 1) * m].astype(F32)
        pg = (fg * sig[:, h * m : (h + 1) * m]).astype(BF16)
        out[:, h * hd : (h + 1) * hd] = dot(pg, om[h], 1, 1).astype(BF16)


def products(g, start, qg, kvg, wq, wkv, out):
    rows = qg.shape[0] // g
    for i in range(start, g, 2):
        tok = slice(i * rows, (i + 1) * rows)
        o = dot(qg[tok, :], wq[...], 1, 1) + dot(kvg[tok, :], wkv[...], 1, 1)
        out[(i // 2) * rows : (i // 2 + 1) * rows, :] = o.astype(out.dtype)


def key_side_kernel(g, p, hp, *refs):
    parts = refs[:p]
    val, feat, sig, om, qg, wq, wkv = refs[p : p + 7]
    odd, kvg = refs[p + 7 :]
    hd, m = om.shape[1], om.shape[2]
    base = hp * m
    cols = hp * hd
    tail = summed(parts, base, parts[0].shape[0])
    for h in range(hp):
        gh = summed(parts, h * m, (h + 1) * m).astype(BF16)
        col = slice(h * hd, (h + 1) * hd)
        fg = dot(val[:, col], gh, 1, 1) + get_total(tail, base // hd, h, m)
        kvg[:, cols + h * hd : cols + (h + 1) * hd] = dot(feat[:, h * m : (h + 1) * m], gh).astype(BF16)
        pg = (fg * sig[:, h * m : (h + 1) * m]).astype(BF16)
        kvg[:, col] = dot(pg, om[h], 1, 1).astype(BF16)
    products(g, 1, qg, kvg, wq, wkv, odd)


def even_kernel(g, qg, kvg, wq, wkv, even):
    products(g, 0, qg, kvg, wq, wkv, even)


def local(events, offsets, cotangent, query_weight, key_weight, value_weight, omega):
    heads, hd, m = omega.shape
    n_seq, n_sub = lax.axis_size("seq"), lax.axis_size("sub")
    rows, width = events.shape
    loss_scale = math.sqrt(rows * n_seq * n_sub)
    g = math.gcd(heads, n_seq)
    r = n_seq // g
    hp = heads // g
    p = r * n_sub
    t = g * rows
    cols = hp * hd
    srows = hp * m + -(-2 * hp * m // hd // 16) * 16

    def over_seq(x, k):
        return lax.ppermute(x, "seq", [(i, i ^ k) for i in range(n_seq)])

    def over_sub(x, k):
        return lax.ppermute(x, "sub", [(i, i ^ k) for i in range(n_sub)])

    def to_all(own, send):
        parts = [own]
        for j in range(r):
            for k in range(n_sub):
                if j or k:
                    perm = [
                        (a * n_sub + b, (a ^ (j * g)) * n_sub + (b ^ k))
                        for a in range(n_seq)
                        for b in range(n_sub)
                    ]
                    parts.append(lax.ppermute(send, ("seq", "sub"), perm))
        return parts

    kv, q = call(
        functools.partial(weight_kernel, g, cols),
        [((key_weight.shape[0], 2 * cols), BF16), ((key_weight.shape[0], cols), BF16)],
        [key_weight, value_weight, query_weight],
        0,
        in_specs=[ANY] * 3,
        scratch_shapes=[pltpu.SemaphoreType.DMA((3,))],
    )
    kvs = [kv] + [over_sub(kv, k) for k in range(1, n_sub)]

    half = width // 2
    frequency = jnp.exp(jnp.arange(half, dtype=F32) * (-2.0 * math.log(10000.0) / width))
    angles = offsets.astype(F32)[:, None] * frequency[None, :]
    bufs = call(
        functools.partial(input_kernel, g, 2 * cols),
        [((rows, width + 2 * cols), BF16)] * (g // 2),
        [events, jnp.sin(angles), jnp.cos(angles), cotangent],
        0,
    )
    xs = [bufs[0]] * g
    for k in range(2, g, 2):
        xs[k] = over_seq(bufs[k // 2], k)
    for k in range(1, g, 2):
        xs[k] = over_seq(xs[k ^ 1], 1)
    qs = [q] + [over_sub(q, k) for k in range(1, n_sub)]
    om = lax.dynamic_slice_in_dim(omega, (lax.axis_index("seq") % g) * hp, hp, 0)

    flop = 2 * t * width * cols
    summary_out = [((srows, hd), F32), ((srows, hd), BF16)]
    wkv_full, key_feat, key_sig, val, own, send = call(
        functools.partial(key_value_kernel, g, n_sub, hp, width),
        [((width, 2 * cols), BF16), ((t, hp * m), BF16), ((t, hp * m), F32), ((t, cols), BF16)] + summary_out,
        [*xs, *kvs, om],
        8 * flop,
    )
    summary = to_all(own, send)
    wq_full, query_feat, query_sig = call(
        functools.partial(query_kernel, g, n_sub, hp, width),
        [((width, cols), BF16), ((t, hp * m), BF16), ((t, hp * m), F32)],
        [*xs, *qs, om],
        8 * flop,
    )
    total_half, summary_half, scaled_half, norm, own, send = call(
        functools.partial(query_side_kernel, g, p, hp, m, width, loss_scale),
        [((1, hp * m), BF16), ((hp * m, hd), BF16), ((t, cols), BF16), ((t, hp), F32)] + summary_out,
        [*summary, *xs, query_feat],
        8 * flop,
    )
    summary_grad = to_all(own, send)
    (query_grad,) = call(
        functools.partial(query_grad_kernel, hp),
        [((t, cols), BF16)],
        [scaled_half, summary_half, norm, total_half, query_sig, om],
        4 * flop,
    )
    odd, key_value_grad = call(
        functools.partial(key_side_kernel, g, p, hp),
        [((t // 2, width), BF16), ((t, 2 * cols), BF16)],
        [*summary_grad, val, key_feat, key_sig, om, query_grad, wq_full, wkv_full],
        8 * flop,
    )
    got = over_seq(odd, 1)
    (even,) = call(
        functools.partial(even_kernel, g),
        [((t // 2, width), F32)],
        [query_grad, key_value_grad, wq_full, wkv_full],
        8 * flop,
    )
    both = even + got.astype(F32)
    out = both[:rows]
    for k in range(2, g, 2):
        at = (k // 2) * rows
        out = out + over_seq(both[at : at + rows].astype(BF16), k).astype(F32)
    return out.astype(BF16)


def solution(mesh):
    in_specs = (
        P(("grp", "seq", "sub"), None),
        P(("grp", "seq", "sub")),
        P(("grp", "seq", "sub"), None),
        P("sub", None),
        P("sub", None),
        P("sub", None),
        P(),
    )
    out_specs = P(("grp", "seq", "sub"), None)
    return jax.shard_map(local, mesh=mesh, in_specs=in_specs, out_specs=out_specs, check_vma=False)
```

```python
import functools
import math

import jax
import jax.numpy as jnp
from jax import lax
from jax.experimental import pallas as pl
from jax.experimental.pallas import tpu as pltpu
from jax.sharding import PartitionSpec as P

F32 = jnp.float32
BF16 = jnp.bfloat16
HBM = pl.BlockSpec(memory_space=pltpu.HBM)


def dot(a, b, ca=1, cb=0):
    return lax.dot_general(a, b, (((ca,), (cb,)), ((), ())), preferred_element_type=F32)


def soft_and_sigmoid(u):
    e = jnp.exp(-jnp.abs(u))
    series = e * (1.0 + e * (-0.5 + e * (1.0 / 3.0)))
    soft = jnp.maximum(u, 0.0) + jnp.where(e < 1e-3, series, jnp.log(1.0 + e))
    r = 1.0 / (1.0 + e)
    return soft, jnp.where(u >= 0.0, r, e * r)


def call(body, outs, args, flops, **kw):
    nbytes = sum(a.size * a.dtype.itemsize for a in args)
    return pl.pallas_call(
        body,
        out_shape=[jax.ShapeDtypeStruct(s, d) for s, d in outs],
        compiler_params=pltpu.CompilerParams(vmem_limit_bytes=24 * 1024 * 1024),
        cost_estimate=pl.CostEstimate(flops=flops, bytes_accessed=nbytes, transcendentals=0),
        **kw,
    )(*args)


def weight_kernel(g, cols, split, wk, wv, wq, *refs):
    outs, sems = refs[:-1], refs[-1]
    at = pl.ds(pl.multiple_of((lax.axis_index("seq") % g) * cols, cols), cols)
    pairs = [(wk.at[:, at], outs[0].at[:, :cols]), (wv.at[:, at], outs[0].at[:, cols:]), (wq.at[:, at], outs[1])]
    if split:
        half = wk.shape[0] // 2
        rows = pl.ds(pl.multiple_of(lax.axis_index("grp") * half, half), half)
        pairs += [
            (wk.at[rows, at], outs[2].at[:, :cols]),
            (wv.at[rows, at], outs[2].at[:, cols:]),
        ]
    copies = [pltpu.make_async_copy(a, b, sems.at[i]) for i, (a, b) in enumerate(pairs)]
    for c in copies:
        c.start()
    for c in copies:
        c.wait()


def input_kernel(g, pair, events, sines, cosines, cot, *outs):
    width = events.shape[1]
    half = width // 2
    mine = (lax.axis_index("seq") % g) // 2
    left = (events[:, :half].astype(F32) + sines[...]).astype(BF16)
    right = (events[:, half:].astype(F32) + cosines[...]).astype(BF16)
    for k, out in enumerate(outs):
        out[:, :half] = left
        out[:, half:width] = right
        out[:, width:] = cot[:, pl.ds(pl.multiple_of((mine ^ k) * pair, pair), pair)]


def place_rows(full, parts, n):
    z = lax.axis_index("sub")
    rows = parts[0].shape[0]
    spots = [(k, 0) for k in range(n)]
    if len(parts) > n:
        half, mine = rows // 2, lax.axis_index("grp")
        spots = [(0, 0), (1, 0)]
        for k in range(2, n):
            spots += [(k, mine * half), (k, half - mine * half)]
    for (k, start), part in zip(spots, parts):
        size = part.shape[0]
        full[pl.ds(pl.multiple_of((z ^ k) * rows + start, size), size), :] = part[...]


def features(act, om, h, i, feat, sig):
    hd, m = om.shape[1], om.shape[2]
    rows = act.shape[0]
    soft, s = soft_and_sigmoid(dot(act[:, h * hd : (h + 1) * hd], om[h]))
    soft = soft.astype(BF16)
    at = (slice(i * rows, (i + 1) * rows), slice(h * m, (h + 1) * m))
    feat[at] = soft
    sig[at] = s
    return soft


def put_total(own, send, base, extra, total):
    hd = own.shape[1]
    n = total.shape[1] // hd
    for j in range(n):
        piece = total[:, j * hd : (j + 1) * hd]
        high = piece.astype(BF16)
        own[base + j : base + j + 1, :] = piece
        send[base + j : base + j + 1, :] = high
        own[base + extra + j : base + extra + j + 1, :] = jnp.zeros_like(piece)
        send[base + extra + j : base + extra + j + 1, :] = (piece - high.astype(F32)).astype(BF16)


def get_total(tail, extra, h, m):
    hd = tail.shape[1]
    n = m // hd
    rows = [
        tail[h * n + j : h * n + j + 1, :] + tail[extra + h * n + j : extra + h * n + j + 1, :]
        for j in range(n)
    ]
    return jnp.concatenate(rows, axis=1)


def summed(parts, lo, hi):
    out = parts[0][lo:hi, :]
    for part in parts[1:]:
        out = out + part[lo:hi, :].astype(F32)
    return out


def key_value_kernel(g, n, nw, hp, width, *refs):
    xs, ws, om = refs[:g], refs[g : g + nw], refs[g + nw]
    w_full, feat, sig, val, own, send = refs[g + nw + 1 :]
    hd, m = om.shape[1], om.shape[2]
    cols = hp * hd
    place_rows(w_full, ws, n)
    rows = xs[0].shape[0]
    sums = [jnp.zeros((1, m), F32) for _ in range(hp)]
    for i, x in enumerate(xs):
        act = dot(x[:, :width], w_full[...]).astype(BF16)
        val[i * rows : (i + 1) * rows, :] = act[:, cols:]
        for h in range(hp):
            soft = features(act, om, h, i, feat, sig)
            sums[h] = sums[h] + jnp.sum(soft.astype(F32), axis=0, keepdims=True)
    base = hp * m
    own[base:, :] = jnp.zeros_like(own[base:, :])
    send[base:, :] = jnp.zeros_like(send[base:, :])
    for h in range(hp):
        s = dot(feat[:, h * m : (h + 1) * m], val[:, h * hd : (h + 1) * hd], 0, 0)
        own[h * m : (h + 1) * m, :] = s
        send[h * m : (h + 1) * m, :] = s.astype(BF16)
    put_total(own, send, base, hp * m // hd, jnp.concatenate(sums, axis=1))


def query_kernel(g, n, nw, hp, width, *refs):
    xs, ws, om = refs[:g], refs[g : g + nw], refs[g + nw]
    w_full, feat, sig = refs[g + nw + 1 :]
    place_rows(w_full, ws, n)
    for i, x in enumerate(xs):
        act = dot(x[:, :width], w_full[...]).astype(BF16)
        for h in range(hp):
            features(act, om, h, i, feat, sig)


def query_side_kernel(g, p, hp, m, width, loss_scale, *refs):
    parts, xs, feat = refs[:p], refs[p : p + g], refs[p + g]
    total_half, summary_half, scaled_half, norm, own, send = refs[p + g + 1 :]
    hd = summary_half.shape[1]
    cols = hp * hd
    base = hp * m
    extra = base // hd
    summary_half[...] = summed(parts, 0, base).astype(BF16)
    tail = summed(parts, base, parts[0].shape[0])
    core = lax.axis_index("seq") % 2
    rows = xs[0].shape[0]
    own[base:, :] = jnp.zeros_like(own[base:, :])
    send[base:, :] = jnp.zeros_like(send[base:, :])
    sums = []
    for h in range(hp):
        row = get_total(tail, extra, h, m).astype(BF16)
        total_half[:, h * m : (h + 1) * m] = row
        spread = jnp.broadcast_to(row.astype(F32), (hd, m)).astype(BF16)
        acc = jnp.zeros((1, m), F32)
        for i in range(g):
            tok = slice(i * rows, (i + 1) * rows)
            qf = feat[tok, h * m : (h + 1) * m]
            at = pl.multiple_of(width + core * cols + h * hd, hd)
            denom = dot(qf, spread, 1, 1)
            numer = dot(qf, summary_half[h * m : (h + 1) * m, :])
            scaled = xs[i][:, pl.ds(at, hd)].astype(F32) * loss_scale / denom
            scaled_half[tok, h * hd : (h + 1) * hd] = scaled.astype(BF16)
            ng = -jnp.sum(scaled * (numer / denom), axis=1, keepdims=True)
            norm[tok, h : h + 1] = ng
            acc = acc + jnp.sum(qf.astype(F32) * ng.astype(BF16).astype(F32), axis=0, keepdims=True)
        s = dot(feat[:, h * m : (h + 1) * m], scaled_half[:, h * hd : (h + 1) * hd], 0, 0)
        own[h * m : (h + 1) * m, :] = s
        send[h * m : (h + 1) * m, :] = s.astype(BF16)
        sums.append(acc)
    put_total(own, send, base, extra, jnp.concatenate(sums, axis=1))


def query_grad_kernel(hp, scaled_half, summary_half, norm, total_half, sig, om, out):
    hd, m = om.shape[1], om.shape[2]
    for h in range(hp):
        fg = dot(scaled_half[:, h * hd : (h + 1) * hd], summary_half[h * m : (h + 1) * m, :], 1, 1)
        fg = fg + norm[:, h : h + 1] * total_half[:, h * m : (h + 1) * m].astype(F32)
        pg = (fg * sig[:, h * m : (h + 1) * m]).astype(BF16)
        out[:, h * hd : (h + 1) * hd] = dot(pg, om[h], 1, 1).astype(BF16)


def products(g, start, qg, kvg, wq, wkv, out):
    rows = qg.shape[0] // g
    for i in range(start, g, 2):
        tok = slice(i * rows, (i + 1) * rows)
        o = dot(qg[tok, :], wq[...], 1, 1) + dot(kvg[tok, :], wkv[...], 1, 1)
        out[(i // 2) * rows : (i // 2 + 1) * rows, :] = o.astype(out.dtype)


def key_side_kernel(g, p, hp, *refs):
    parts = refs[:p]
    val, feat, sig, om, qg, wq, wkv = refs[p : p + 7]
    odd, kvg = refs[p + 7 :]
    hd, m = om.shape[1], om.shape[2]
    base = hp * m
    cols = hp * hd
    tail = summed(parts, base, parts[0].shape[0])
    for h in range(hp):
        gh = summed(parts, h * m, (h + 1) * m).astype(BF16)
        col = slice(h * hd, (h + 1) * hd)
        fg = dot(val[:, col], gh, 1, 1) + get_total(tail, base // hd, h, m)
        kvg[:, cols + h * hd : cols + (h + 1) * hd] = dot(feat[:, h * m : (h + 1) * m], gh).astype(BF16)
        pg = (fg * sig[:, h * m : (h + 1) * m]).astype(BF16)
        kvg[:, col] = dot(pg, om[h], 1, 1).astype(BF16)
    products(g, 1, qg, kvg, wq, wkv, odd)


def even_kernel(g, qg, kvg, wq, wkv, even):
    products(g, 0, qg, kvg, wq, wkv, even)


def local(events, offsets, cotangent, query_weight, key_weight, value_weight, omega):
    heads, hd, m = omega.shape
    n_seq, n_sub = lax.axis_size("seq"), lax.axis_size("sub")
    rows, width = events.shape
    loss_scale = math.sqrt(rows * n_seq * n_sub)
    g = math.gcd(heads, n_seq)
    r = n_seq // g
    hp = heads // g
    p = r * n_sub
    t = g * rows
    cols = hp * hd
    srows = hp * m + -(-2 * hp * m // hd // 16) * 16

    def over_seq(x, k):
        return lax.ppermute(x, "seq", [(i, i ^ k) for i in range(n_seq)])

    def over_sub(x, k):
        return lax.ppermute(x, "sub", [(i, i ^ k) for i in range(n_sub)])

    def to_all(own, send):
        parts = [own]
        for j in range(r):
            for k in range(n_sub):
                if j or k:
                    perm = [
                        (a * n_sub + b, (a ^ (j * g)) * n_sub + (b ^ k))
                        for a in range(n_seq)
                        for b in range(n_sub)
                    ]
                    parts.append(lax.ppermute(send, ("seq", "sub"), perm))
        return parts

    wrows = key_weight.shape[0]
    split = lax.axis_size("grp") == 2 and wrows % 32 == 0
    wouts = [((wrows, 2 * cols), BF16), ((wrows, cols), BF16)]
    if split:
        wouts.append(((wrows // 2, 2 * cols), BF16))
    pieces = list(call(
        functools.partial(weight_kernel, g, cols, split),
        wouts,
        [key_weight, value_weight, query_weight],
        0,
        in_specs=[HBM] * 3,
        scratch_shapes=[pltpu.SemaphoreType.DMA((5 if split else 3,))],
    ))

    def weight_rows(i, split):
        if not split:
            return [pieces[i]] + [over_sub(pieces[i], k) for k in range(1, n_sub)]
        far = []
        for k in range(2, n_sub):
            part = over_sub(pieces[i + 2], k)
            far += [part, lax.ppermute(part, "grp", [(0, 1), (1, 0)])]
        return [pieces[i], over_sub(pieces[i], 1)] + far

    kvs = weight_rows(0, split)

    events, offsets, _ = lax.optimization_barrier((events, offsets, pieces[0]))
    half = width // 2
    frequency = jnp.exp(jnp.arange(half, dtype=F32) * (-2.0 * math.log(10000.0) / width))
    angles = offsets.astype(F32)[:, None] * frequency[None, :]
    bufs = call(
        functools.partial(input_kernel, g, 2 * cols),
        [((rows, width + 2 * cols), BF16)] * (g // 2),
        [events, jnp.sin(angles), jnp.cos(angles), cotangent],
        16 * 2**30,
    )
    xs = [bufs[0]] * g
    for k in range(2, g, 2):
        xs[k] = over_seq(bufs[k // 2], k)
    xs[1] = over_seq(bufs[0], 1)
    arrived = kvs[1:2] + kvs[2::2] if split else kvs[1:]
    xs[2:], _ = lax.optimization_barrier((xs[2:], arrived[1:]))
    for k in range(3, g, 2):
        xs[k] = over_seq(xs[k ^ 1], 1)
    pieces, _ = lax.optimization_barrier((pieces, arrived + xs[1:2]))
    qs = weight_rows(1, False)
    om = lax.dynamic_slice_in_dim(omega, (lax.axis_index("seq") % g) * hp, hp, 0)

    flop = 2 * t * width * cols
    summary_out = [((srows, hd), F32), ((srows, hd), BF16)]
    wkv_full, key_feat, key_sig, val, own, send = call(
        functools.partial(key_value_kernel, g, n_sub, len(kvs), hp, width),
        [((width, 2 * cols), BF16), ((t, hp * m), BF16), ((t, hp * m), F32), ((t, cols), BF16)] + summary_out,
        [*xs, *kvs, om],
        8 * flop,
    )
    summary = to_all(own, send)
    wq_full, query_feat, query_sig = call(
        functools.partial(query_kernel, g, n_sub, len(qs), hp, width),
        [((width, cols), BF16), ((t, hp * m), BF16), ((t, hp * m), F32)],
        [*xs, *qs, om],
        8 * flop,
    )
    total_half, summary_half, scaled_half, norm, own, send = call(
        functools.partial(query_side_kernel, g, p, hp, m, width, loss_scale),
        [((1, hp * m), BF16), ((hp * m, hd), BF16), ((t, cols), BF16), ((t, hp), F32)] + summary_out,
        [*summary, *xs, query_feat],
        8 * flop,
    )
    summary_grad = to_all(own, send)
    (query_grad,) = call(
        functools.partial(query_grad_kernel, hp),
        [((t, cols), BF16)],
        [scaled_half, summary_half, norm, total_half, query_sig, om],
        4 * flop,
    )
    odd, key_value_grad = call(
        functools.partial(key_side_kernel, g, p, hp),
        [((t // 2, width), BF16), ((t, 2 * cols), BF16)],
        [*summary_grad, val, key_feat, key_sig, om, query_grad, wq_full, wkv_full],
        8 * flop,
    )
    got = over_seq(odd, 1)
    (even,) = call(
        functools.partial(even_kernel, g),
        [((t // 2, width), F32)],
        [query_grad, key_value_grad, wq_full, wkv_full],
        8 * flop,
    )
    both = even + got.astype(F32)
    out = both[:rows]
    for k in range(2, g, 2):
        at = (k // 2) * rows
        out = out + over_seq(both[at : at + rows].astype(BF16), k).astype(F32)
    return out.astype(BF16)


def solution(mesh):
    in_specs = (
        P(("grp", "seq", "sub"), None),
        P(("grp", "seq", "sub")),
        P(("grp", "seq", "sub"), None),
        P("sub", None),
        P("sub", None),
        P("sub", None),
        P(),
    )
    out_specs = P(("grp", "seq", "sub"), None)
    return jax.shard_map(local, mesh=mesh, in_specs=in_specs, out_specs=out_specs, check_vma=False)
```

```python
import functools
import math

import jax
import jax.numpy as jnp
from jax import lax
from jax.experimental import pallas as pl
from jax.experimental.pallas import tpu as pltpu
from jax.sharding import PartitionSpec as P

F32 = jnp.float32
BF16 = jnp.bfloat16
HBM = pl.BlockSpec(memory_space=pltpu.HBM)


def dot(a, b, ca=1, cb=0):
    return lax.dot_general(a, b, (((ca,), (cb,)), ((), ())), preferred_element_type=F32)


def soft_and_sigmoid(u):
    e = jnp.exp(-jnp.abs(u))
    series = e * (1.0 + e * (-0.5 + e * (1.0 / 3.0)))
    soft = jnp.maximum(u, 0.0) + jnp.where(e < 1e-3, series, jnp.log(1.0 + e))
    r = 1.0 / (1.0 + e)
    return soft, jnp.where(u >= 0.0, r, e * r)


def call(body, outs, args, flops, vmem=24, **kw):
    nbytes = sum(a.size * a.dtype.itemsize for a in args)
    return pl.pallas_call(
        body,
        out_shape=[jax.ShapeDtypeStruct(s, d) for s, d in outs],
        compiler_params=pltpu.CompilerParams(vmem_limit_bytes=vmem * 2**20),
        cost_estimate=pl.CostEstimate(flops=flops, bytes_accessed=nbytes, transcendentals=0),
        **kw,
    )(*args)


def weight_kernel(g, cols, split, *refs):
    ws, outs, sems = refs[:3], refs[3:-1], refs[-1]
    at = pl.ds(pl.multiple_of((lax.axis_index("seq") % g) * cols, cols), cols)
    half = ws[0].shape[0] // 2
    copies = []
    for i, w in enumerate(ws):
        to = slice(i * cols, (i + 1) * cols)
        pairs = [(w.at[:, at], outs[0].at[:, to])]
        if split:
            rows = pl.ds(pl.multiple_of(lax.axis_index("grp") * half, half), half)
            pairs.append((w.at[rows, at], outs[1].at[:, to]))
        copies += pairs
    copies = [pltpu.make_async_copy(a, b, sems.at[i]) for i, (a, b) in enumerate(copies)]
    for c in copies:
        c.start()
    for c in copies:
        c.wait()


def input_kernel(g, pair, events, sines, cosines, cot, *outs):
    width = events.shape[1]
    half = width // 2
    mine = (lax.axis_index("seq") % g) // 2
    left = (events[:, :half].astype(F32) + sines[...]).astype(BF16)
    right = (events[:, half:].astype(F32) + cosines[...]).astype(BF16)
    for k, out in enumerate(outs):
        out[:, :half] = left
        out[:, half:width] = right
        out[:, width:] = cot[:, pl.ds(pl.multiple_of((mine ^ k) * pair, pair), pair)]


def place_rows(full, parts, n):
    z = lax.axis_index("sub")
    rows = parts[0].shape[0]
    spots = [(k, 0) for k in range(n)]
    if len(parts) > n:
        half, mine = rows // 2, lax.axis_index("grp")
        spots = [(0, 0), (1, 0)]
        for k in range(2, n):
            spots += [(k, mine * half), (k, half - mine * half)]
    for (k, start), part in zip(spots, parts):
        size = part.shape[0]
        full[pl.ds(pl.multiple_of((z ^ k) * rows + start, size), size), :] = part[...]


def features(act, om, h, i, feat, sig):
    hd, m = om.shape[1], om.shape[2]
    rows = act.shape[0]
    soft, s = soft_and_sigmoid(dot(act[:, h * hd : (h + 1) * hd], om[h]))
    soft = soft.astype(BF16)
    at = (slice(i * rows, (i + 1) * rows), slice(h * m, (h + 1) * m))
    feat[at] = soft
    sig[at] = s
    return soft


def put_total(own, send, base, extra, total):
    hd = own.shape[1]
    n = total.shape[1] // hd
    for j in range(n):
        piece = total[:, j * hd : (j + 1) * hd]
        high = piece.astype(BF16)
        own[base + j : base + j + 1, :] = piece
        send[base + j : base + j + 1, :] = high
        own[base + extra + j : base + extra + j + 1, :] = jnp.zeros_like(piece)
        send[base + extra + j : base + extra + j + 1, :] = (piece - high.astype(F32)).astype(BF16)


def get_total(tail, extra, h, m):
    hd = tail.shape[1]
    n = m // hd
    rows = [
        tail[h * n + j : h * n + j + 1, :] + tail[extra + h * n + j : extra + h * n + j + 1, :]
        for j in range(n)
    ]
    return jnp.concatenate(rows, axis=1)


def summed(parts, lo, hi):
    out = parts[0][lo:hi, :]
    for part in parts[1:]:
        out = out + part[lo:hi, :].astype(F32)
    return out


def key_value_kernel(g, n, nw, hp, width, *refs):
    xs, ws, om = refs[:g], refs[g : g + nw], refs[g + nw]
    w_full, feat, sig, val, own, send = refs[g + nw + 1 :]
    hd, m = om.shape[1], om.shape[2]
    cols = hp * hd
    place_rows(w_full, ws, n)
    rows = xs[0].shape[0]
    sums = [jnp.zeros((1, m), F32) for _ in range(hp)]
    for i, x in enumerate(xs):
        act = dot(x[:, :width], w_full[:, : 2 * cols]).astype(BF16)
        val[i * rows : (i + 1) * rows, :] = act[:, cols:]
        for h in range(hp):
            soft = features(act, om, h, i, feat, sig)
            sums[h] = sums[h] + jnp.sum(soft.astype(F32), axis=0, keepdims=True)
    base = hp * m
    own[base:, :] = jnp.zeros_like(own[base:, :])
    send[base:, :] = jnp.zeros_like(send[base:, :])
    for h in range(hp):
        s = dot(feat[:, h * m : (h + 1) * m], val[:, h * hd : (h + 1) * hd], 0, 0)
        own[h * m : (h + 1) * m, :] = s
        send[h * m : (h + 1) * m, :] = s.astype(BF16)
    put_total(own, send, base, hp * m // hd, jnp.concatenate(sums, axis=1))


def query_kernel(g, hp, width, *refs):
    xs, w_full, om = refs[:g], refs[g], refs[g + 1]
    feat, sig = refs[g + 2 :]
    cols = hp * om.shape[1]
    for i, x in enumerate(xs):
        act = dot(x[:, :width], w_full[:, 2 * cols :]).astype(BF16)
        for h in range(hp):
            features(act, om, h, i, feat, sig)


def query_side_kernel(g, p, hp, m, width, loss_scale, *refs):
    parts, xs, feat = refs[:p], refs[p : p + g], refs[p + g]
    total_half, summary_half, scaled_half, norm, own, send = refs[p + g + 1 :]
    hd = summary_half.shape[1]
    cols = hp * hd
    base = hp * m
    extra = base // hd
    summary_half[...] = summed(parts, 0, base).astype(BF16)
    tail = summed(parts, base, parts[0].shape[0])
    core = lax.axis_index("seq") % 2
    rows = xs[0].shape[0]
    own[base:, :] = jnp.zeros_like(own[base:, :])
    send[base:, :] = jnp.zeros_like(send[base:, :])
    sums = []
    for h in range(hp):
        row = get_total(tail, extra, h, m).astype(BF16)
        total_half[:, h * m : (h + 1) * m] = row
        spread = jnp.broadcast_to(row.astype(F32), (hd, m)).astype(BF16)
        acc = jnp.zeros((1, m), F32)
        for i in range(g):
            tok = slice(i * rows, (i + 1) * rows)
            qf = feat[tok, h * m : (h + 1) * m]
            at = pl.multiple_of(width + core * cols + h * hd, hd)
            denom = dot(qf, spread, 1, 1)
            numer = dot(qf, summary_half[h * m : (h + 1) * m, :])
            scaled = xs[i][:, pl.ds(at, hd)].astype(F32) * loss_scale / denom
            scaled_half[tok, h * hd : (h + 1) * hd] = scaled.astype(BF16)
            ng = -jnp.sum(scaled * (numer / denom), axis=1, keepdims=True)
            norm[tok, h : h + 1] = ng
            acc = acc + jnp.sum(qf.astype(F32) * ng.astype(BF16).astype(F32), axis=0, keepdims=True)
        s = dot(feat[:, h * m : (h + 1) * m], scaled_half[:, h * hd : (h + 1) * hd], 0, 0)
        own[h * m : (h + 1) * m, :] = s
        send[h * m : (h + 1) * m, :] = s.astype(BF16)
        sums.append(acc)
    put_total(own, send, base, extra, jnp.concatenate(sums, axis=1))


def query_grad_kernel(hp, scaled_half, summary_half, norm, total_half, sig, om, out):
    hd, m = om.shape[1], om.shape[2]
    for h in range(hp):
        fg = dot(scaled_half[:, h * hd : (h + 1) * hd], summary_half[h * m : (h + 1) * m, :], 1, 1)
        fg = fg + norm[:, h : h + 1] * total_half[:, h * m : (h + 1) * m].astype(F32)
        pg = (fg * sig[:, h * m : (h + 1) * m]).astype(BF16)
        out[:, h * hd : (h + 1) * hd] = dot(pg, om[h], 1, 1).astype(BF16)


def products(g, start, qg, kvg, w, out):
    rows = qg.shape[0] // g
    two = kvg.shape[1]
    for i in range(start, g, 2):
        tok = slice(i * rows, (i + 1) * rows)
        o = dot(kvg[tok, :], w[:, :two], 1, 1) + dot(qg[tok, :], w[:, two:], 1, 1)
        out[(i // 2) * rows : (i // 2 + 1) * rows, :] = o.astype(out.dtype)


def key_side_kernel(g, p, hp, *refs):
    parts = refs[:p]
    val, feat, sig, om, qg, w = refs[p : p + 6]
    odd, kvg = refs[p + 6 :]
    hd, m = om.shape[1], om.shape[2]
    base = hp * m
    cols = hp * hd
    tail = summed(parts, base, parts[0].shape[0])
    for h in range(hp):
        gh = summed(parts, h * m, (h + 1) * m).astype(BF16)
        col = slice(h * hd, (h + 1) * hd)
        fg = dot(val[:, col], gh, 1, 1) + get_total(tail, base // hd, h, m)
        kvg[:, cols + h * hd : cols + (h + 1) * hd] = dot(feat[:, h * m : (h + 1) * m], gh).astype(BF16)
        pg = (fg * sig[:, h * m : (h + 1) * m]).astype(BF16)
        kvg[:, col] = dot(pg, om[h], 1, 1).astype(BF16)
    products(g, 1, qg, kvg, w, odd)


def even_kernel(g, qg, kvg, w, even):
    products(g, 0, qg, kvg, w, even)


def local(events, offsets, cotangent, query_weight, key_weight, value_weight, omega):
    heads, hd, m = omega.shape
    n_seq, n_sub = lax.axis_size("seq"), lax.axis_size("sub")
    rows, width = events.shape
    loss_scale = math.sqrt(rows * n_seq * n_sub)
    g = math.gcd(heads, n_seq)
    r = n_seq // g
    hp = heads // g
    p = r * n_sub
    t = g * rows
    cols = hp * hd
    srows = hp * m + -(-2 * hp * m // hd // 16) * 16

    def over_seq(x, k):
        return lax.ppermute(x, "seq", [(i, i ^ k) for i in range(n_seq)])

    def over_sub(x, k):
        return lax.ppermute(x, "sub", [(i, i ^ k) for i in range(n_sub)])

    def to_all(own, send):
        parts = [own]
        for j in range(r):
            for k in range(n_sub):
                if j or k:
                    perm = [
                        (a * n_sub + b, (a ^ (j * g)) * n_sub + (b ^ k))
                        for a in range(n_seq)
                        for b in range(n_sub)
                    ]
                    parts.append(lax.ppermute(send, ("seq", "sub"), perm))
        return parts

    wrows = key_weight.shape[0]
    split = lax.axis_size("grp") == 2 and wrows % 32 == 0
    wouts = [((wrows, 3 * cols), BF16), ((wrows // 2, 3 * cols), BF16)]
    pieces = call(
        functools.partial(weight_kernel, g, cols, split),
        wouts if split else wouts[:1],
        [key_weight, value_weight, query_weight],
        0,
        vmem=56,
        in_specs=[HBM] * 3,
        scratch_shapes=[pltpu.SemaphoreType.DMA((6 if split else 3,))],
    )
    if split:
        arrived = [over_sub(pieces[0], 1)] + [over_sub(pieces[1], k) for k in range(2, n_sub)]
        ws = [pieces[0], arrived[0]]
        for part in arrived[1:]:
            ws += [part, lax.ppermute(part, "grp", [(0, 1), (1, 0)])]
    else:
        arrived = [over_sub(pieces[0], k) for k in range(1, n_sub)]
        ws = [pieces[0]] + arrived

    events, offsets, _ = lax.optimization_barrier((events, offsets, pieces[0]))
    half = width // 2
    frequency = jnp.exp(jnp.arange(half, dtype=F32) * (-2.0 * math.log(10000.0) / width))
    angles = offsets.astype(F32)[:, None] * frequency[None, :]
    bufs = call(
        functools.partial(input_kernel, g, 2 * cols),
        [((rows, width + 2 * cols), BF16)] * (g // 2),
        [events, jnp.sin(angles), jnp.cos(angles), cotangent],
        16 * 2**30,
    )
    xs = [bufs[0]] * g
    for k in range(2, g, 2):
        xs[k] = over_seq(bufs[k // 2], k)
    xs[1] = over_seq(bufs[0], 1)
    xs[2:], _ = lax.optimization_barrier((xs[2:], arrived))
    for k in range(3, g, 2):
        xs[k] = over_seq(xs[k ^ 1], 1)
    om = lax.dynamic_slice_in_dim(omega, (lax.axis_index("seq") % g) * hp, hp, 0)

    flop = 2 * t * width * cols
    summary_out = [((srows, hd), F32), ((srows, hd), BF16)]
    w_full, key_feat, key_sig, val, own, send = call(
        functools.partial(key_value_kernel, g, n_sub, len(ws), hp, width),
        [((width, 3 * cols), BF16), ((t, hp * m), BF16), ((t, hp * m), F32), ((t, cols), BF16)] + summary_out,
        [*xs, *ws, om],
        8 * flop,
    )
    summary = to_all(own, send)
    query_feat, query_sig = call(
        functools.partial(query_kernel, g, hp, width),
        [((t, hp * m), BF16), ((t, hp * m), F32)],
        [*xs, w_full, om],
        8 * flop,
    )
    total_half, summary_half, scaled_half, norm, own, send = call(
        functools.partial(query_side_kernel, g, p, hp, m, width, loss_scale),
        [((1, hp * m), BF16), ((hp * m, hd), BF16), ((t, cols), BF16), ((t, hp), F32)] + summary_out,
        [*summary, *xs, query_feat],
        8 * flop,
    )
    summary_grad = to_all(own, send)
    (query_grad,) = call(
        functools.partial(query_grad_kernel, hp),
        [((t, cols), BF16)],
        [scaled_half, summary_half, norm, total_half, query_sig, om],
        4 * flop,
    )
    odd, key_value_grad = call(
        functools.partial(key_side_kernel, g, p, hp),
        [((t // 2, width), BF16), ((t, 2 * cols), BF16)],
        [*summary_grad, val, key_feat, key_sig, om, query_grad, w_full],
        8 * flop,
    )
    got = over_seq(odd, 1)
    (even,) = call(
        functools.partial(even_kernel, g),
        [((t // 2, width), F32)],
        [query_grad, key_value_grad, w_full],
        8 * flop,
    )
    both = even + got.astype(F32)
    out = both[:rows]
    for k in range(2, g, 2):
        at = (k // 2) * rows
        out = out + over_seq(both[at : at + rows].astype(BF16), k).astype(F32)
    return out.astype(BF16)


def solution(mesh):
    in_specs = (
        P(("grp", "seq", "sub"), None),
        P(("grp", "seq", "sub")),
        P(("grp", "seq", "sub"), None),
        P("sub", None),
        P("sub", None),
        P("sub", None),
        P(),
    )
    out_specs = P(("grp", "seq", "sub"), None)
    return jax.shard_map(local, mesh=mesh, in_specs=in_specs, out_specs=out_specs, check_vma=False)
```

```python
import functools
import math

import jax
import jax.numpy as jnp
from jax import lax
from jax.experimental import pallas as pl
from jax.experimental.pallas import tpu as pltpu
from jax.sharding import PartitionSpec as P

F32 = jnp.float32
BF16 = jnp.bfloat16
HBM = pl.BlockSpec(memory_space=pltpu.HBM)


def dot(a, b, ca=1, cb=0):
    return lax.dot_general(a, b, (((ca,), (cb,)), ((), ())), preferred_element_type=F32)


def soft_and_sigmoid(u):
    e = jnp.exp(-jnp.abs(u))
    series = e * (1.0 + e * (-0.5 + e * (1.0 / 3.0)))
    soft = jnp.maximum(u, 0.0) + jnp.where(e < 1e-3, series, jnp.log(1.0 + e))
    r = 1.0 / (1.0 + e)
    return soft, jnp.where(u >= 0.0, r, e * r)


def call(body, outs, args, flops, vmem=24, **kw):
    nbytes = sum(a.size * a.dtype.itemsize for a in args)
    return pl.pallas_call(
        body,
        out_shape=[jax.ShapeDtypeStruct(s, d) for s, d in outs],
        compiler_params=pltpu.CompilerParams(vmem_limit_bytes=vmem * 2**20),
        cost_estimate=pl.CostEstimate(flops=flops, bytes_accessed=nbytes, transcendentals=0),
        **kw,
    )(*args)


def weight_kernel(g, cols, split, wk, wv, wq, *refs):
    outs, sems = refs[:-1], refs[-1]
    at = pl.ds(pl.multiple_of((lax.axis_index("seq") % g) * cols, cols), cols)
    pairs = [(wk.at[:, at], outs[0].at[:, :cols]), (wv.at[:, at], outs[0].at[:, cols:]), (wq.at[:, at], outs[1])]
    if split:
        half = wk.shape[0] // 2
        rows = pl.ds(pl.multiple_of(lax.axis_index("grp") * half, half), half)
        pairs += [
            (wk.at[rows, at], outs[2].at[:, :cols]),
            (wv.at[rows, at], outs[2].at[:, cols:]),
        ]
    copies = [pltpu.make_async_copy(a, b, sems.at[i]) for i, (a, b) in enumerate(pairs)]
    for c in copies:
        c.start()
    for c in copies:
        c.wait()


def input_kernel(g, pair, events, sines, cosines, cot, *outs):
    width = events.shape[1]
    half = width // 2
    mine = (lax.axis_index("seq") % g) // 2
    left = (events[:, :half].astype(F32) + sines[...]).astype(BF16)
    right = (events[:, half:].astype(F32) + cosines[...]).astype(BF16)
    for k, out in enumerate(outs):
        out[:, :half] = left
        out[:, half:width] = right
        out[:, width:] = cot[:, pl.ds(pl.multiple_of((mine ^ k) * pair, pair), pair)]


def place_rows(full, parts, n):
    z = lax.axis_index("sub")
    rows = parts[0].shape[0]
    spots = [(k, 0) for k in range(n)]
    if len(parts) > n:
        half, mine = rows // 2, lax.axis_index("grp")
        spots = [(0, 0), (1, 0)]
        for k in range(2, n):
            spots += [(k, mine * half), (k, half - mine * half)]
    for (k, start), part in zip(spots, parts):
        size = part.shape[0]
        full[pl.ds(pl.multiple_of((z ^ k) * rows + start, size), size), :] = part[...]


def features(act, om, h, i, feat, sig):
    hd, m = om.shape[1], om.shape[2]
    rows = act.shape[0]
    soft, s = soft_and_sigmoid(dot(act[:, h * hd : (h + 1) * hd], om[h]))
    soft = soft.astype(BF16)
    at = (slice(i * rows, (i + 1) * rows), slice(h * m, (h + 1) * m))
    feat[at] = soft
    sig[at] = s
    return soft


def put_total(own, send, base, extra, total):
    hd = own.shape[1]
    n = total.shape[1] // hd
    for j in range(n):
        piece = total[:, j * hd : (j + 1) * hd]
        high = piece.astype(BF16)
        own[base + j : base + j + 1, :] = piece
        send[base + j : base + j + 1, :] = high
        own[base + extra + j : base + extra + j + 1, :] = jnp.zeros_like(piece)
        send[base + extra + j : base + extra + j + 1, :] = (piece - high.astype(F32)).astype(BF16)


def get_total(tail, extra, h, m):
    hd = tail.shape[1]
    n = m // hd
    rows = [
        tail[h * n + j : h * n + j + 1, :] + tail[extra + h * n + j : extra + h * n + j + 1, :]
        for j in range(n)
    ]
    return jnp.concatenate(rows, axis=1)


def summed(parts, lo, hi):
    out = parts[0][lo:hi, :]
    for part in parts[1:]:
        out = out + part[lo:hi, :].astype(F32)
    return out


def key_value_kernel(g, n, nw, hp, width, *refs):
    xs, ws, om = refs[:g], refs[g : g + nw], refs[g + nw]
    w_full, feat, sig, val, own, send = refs[g + nw + 1 :]
    hd, m = om.shape[1], om.shape[2]
    cols = hp * hd
    place_rows(w_full, ws, n)
    rows = xs[0].shape[0]
    sums = [jnp.zeros((1, m), F32) for _ in range(hp)]
    for i, x in enumerate(xs):
        act = dot(x[:, :width], w_full[...]).astype(BF16)
        val[i * rows : (i + 1) * rows, :] = act[:, cols:]
        for h in range(hp):
            soft = features(act, om, h, i, feat, sig)
            sums[h] = sums[h] + jnp.sum(soft.astype(F32), axis=0, keepdims=True)
    base = hp * m
    own[base:, :] = jnp.zeros_like(own[base:, :])
    send[base:, :] = jnp.zeros_like(send[base:, :])
    for h in range(hp):
        s = dot(feat[:, h * m : (h + 1) * m], val[:, h * hd : (h + 1) * hd], 0, 0)
        own[h * m : (h + 1) * m, :] = s
        send[h * m : (h + 1) * m, :] = s.astype(BF16)
    put_total(own, send, base, hp * m // hd, jnp.concatenate(sums, axis=1))


def query_kernel(g, n, nw, hp, width, *refs):
    xs, ws, om = refs[:g], refs[g : g + nw], refs[g + nw]
    w_full, feat, sig = refs[g + nw + 1 :]
    place_rows(w_full, ws, n)
    for i, x in enumerate(xs):
        act = dot(x[:, :width], w_full[...]).astype(BF16)
        for h in range(hp):
            features(act, om, h, i, feat, sig)


def query_side_kernel(g, p, hp, m, width, loss_scale, *refs):
    parts, xs, feat = refs[:p], refs[p : p + g], refs[p + g]
    total_half, summary_half, scaled_half, norm, own, send = refs[p + g + 1 :]
    hd = summary_half.shape[1]
    cols = hp * hd
    base = hp * m
    extra = base // hd
    summary_half[...] = summed(parts, 0, base).astype(BF16)
    tail = summed(parts, base, parts[0].shape[0])
    core = lax.axis_index("seq") % 2
    rows = xs[0].shape[0]
    own[base:, :] = jnp.zeros_like(own[base:, :])
    send[base:, :] = jnp.zeros_like(send[base:, :])
    sums = []
    for h in range(hp):
        row = get_total(tail, extra, h, m).astype(BF16)
        total_half[:, h * m : (h + 1) * m] = row
        spread = jnp.broadcast_to(row.astype(F32), (hd, m)).astype(BF16)
        acc = jnp.zeros((1, m), F32)
        for i in range(g):
            tok = slice(i * rows, (i + 1) * rows)
            qf = feat[tok, h * m : (h + 1) * m]
            at = pl.multiple_of(width + core * cols + h * hd, hd)
            denom = dot(qf, spread, 1, 1)
            numer = dot(qf, summary_half[h * m : (h + 1) * m, :])
            scaled = xs[i][:, pl.ds(at, hd)].astype(F32) * loss_scale / denom
            scaled_half[tok, h * hd : (h + 1) * hd] = scaled.astype(BF16)
            ng = -jnp.sum(scaled * (numer / denom), axis=1, keepdims=True)
            norm[tok, h : h + 1] = ng
            acc = acc + jnp.sum(qf.astype(F32) * ng.astype(BF16).astype(F32), axis=0, keepdims=True)
        s = dot(feat[:, h * m : (h + 1) * m], scaled_half[:, h * hd : (h + 1) * hd], 0, 0)
        own[h * m : (h + 1) * m, :] = s
        send[h * m : (h + 1) * m, :] = s.astype(BF16)
        sums.append(acc)
    put_total(own, send, base, extra, jnp.concatenate(sums, axis=1))


def query_grad_kernel(hp, scaled_half, summary_half, norm, total_half, sig, om, out):
    hd, m = om.shape[1], om.shape[2]
    for h in range(hp):
        fg = dot(scaled_half[:, h * hd : (h + 1) * hd], summary_half[h * m : (h + 1) * m, :], 1, 1)
        fg = fg + norm[:, h : h + 1] * total_half[:, h * m : (h + 1) * m].astype(F32)
        pg = (fg * sig[:, h * m : (h + 1) * m]).astype(BF16)
        out[:, h * hd : (h + 1) * hd] = dot(pg, om[h], 1, 1).astype(BF16)


def products(g, start, qg, kvg, wq, wkv, out):
    rows = qg.shape[0] // g
    for i in range(start, g, 2):
        tok = slice(i * rows, (i + 1) * rows)
        o = dot(qg[tok, :], wq[...], 1, 1) + dot(kvg[tok, :], wkv[...], 1, 1)
        out[(i // 2) * rows : (i // 2 + 1) * rows, :] = o.astype(out.dtype)


def key_side_kernel(g, p, hp, *refs):
    parts = refs[:p]
    val, feat, sig, om, qg, wq, wkv = refs[p : p + 7]
    odd, kvg = refs[p + 7 :]
    hd, m = om.shape[1], om.shape[2]
    base = hp * m
    cols = hp * hd
    tail = summed(parts, base, parts[0].shape[0])
    for h in range(hp):
        gh = summed(parts, h * m, (h + 1) * m).astype(BF16)
        col = slice(h * hd, (h + 1) * hd)
        fg = dot(val[:, col], gh, 1, 1) + get_total(tail, base // hd, h, m)
        kvg[:, cols + h * hd : cols + (h + 1) * hd] = dot(feat[:, h * m : (h + 1) * m], gh).astype(BF16)
        pg = (fg * sig[:, h * m : (h + 1) * m]).astype(BF16)
        kvg[:, col] = dot(pg, om[h], 1, 1).astype(BF16)
    products(g, 1, qg, kvg, wq, wkv, odd)


def even_kernel(g, qg, kvg, wq, wkv, even):
    products(g, 0, qg, kvg, wq, wkv, even)


def local(events, offsets, cotangent, query_weight, key_weight, value_weight, omega):
    heads, hd, m = omega.shape
    n_seq, n_sub = lax.axis_size("seq"), lax.axis_size("sub")
    rows, width = events.shape
    loss_scale = math.sqrt(rows * n_seq * n_sub)
    g = math.gcd(heads, n_seq)
    r = n_seq // g
    hp = heads // g
    p = r * n_sub
    t = g * rows
    cols = hp * hd
    srows = hp * m + -(-2 * hp * m // hd // 16) * 16

    def over_seq(x, k):
        return lax.ppermute(x, "seq", [(i, i ^ k) for i in range(n_seq)])

    def over_sub(x, k):
        return lax.ppermute(x, "sub", [(i, i ^ k) for i in range(n_sub)])

    def to_all(own, send):
        parts = [own]
        for j in range(r):
            for k in range(n_sub):
                if j or k:
                    perm = [
                        (a * n_sub + b, (a ^ (j * g)) * n_sub + (b ^ k))
                        for a in range(n_seq)
                        for b in range(n_sub)
                    ]
                    parts.append(lax.ppermute(send, ("seq", "sub"), perm))
        return parts

    wrows = key_weight.shape[0]
    split = lax.axis_size("grp") == 2 and wrows % 32 == 0
    wouts = [((wrows, 2 * cols), BF16), ((wrows, cols), BF16)]
    if split:
        wouts.append(((wrows // 2, 2 * cols), BF16))
    pieces = list(call(
        functools.partial(weight_kernel, g, cols, split),
        wouts,
        [key_weight, value_weight, query_weight],
        0,
        vmem=56,
        in_specs=[HBM] * 3,
        scratch_shapes=[pltpu.SemaphoreType.DMA((5 if split else 3,))],
    ))

    def weight_rows(i, split):
        if not split:
            return [pieces[i]] + [over_sub(pieces[i], k) for k in range(1, n_sub)]
        far = []
        for k in range(2, n_sub):
            part = over_sub(pieces[i + 2], k)
            far += [part, lax.ppermute(part, "grp", [(0, 1), (1, 0)])]
        return [pieces[i], over_sub(pieces[i], 1)] + far

    kvs = weight_rows(0, split)

    events, offsets, _ = lax.optimization_barrier((events, offsets, pieces[0]))
    half = width // 2
    frequency = jnp.exp(jnp.arange(half, dtype=F32) * (-2.0 * math.log(10000.0) / width))
    angles = offsets.astype(F32)[:, None] * frequency[None, :]
    bufs = call(
        functools.partial(input_kernel, g, 2 * cols),
        [((rows, width + 2 * cols), BF16)] * (g // 2),
        [events, jnp.sin(angles), jnp.cos(angles), cotangent],
        16 * 2**30,
    )
    xs = [bufs[0]] * g
    for k in range(2, g, 2):
        xs[k] = over_seq(bufs[k // 2], k)
    xs[1] = over_seq(bufs[0], 1)
    arrived = kvs[1:2] + kvs[2::2] if split else kvs[1:]
    xs[2:], _ = lax.optimization_barrier((xs[2:], arrived))
    for k in range(3, g, 2):
        xs[k] = over_seq(xs[k ^ 1], 1)
    pieces, _ = lax.optimization_barrier((pieces, arrived + xs[1:2]))
    qs = weight_rows(1, False)
    om = lax.dynamic_slice_in_dim(omega, (lax.axis_index("seq") % g) * hp, hp, 0)

    flop = 2 * t * width * cols
    summary_out = [((srows, hd), F32), ((srows, hd), BF16)]
    wkv_full, key_feat, key_sig, val, own, send = call(
        functools.partial(key_value_kernel, g, n_sub, len(kvs), hp, width),
        [((width, 2 * cols), BF16), ((t, hp * m), BF16), ((t, hp * m), F32), ((t, cols), BF16)] + summary_out,
        [*xs, *kvs, om],
        8 * flop,
    )
    summary = to_all(own, send)
    wq_full, query_feat, query_sig = call(
        functools.partial(query_kernel, g, n_sub, len(qs), hp, width),
        [((width, cols), BF16), ((t, hp * m), BF16), ((t, hp * m), F32)],
        [*xs, *qs, om],
        8 * flop,
    )
    total_half, summary_half, scaled_half, norm, own, send = call(
        functools.partial(query_side_kernel, g, p, hp, m, width, loss_scale),
        [((1, hp * m), BF16), ((hp * m, hd), BF16), ((t, cols), BF16), ((t, hp), F32)] + summary_out,
        [*summary, *xs, query_feat],
        8 * flop,
    )
    summary_grad = to_all(own, send)
    (query_grad,) = call(
        functools.partial(query_grad_kernel, hp),
        [((t, cols), BF16)],
        [scaled_half, summary_half, norm, total_half, query_sig, om],
        4 * flop,
    )
    odd, key_value_grad = call(
        functools.partial(key_side_kernel, g, p, hp),
        [((t // 2, width), BF16), ((t, 2 * cols), BF16)],
        [*summary_grad, val, key_feat, key_sig, om, query_grad, wq_full, wkv_full],
        8 * flop,
    )
    got = over_seq(odd, 1)
    (even,) = call(
        functools.partial(even_kernel, g),
        [((t // 2, width), F32)],
        [query_grad, key_value_grad, wq_full, wkv_full],
        8 * flop,
    )
    both = even + got.astype(F32)
    out = both[:rows]
    for k in range(2, g, 2):
        at = (k // 2) * rows
        out = out + over_seq(both[at : at + rows].astype(BF16), k).astype(F32)
    return out.astype(BF16)


def solution(mesh):
    in_specs = (
        P(("grp", "seq", "sub"), None),
        P(("grp", "seq", "sub")),
        P(("grp", "seq", "sub"), None),
        P("sub", None),
        P("sub", None),
        P("sub", None),
        P(),
    )
    out_specs = P(("grp", "seq", "sub"), None)
    return jax.shard_map(local, mesh=mesh, in_specs=in_specs, out_specs=out_specs, check_vma=False)
```

```python
import functools
import math

import jax
import jax.numpy as jnp
from jax import lax
from jax.experimental import pallas as pl
from jax.experimental.pallas import tpu as pltpu
from jax.sharding import PartitionSpec as P

F32 = jnp.float32
BF16 = jnp.bfloat16
HBM = pl.BlockSpec(memory_space=pltpu.HBM)


def dot(a, b, ca=1, cb=0):
    return lax.dot_general(a, b, (((ca,), (cb,)), ((), ())), preferred_element_type=F32)


def soft_and_sigmoid(u):
    e = jnp.exp(-jnp.abs(u))
    series = e * (1.0 + e * (-0.5 + e * (1.0 / 3.0)))
    soft = jnp.maximum(u, 0.0) + jnp.where(e < 1e-3, series, jnp.log(1.0 + e))
    r = 1.0 / (1.0 + e)
    return soft, jnp.where(u >= 0.0, r, e * r)


def call(body, outs, args, flops, vmem=24, **kw):
    nbytes = sum(a.size * a.dtype.itemsize for a in args)
    return pl.pallas_call(
        body,
        out_shape=[jax.ShapeDtypeStruct(s, d) for s, d in outs],
        compiler_params=pltpu.CompilerParams(vmem_limit_bytes=vmem * 2**20),
        cost_estimate=pl.CostEstimate(flops=flops, bytes_accessed=nbytes, transcendentals=0),
        **kw,
    )(*args)


def first_kernel(g, cols, split, *refs):
    wk, wv, wq, events, offsets, frequency, cot = refs[:7]
    n = 4 if split else 2
    pieces, bufs, sems = refs[7 : 7 + n], refs[7 + n : -1], refs[-1]
    mine = lax.axis_index("seq") % g
    at = pl.ds(pl.multiple_of(mine * cols, cols), cols)
    pairs = [(wk.at[:, at], pieces[0].at[:, :cols]), (wv.at[:, at], pieces[0].at[:, cols:]), (wq.at[:, at], pieces[1])]
    if split:
        half = wk.shape[0] // 2
        rows = pl.ds(pl.multiple_of(lax.axis_index("grp") * half, half), half)
        pairs += [
            (wk.at[rows, at], pieces[2].at[:, :cols]),
            (wv.at[rows, at], pieces[2].at[:, cols:]),
            (wq.at[rows, at], pieces[3]),
        ]
    copies = [pltpu.make_async_copy(a, b, sems.at[i]) for i, (a, b) in enumerate(pairs)]
    for c in copies:
        c.start()
    tokens, width = events.shape
    half = width // 2
    lanes = 128
    column = jnp.transpose(jnp.broadcast_to(offsets[...].astype(F32), (lanes, tokens)))
    for j in range(0, half, lanes):
        angle = column * frequency[:, j : j + lanes]
        for value, start in ((jnp.sin(angle), j), (jnp.cos(angle), half + j)):
            to = slice(start, start + lanes)
            x = (events[:, to].astype(F32) + value).astype(BF16)
            for buf in bufs:
                buf[:, to] = x
    for k, buf in enumerate(bufs):
        buf[:, width:] = cot[:, pl.ds(pl.multiple_of(((mine // 2) ^ k) * 2 * cols, 2 * cols), 2 * cols)]
    for c in copies:
        c.wait()


def place_rows(full, parts, n):
    z = lax.axis_index("sub")
    rows = parts[0].shape[0]
    spots = [(k, 0) for k in range(n)]
    if len(parts) > n:
        half, mine = rows // 2, lax.axis_index("grp")
        spots = [(0, 0), (1, 0)]
        for k in range(2, n):
            spots += [(k, mine * half), (k, half - mine * half)]
    for (k, start), part in zip(spots, parts):
        size = part.shape[0]
        full[pl.ds(pl.multiple_of((z ^ k) * rows + start, size), size), :] = part[...]


def features(act, om, h, i, feat, sig):
    hd, m = om.shape[1], om.shape[2]
    rows = act.shape[0]
    soft, s = soft_and_sigmoid(dot(act[:, h * hd : (h + 1) * hd], om[h]))
    soft = soft.astype(BF16)
    at = (slice(i * rows, (i + 1) * rows), slice(h * m, (h + 1) * m))
    feat[at] = soft
    sig[at] = s
    return soft


def put_total(own, send, base, extra, total):
    hd = own.shape[1]
    n = total.shape[1] // hd
    for j in range(n):
        piece = total[:, j * hd : (j + 1) * hd]
        high = piece.astype(BF16)
        own[base + j : base + j + 1, :] = piece
        send[base + j : base + j + 1, :] = high
        own[base + extra + j : base + extra + j + 1, :] = jnp.zeros_like(piece)
        send[base + extra + j : base + extra + j + 1, :] = (piece - high.astype(F32)).astype(BF16)


def get_total(tail, extra, h, m):
    hd = tail.shape[1]
    n = m // hd
    rows = [
        tail[h * n + j : h * n + j + 1, :] + tail[extra + h * n + j : extra + h * n + j + 1, :]
        for j in range(n)
    ]
    return jnp.concatenate(rows, axis=1)


def summed(parts, lo, hi):
    out = parts[0][lo:hi, :]
    for part in parts[1:]:
        out = out + part[lo:hi, :].astype(F32)
    return out


def key_value_kernel(g, n, nw, hp, width, *refs):
    xs, ws, om = refs[:g], refs[g : g + nw], refs[g + nw]
    w_full, feat, sig, val, own, send = refs[g + nw + 1 :]
    hd, m = om.shape[1], om.shape[2]
    cols = hp * hd
    place_rows(w_full, ws, n)
    rows = xs[0].shape[0]
    sums = [jnp.zeros((1, m), F32) for _ in range(hp)]
    for i, x in enumerate(xs):
        act = dot(x[:, :width], w_full[...]).astype(BF16)
        val[i * rows : (i + 1) * rows, :] = act[:, cols:]
        for h in range(hp):
            soft = features(act, om, h, i, feat, sig)
            sums[h] = sums[h] + jnp.sum(soft.astype(F32), axis=0, keepdims=True)
    base = hp * m
    own[base:, :] = jnp.zeros_like(own[base:, :])
    send[base:, :] = jnp.zeros_like(send[base:, :])
    for h in range(hp):
        s = dot(feat[:, h * m : (h + 1) * m], val[:, h * hd : (h + 1) * hd], 0, 0)
        own[h * m : (h + 1) * m, :] = s
        send[h * m : (h + 1) * m, :] = s.astype(BF16)
    put_total(own, send, base, hp * m // hd, jnp.concatenate(sums, axis=1))


def query_kernel(g, n, nw, hp, width, *refs):
    xs, ws, om = refs[:g], refs[g : g + nw], refs[g + nw]
    w_full, feat, sig = refs[g + nw + 1 :]
    place_rows(w_full, ws, n)
    for i, x in enumerate(xs):
        act = dot(x[:, :width], w_full[...]).astype(BF16)
        for h in range(hp):
            features(act, om, h, i, feat, sig)


def query_side_kernel(g, p, hp, m, width, loss_scale, *refs):
    parts, xs, feat = refs[:p], refs[p : p + g], refs[p + g]
    total_half, summary_half, scaled_half, norm, own, send = refs[p + g + 1 :]
    hd = summary_half.shape[1]
    cols = hp * hd
    base = hp * m
    extra = base // hd
    summary_half[...] = summed(parts, 0, base).astype(BF16)
    tail = summed(parts, base, parts[0].shape[0])
    core = lax.axis_index("seq") % 2
    rows = xs[0].shape[0]
    own[base:, :] = jnp.zeros_like(own[base:, :])
    send[base:, :] = jnp.zeros_like(send[base:, :])
    sums = []
    for h in range(hp):
        row = get_total(tail, extra, h, m).astype(BF16)
        total_half[:, h * m : (h + 1) * m] = row
        spread = jnp.broadcast_to(row.astype(F32), (hd, m)).astype(BF16)
        acc = jnp.zeros((1, m), F32)
        for i in range(g):
            tok = slice(i * rows, (i + 1) * rows)
            qf = feat[tok, h * m : (h + 1) * m]
            at = pl.multiple_of(width + core * cols + h * hd, hd)
            denom = dot(qf, spread, 1, 1)
            numer = dot(qf, summary_half[h * m : (h + 1) * m, :])
            scaled = xs[i][:, pl.ds(at, hd)].astype(F32) * loss_scale / denom
            scaled_half[tok, h * hd : (h + 1) * hd] = scaled.astype(BF16)
            ng = -jnp.sum(scaled * (numer / denom), axis=1, keepdims=True)
            norm[tok, h : h + 1] = ng
            acc = acc + jnp.sum(qf.astype(F32) * ng.astype(BF16).astype(F32), axis=0, keepdims=True)
        s = dot(feat[:, h * m : (h + 1) * m], scaled_half[:, h * hd : (h + 1) * hd], 0, 0)
        own[h * m : (h + 1) * m, :] = s
        send[h * m : (h + 1) * m, :] = s.astype(BF16)
        sums.append(acc)
    put_total(own, send, base, extra, jnp.concatenate(sums, axis=1))


def query_grad_kernel(hp, scaled_half, summary_half, norm, total_half, sig, om, out):
    hd, m = om.shape[1], om.shape[2]
    for h in range(hp):
        fg = dot(scaled_half[:, h * hd : (h + 1) * hd], summary_half[h * m : (h + 1) * m, :], 1, 1)
        fg = fg + norm[:, h : h + 1] * total_half[:, h * m : (h + 1) * m].astype(F32)
        pg = (fg * sig[:, h * m : (h + 1) * m]).astype(BF16)
        out[:, h * hd : (h + 1) * hd] = dot(pg, om[h], 1, 1).astype(BF16)


def products(g, start, qg, kvg, wq, wkv, out):
    rows = qg.shape[0] // g
    for i in range(start, g, 2):
        tok = slice(i * rows, (i + 1) * rows)
        o = dot(qg[tok, :], wq[...], 1, 1) + dot(kvg[tok, :], wkv[...], 1, 1)
        out[(i // 2) * rows : (i // 2 + 1) * rows, :] = o.astype(out.dtype)


def key_side_kernel(g, p, hp, *refs):
    parts = refs[:p]
    val, feat, sig, om, qg, wq, wkv = refs[p : p + 7]
    odd, kvg = refs[p + 7 :]
    hd, m = om.shape[1], om.shape[2]
    base = hp * m
    cols = hp * hd
    tail = summed(parts, base, parts[0].shape[0])
    for h in range(hp):
        gh = summed(parts, h * m, (h + 1) * m).astype(BF16)
        col = slice(h * hd, (h + 1) * hd)
        fg = dot(val[:, col], gh, 1, 1) + get_total(tail, base // hd, h, m)
        kvg[:, cols + h * hd : cols + (h + 1) * hd] = dot(feat[:, h * m : (h + 1) * m], gh).astype(BF16)
        pg = (fg * sig[:, h * m : (h + 1) * m]).astype(BF16)
        kvg[:, col] = dot(pg, om[h], 1, 1).astype(BF16)
    products(g, 1, qg, kvg, wq, wkv, odd)


def even_kernel(g, qg, kvg, wq, wkv, even):
    products(g, 0, qg, kvg, wq, wkv, even)


def local(events, offsets, cotangent, query_weight, key_weight, value_weight, omega):
    heads, hd, m = omega.shape
    n_seq, n_sub = lax.axis_size("seq"), lax.axis_size("sub")
    rows, width = events.shape
    loss_scale = math.sqrt(rows * n_seq * n_sub)
    g = math.gcd(heads, n_seq)
    r = n_seq // g
    hp = heads // g
    p = r * n_sub
    t = g * rows
    cols = hp * hd
    srows = hp * m + -(-2 * hp * m // hd // 16) * 16

    def over_seq(x, k):
        return lax.ppermute(x, "seq", [(i, i ^ k) for i in range(n_seq)])

    def over_sub(x, k):
        return lax.ppermute(x, "sub", [(i, i ^ k) for i in range(n_sub)])

    def to_all(own, send):
        parts = [own]
        for j in range(r):
            for k in range(n_sub):
                if j or k:
                    perm = [
                        (a * n_sub + b, (a ^ (j * g)) * n_sub + (b ^ k))
                        for a in range(n_seq)
                        for b in range(n_sub)
                    ]
                    parts.append(lax.ppermute(send, ("seq", "sub"), perm))
        return parts

    wrows = key_weight.shape[0]
    split = lax.axis_size("grp") == 2 and wrows % 32 == 0
    wouts = [((wrows, 2 * cols), BF16), ((wrows, cols), BF16), ((wrows // 2, 2 * cols), BF16), ((wrows // 2, cols), BF16)]
    wouts = wouts if split else wouts[:2]
    n = len(wouts)
    frequency = jnp.exp(jnp.arange(width // 2, dtype=F32) * (-2.0 * math.log(10000.0) / width))
    whole = pl.BlockSpec(memory_space=pltpu.VMEM)
    firsts = call(
        functools.partial(first_kernel, g, cols, split),
        wouts + [((rows, width + 2 * cols), BF16)] * (g // 2),
        [key_weight, value_weight, query_weight, events, offsets[None], frequency[None], cotangent],
        0,
        vmem=56,
        in_specs=[HBM] * 3 + [whole] * 4,
        out_specs=[HBM] * n + [whole] * (g // 2),
        scratch_shapes=[pltpu.SemaphoreType.DMA((6 if split else 3,))],
    )
    pieces, bufs = firsts[:n], firsts[n:]

    def from_sub(i):
        return [over_sub(pieces[i], 1)] + [over_sub(pieces[i + 2 if split else i], k) for k in range(2, n_sub)]

    def weight_rows(i, arrived):
        if not split:
            return [pieces[i]] + arrived
        far = []
        for part in arrived[1:]:
            far += [part, lax.ppermute(part, "grp", [(0, 1), (1, 0)])]
        return [pieces[i], arrived[0]] + far

    arrived = from_sub(0)
    kvs = weight_rows(0, arrived)
    xs = [bufs[0]] * g
    for k in range(2, g, 2):
        xs[k] = over_seq(bufs[k // 2], k)
    xs[1] = over_seq(bufs[0], 1)
    xs[2:], _ = lax.optimization_barrier((xs[2:], arrived))
    for k in range(3, g, 2):
        xs[k] = over_seq(xs[k ^ 1], 1)
    pieces, _ = lax.optimization_barrier((pieces, arrived + xs[1:2]))
    query_rows = from_sub(1)
    om = lax.dynamic_slice_in_dim(omega, (lax.axis_index("seq") % g) * hp, hp, 0)

    flop = 2 * t * width * cols
    summary_out = [((srows, hd), F32), ((srows, hd), BF16)]
    wkv_full, key_feat, key_sig, val, own, send = call(
        functools.partial(key_value_kernel, g, n_sub, len(kvs), hp, width),
        [((width, 2 * cols), BF16), ((t, hp * m), BF16), ((t, hp * m), F32), ((t, cols), BF16)] + summary_out,
        [*xs, *kvs, om],
        8 * flop,
    )
    summary = to_all(own, send)
    query_rows, _ = lax.optimization_barrier((query_rows, val))
    qs = weight_rows(1, query_rows)
    wq_full, query_feat, query_sig = call(
        functools.partial(query_kernel, g, n_sub, len(qs), hp, width),
        [((width, cols), BF16), ((t, hp * m), BF16), ((t, hp * m), F32)],
        [*xs, *qs, om],
        8 * flop,
    )
    total_half, summary_half, scaled_half, norm, own, send = call(
        functools.partial(query_side_kernel, g, p, hp, m, width, loss_scale),
        [((1, hp * m), BF16), ((hp * m, hd), BF16), ((t, cols), BF16), ((t, hp), F32)] + summary_out,
        [*summary, *xs, query_feat],
        8 * flop,
    )
    summary_grad = to_all(own, send)
    (query_grad,) = call(
        functools.partial(query_grad_kernel, hp),
        [((t, cols), BF16)],
        [scaled_half, summary_half, norm, total_half, query_sig, om],
        4 * flop,
    )
    odd, key_value_grad = call(
        functools.partial(key_side_kernel, g, p, hp),
        [((t // 2, width), BF16), ((t, 2 * cols), BF16)],
        [*summary_grad, val, key_feat, key_sig, om, query_grad, wq_full, wkv_full],
        8 * flop,
    )
    got = over_seq(odd, 1)
    (even,) = call(
        functools.partial(even_kernel, g),
        [((t // 2, width), F32)],
        [query_grad, key_value_grad, wq_full, wkv_full],
        8 * flop,
    )
    both = even + got.astype(F32)
    out = both[:rows]
    for k in range(2, g, 2):
        at = (k // 2) * rows
        out = out + over_seq(both[at : at + rows].astype(BF16), k).astype(F32)
    return out.astype(BF16)


def solution(mesh):
    in_specs = (
        P(("grp", "seq", "sub"), None),
        P(("grp", "seq", "sub")),
        P(("grp", "seq", "sub"), None),
        P("sub", None),
        P("sub", None),
        P("sub", None),
        P(),
    )
    out_specs = P(("grp", "seq", "sub"), None)
    return jax.shard_map(local, mesh=mesh, in_specs=in_specs, out_specs=out_specs, check_vma=False)
```

```python
import functools
import math

import jax
import jax.numpy as jnp
from jax import lax
from jax.experimental import pallas as pl
from jax.experimental.pallas import tpu as pltpu
from jax.sharding import PartitionSpec as P

F32 = jnp.float32
BF16 = jnp.bfloat16
HBM = pl.BlockSpec(memory_space=pltpu.HBM)


def dot(a, b, ca=1, cb=0):
    return lax.dot_general(a, b, (((ca,), (cb,)), ((), ())), preferred_element_type=F32)


def soft_and_sigmoid(u):
    e = jnp.exp(-jnp.abs(u))
    series = e * (1.0 + e * (-0.5 + e * (1.0 / 3.0)))
    soft = jnp.maximum(u, 0.0) + jnp.where(e < 1e-3, series, jnp.log(1.0 + e))
    r = 1.0 / (1.0 + e)
    return soft, jnp.where(u >= 0.0, r, e * r)


def call(body, outs, args, flops, vmem=24, **kw):
    nbytes = sum(a.size * a.dtype.itemsize for a in args) if flops else 0
    return pl.pallas_call(
        body,
        out_shape=[jax.ShapeDtypeStruct(s, d) for s, d in outs],
        compiler_params=pltpu.CompilerParams(vmem_limit_bytes=vmem * 2**20),
        cost_estimate=pl.CostEstimate(flops=flops, bytes_accessed=nbytes, transcendentals=0),
        **kw,
    )(*args)


def first_kernel(g, cols, *refs):
    ws, (events, offsets, frequency, cot) = refs[:3], refs[3:7]
    (near, far, far_query), bufs, sems = refs[7:10], refs[10:-1], refs[-1]
    mine = lax.axis_index("seq") % g
    at = pl.ds(pl.multiple_of(mine * cols, cols), cols)
    size = far.shape[0]
    rows = slice(None)
    if size < near.shape[0]:
        rows = pl.ds(pl.multiple_of(lax.axis_index("grp") * size, size), size)
    copies = []
    for i, w in enumerate(ws):
        to = slice(i * cols, (i + 1) * cols)
        copies.append((w.at[:, at], near.at[:, to]))
        copies.append((w.at[rows, at], far.at[:, to] if i < 2 else far_query))
    copies = [pltpu.make_async_copy(a, b, sems.at[i]) for i, (a, b) in enumerate(copies)]
    for c in copies:
        c.start()
    tokens, width = events.shape
    half = width // 2
    lanes = 128
    column = jnp.transpose(jnp.broadcast_to(offsets[...].astype(F32), (lanes, tokens)))
    for j in range(0, half, lanes):
        angle = column * frequency[:, j : j + lanes]
        for value, start in ((jnp.sin(angle), j), (jnp.cos(angle), half + j)):
            to = slice(start, start + lanes)
            x = (events[:, to].astype(F32) + value).astype(BF16)
            for buf in bufs:
                buf[:, to] = x
    for k, buf in enumerate(bufs):
        buf[:, width:] = cot[:, pl.ds(pl.multiple_of(((mine // 2) ^ k) * 2 * cols, 2 * cols), 2 * cols)]
    for c in copies:
        c.wait()


def place_rows(full, parts, n, start):
    z = lax.axis_index("sub")
    rows, cols = parts[0].shape[0], full.shape[1]
    full[pl.ds(pl.multiple_of(z * rows, rows), rows), :] = parts[0][:, start : start + cols]
    full[pl.ds(pl.multiple_of((z ^ 1) * rows, rows), rows), :] = parts[1][:, start : start + cols]
    far = parts[2:]
    halves = len(far) // (n - 2)
    size = rows // halves
    for i, part in enumerate(far):
        k = 2 + i // halves
        where = (z ^ k) * rows
        if halves == 2:
            mine = lax.axis_index("grp") * size
            where = where + (size - mine if i % 2 else mine)
        full[pl.ds(pl.multiple_of(where, size), size), :] = part[...]


def features(act, om, h, i, feat, sig):
    hd, m = om.shape[1], om.shape[2]
    rows = act.shape[0]
    soft, s = soft_and_sigmoid(dot(act[:, h * hd : (h + 1) * hd], om[h]))
    soft = soft.astype(BF16)
    at = (slice(i * rows, (i + 1) * rows), slice(h * m, (h + 1) * m))
    feat[at] = soft
    sig[at] = s
    return soft


def put_total(own, send, base, extra, total):
    hd = own.shape[1]
    n = total.shape[1] // hd
    for j in range(n):
        piece = total[:, j * hd : (j + 1) * hd]
        high = piece.astype(BF16)
        own[base + j : base + j + 1, :] = piece
        send[base + j : base + j + 1, :] = high
        own[base + extra + j : base + extra + j + 1, :] = jnp.zeros_like(piece)
        send[base + extra + j : base + extra + j + 1, :] = (piece - high.astype(F32)).astype(BF16)


def get_total(tail, extra, h, m):
    hd = tail.shape[1]
    n = m // hd
    rows = [
        tail[h * n + j : h * n + j + 1, :] + tail[extra + h * n + j : extra + h * n + j + 1, :]
        for j in range(n)
    ]
    return jnp.concatenate(rows, axis=1)


def summed(parts, lo, hi):
    out = parts[0][lo:hi, :]
    for part in parts[1:]:
        out = out + part[lo:hi, :].astype(F32)
    return out


def key_value_kernel(g, n, nw, hp, width, *refs):
    xs, ws, om = refs[:g], refs[g : g + nw], refs[g + nw]
    w_full, feat, sig, val, own, send = refs[g + nw + 1 :]
    hd, m = om.shape[1], om.shape[2]
    cols = hp * hd
    place_rows(w_full, ws, n, 0)
    rows = xs[0].shape[0]
    sums = [jnp.zeros((1, m), F32) for _ in range(hp)]
    for i, x in enumerate(xs):
        act = dot(x[:, :width], w_full[...]).astype(BF16)
        val[i * rows : (i + 1) * rows, :] = act[:, cols:]
        for h in range(hp):
            soft = features(act, om, h, i, feat, sig)
            sums[h] = sums[h] + jnp.sum(soft.astype(F32), axis=0, keepdims=True)
    base = hp * m
    own[base:, :] = jnp.zeros_like(own[base:, :])
    send[base:, :] = jnp.zeros_like(send[base:, :])
    for h in range(hp):
        s = dot(feat[:, h * m : (h + 1) * m], val[:, h * hd : (h + 1) * hd], 0, 0)
        own[h * m : (h + 1) * m, :] = s
        send[h * m : (h + 1) * m, :] = s.astype(BF16)
    put_total(own, send, base, hp * m // hd, jnp.concatenate(sums, axis=1))


def query_kernel(g, n, nw, hp, width, *refs):
    xs, ws, om = refs[:g], refs[g : g + nw], refs[g + nw]
    w_full, feat, sig = refs[g + nw + 1 :]
    place_rows(w_full, ws, n, 2 * w_full.shape[1])
    for i, x in enumerate(xs):
        act = dot(x[:, :width], w_full[...]).astype(BF16)
        for h in range(hp):
            features(act, om, h, i, feat, sig)


def query_side_kernel(g, p, hp, m, width, loss_scale, *refs):
    parts, xs, feat = refs[:p], refs[p : p + g], refs[p + g]
    total_half, summary_half, scaled_half, norm, own, send = refs[p + g + 1 :]
    hd = summary_half.shape[1]
    cols = hp * hd
    base = hp * m
    extra = base // hd
    summary_half[...] = summed(parts, 0, base).astype(BF16)
    tail = summed(parts, base, parts[0].shape[0])
    core = lax.axis_index("seq") % 2
    rows = xs[0].shape[0]
    own[base:, :] = jnp.zeros_like(own[base:, :])
    send[base:, :] = jnp.zeros_like(send[base:, :])
    sums = []
    for h in range(hp):
        row = get_total(tail, extra, h, m).astype(BF16)
        total_half[:, h * m : (h + 1) * m] = row
        spread = jnp.broadcast_to(row.astype(F32), (hd, m)).astype(BF16)
        acc = jnp.zeros((1, m), F32)
        for i in range(g):
            tok = slice(i * rows, (i + 1) * rows)
            qf = feat[tok, h * m : (h + 1) * m]
            at = pl.multiple_of(width + core * cols + h * hd, hd)
            denom = dot(qf, spread, 1, 1)
            numer = dot(qf, summary_half[h * m : (h + 1) * m, :])
            scaled = xs[i][:, pl.ds(at, hd)].astype(F32) * loss_scale / denom
            scaled_half[tok, h * hd : (h + 1) * hd] = scaled.astype(BF16)
            ng = -jnp.sum(scaled * (numer / denom), axis=1, keepdims=True)
            norm[tok, h : h + 1] = ng
            acc = acc + jnp.sum(qf.astype(F32) * ng.astype(BF16).astype(F32), axis=0, keepdims=True)
        s = dot(feat[:, h * m : (h + 1) * m], scaled_half[:, h * hd : (h + 1) * hd], 0, 0)
        own[h * m : (h + 1) * m, :] = s
        send[h * m : (h + 1) * m, :] = s.astype(BF16)
        sums.append(acc)
    put_total(own, send, base, extra, jnp.concatenate(sums, axis=1))


def query_grad_kernel(hp, scaled_half, summary_half, norm, total_half, sig, om, out):
    hd, m = om.shape[1], om.shape[2]
    for h in range(hp):
        fg = dot(scaled_half[:, h * hd : (h + 1) * hd], summary_half[h * m : (h + 1) * m, :], 1, 1)
        fg = fg + norm[:, h : h + 1] * total_half[:, h * m : (h + 1) * m].astype(F32)
        pg = (fg * sig[:, h * m : (h + 1) * m]).astype(BF16)
        out[:, h * hd : (h + 1) * hd] = dot(pg, om[h], 1, 1).astype(BF16)


def products(g, start, qg, kvg, wq, wkv, out):
    rows = qg.shape[0] // g
    for i in range(start, g, 2):
        tok = slice(i * rows, (i + 1) * rows)
        o = dot(qg[tok, :], wq[...], 1, 1) + dot(kvg[tok, :], wkv[...], 1, 1)
        out[(i // 2) * rows : (i // 2 + 1) * rows, :] = o.astype(out.dtype)


def key_side_kernel(g, p, hp, *refs):
    parts = refs[:p]
    val, feat, sig, om, qg, wq, wkv = refs[p : p + 7]
    odd, kvg = refs[p + 7 :]
    hd, m = om.shape[1], om.shape[2]
    base = hp * m
    cols = hp * hd
    tail = summed(parts, base, parts[0].shape[0])
    for h in range(hp):
        gh = summed(parts, h * m, (h + 1) * m).astype(BF16)
        col = slice(h * hd, (h + 1) * hd)
        fg = dot(val[:, col], gh, 1, 1) + get_total(tail, base // hd, h, m)
        kvg[:, cols + h * hd : cols + (h + 1) * hd] = dot(feat[:, h * m : (h + 1) * m], gh).astype(BF16)
        pg = (fg * sig[:, h * m : (h + 1) * m]).astype(BF16)
        kvg[:, col] = dot(pg, om[h], 1, 1).astype(BF16)
    products(g, 1, qg, kvg, wq, wkv, odd)


def even_kernel(g, qg, kvg, wq, wkv, even):
    products(g, 0, qg, kvg, wq, wkv, even)


def local(events, offsets, cotangent, query_weight, key_weight, value_weight, omega):
    heads, hd, m = omega.shape
    n_seq, n_sub = lax.axis_size("seq"), lax.axis_size("sub")
    rows, width = events.shape
    loss_scale = math.sqrt(rows * n_seq * n_sub)
    g = math.gcd(heads, n_seq)
    r = n_seq // g
    hp = heads // g
    p = r * n_sub
    t = g * rows
    cols = hp * hd
    srows = hp * m + -(-2 * hp * m // hd // 16) * 16

    def over_seq(x, k):
        return lax.ppermute(x, "seq", [(i, i ^ k) for i in range(n_seq)])

    def over_sub(x, k):
        return lax.ppermute(x, "sub", [(i, i ^ k) for i in range(n_sub)])

    def to_all(own, send):
        parts = [own]
        for j in range(r):
            for k in range(n_sub):
                if j or k:
                    perm = [
                        (a * n_sub + b, (a ^ (j * g)) * n_sub + (b ^ k))
                        for a in range(n_seq)
                        for b in range(n_sub)
                    ]
                    parts.append(lax.ppermute(send, ("seq", "sub"), perm))
        return parts

    wrows = key_weight.shape[0]
    split = lax.axis_size("grp") == 2 and wrows % 32 == 0
    size = wrows // 2 if split else wrows
    wouts = [((wrows, 3 * cols), BF16), ((size, 2 * cols), BF16), ((size, cols), BF16)]
    frequency = jnp.exp(jnp.arange(width // 2, dtype=F32) * (-2.0 * math.log(10000.0) / width))
    whole = pl.BlockSpec(memory_space=pltpu.VMEM)
    firsts = call(
        functools.partial(first_kernel, g, cols),
        wouts + [((rows, width + 2 * cols), BF16)] * (g // 2),
        [key_weight, value_weight, query_weight, events, offsets[None], frequency[None], cotangent],
        0,
        vmem=52,
        in_specs=[HBM] * 3 + [whole] * 4,
        scratch_shapes=[pltpu.SemaphoreType.DMA((6,))],
    )
    (near, far, far_query), bufs = firsts[:3], firsts[3:]

    def swapped(parts):
        if not split:
            return parts
        return [x for part in parts for x in (part, lax.ppermute(part, "grp", [(0, 1), (1, 0)]))]

    nearest = over_sub(near, 1)
    arrived = [over_sub(far, k) for k in range(2, n_sub)]
    kvs = [near, nearest] + swapped(arrived)
    xs = [bufs[0]] * g
    for k in range(2, g, 2):
        xs[k] = over_seq(bufs[k // 2], k)
    xs[1] = over_seq(bufs[0], 1)
    xs[2:], _ = lax.optimization_barrier((xs[2:], arrived))
    for k in range(3, g, 2):
        xs[k] = over_seq(xs[k ^ 1], 1)
    far_query, _ = lax.optimization_barrier((far_query, arrived + xs[1:2]))
    query_rows = [over_sub(far_query, k) for k in range(2, n_sub)]
    kvs, _ = lax.optimization_barrier((kvs, query_rows))
    om = lax.dynamic_slice_in_dim(omega, (lax.axis_index("seq") % g) * hp, hp, 0)

    flop = 2 * t * width * cols
    summary_out = [((srows, hd), F32), ((srows, hd), BF16)]
    wkv_full, key_feat, key_sig, val, own, send = call(
        functools.partial(key_value_kernel, g, n_sub, len(kvs), hp, width),
        [((width, 2 * cols), BF16), ((t, hp * m), BF16), ((t, hp * m), F32), ((t, cols), BF16)] + summary_out,
        [*xs, *kvs, om],
        8 * flop,
    )
    summary = to_all(own, send)
    query_rows, _ = lax.optimization_barrier((query_rows, val))
    qs = [near, nearest] + swapped(query_rows)
    wq_full, query_feat, query_sig = call(
        functools.partial(query_kernel, g, n_sub, len(qs), hp, width),
        [((width, cols), BF16), ((t, hp * m), BF16), ((t, hp * m), F32)],
        [*xs, *qs, om],
        0,
    )
    total_half, summary_half, scaled_half, norm, own, send = call(
        functools.partial(query_side_kernel, g, p, hp, m, width, loss_scale),
        [((1, hp * m), BF16), ((hp * m, hd), BF16), ((t, cols), BF16), ((t, hp), F32)] + summary_out,
        [*summary, *xs, query_feat],
        8 * flop,
    )
    summary_grad = to_all(own, send)
    (query_grad,) = call(
        functools.partial(query_grad_kernel, hp),
        [((t, cols), BF16)],
        [scaled_half, summary_half, norm, total_half, query_sig, om],
        4 * flop,
    )
    odd, key_value_grad = call(
        functools.partial(key_side_kernel, g, p, hp),
        [((t // 2, width), BF16), ((t, 2 * cols), BF16)],
        [*summary_grad, val, key_feat, key_sig, om, query_grad, wq_full, wkv_full],
        8 * flop,
    )
    got = over_seq(odd, 1)
    (even,) = call(
        functools.partial(even_kernel, g),
        [((t // 2, width), F32)],
        [query_grad, key_value_grad, wq_full, wkv_full],
        8 * flop,
    )
    both = even + got.astype(F32)
    out = both[:rows]
    for k in range(2, g, 2):
        at = (k // 2) * rows
        out = out + over_seq(both[at : at + rows].astype(BF16), k).astype(F32)
    return out.astype(BF16)


def solution(mesh):
    in_specs = (
        P(("grp", "seq", "sub"), None),
        P(("grp", "seq", "sub")),
        P(("grp", "seq", "sub"), None),
        P("sub", None),
        P("sub", None),
        P("sub", None),
        P(),
    )
    out_specs = P(("grp", "seq", "sub"), None)
    return jax.shard_map(local, mesh=mesh, in_specs=in_specs, out_specs=out_specs, check_vma=False)
```

```python
import functools
import math

import jax
import jax.numpy as jnp
from jax import lax
from jax.experimental import pallas as pl
from jax.experimental.pallas import tpu as pltpu
from jax.sharding import PartitionSpec as P

F32 = jnp.float32
BF16 = jnp.bfloat16
HBM = pl.BlockSpec(memory_space=pltpu.HBM)


def dot(a, b, ca=1, cb=0):
    return lax.dot_general(a, b, (((ca,), (cb,)), ((), ())), preferred_element_type=F32)


def soft_and_sigmoid(u):
    e = jnp.exp(-jnp.abs(u))
    series = e * (1.0 + e * (-0.5 + e * (1.0 / 3.0)))
    soft = jnp.maximum(u, 0.0) + jnp.where(e < 1e-3, series, jnp.log(1.0 + e))
    r = 1.0 / (1.0 + e)
    return soft, jnp.where(u >= 0.0, r, e * r)


def call(body, outs, args, flops, vmem=24, **kw):
    nbytes = sum(a.size * a.dtype.itemsize for a in args) if flops else 0
    return pl.pallas_call(
        body,
        out_shape=[jax.ShapeDtypeStruct(s, d) for s, d in outs],
        compiler_params=pltpu.CompilerParams(vmem_limit_bytes=int(vmem * 2**20)),
        cost_estimate=pl.CostEstimate(flops=flops, bytes_accessed=nbytes, transcendentals=0),
        **kw,
    )(*args)


def weight_kernel(g, cols, *refs):
    ws, (near, far, far_query), sems = refs[:3], refs[3:6], refs[6]
    mine = lax.axis_index("seq") % g
    at = pl.ds(pl.multiple_of(mine * cols, cols), cols)
    size = far.shape[0]
    rows = slice(None)
    if size < near.shape[0]:
        rows = pl.ds(pl.multiple_of(lax.axis_index("grp") * size, size), size)
    copies = []
    for i, w in enumerate(ws):
        to = slice(i * cols, (i + 1) * cols)
        copies.append((w.at[:, at], near.at[:, to]))
        copies.append((w.at[rows, at], far.at[:, to] if i < 2 else far_query))
    copies = [pltpu.make_async_copy(a, b, sems.at[i]) for i, (a, b) in enumerate(copies)]
    for c in copies:
        c.start()
    for c in copies:
        c.wait()


def input_kernel(g, cols, events, offsets, frequency, cot, *bufs):
    mine = (lax.axis_index("seq") % g) // 2
    tokens, width = events.shape
    half = width // 2
    lanes = 128
    column = jnp.transpose(jnp.broadcast_to(offsets[...].astype(F32), (lanes, tokens)))
    for j in range(0, half, lanes):
        angle = column * frequency[:, j : j + lanes]
        for value, start in ((jnp.sin(angle), j), (jnp.cos(angle), half + j)):
            to = slice(start, start + lanes)
            x = (events[:, to].astype(F32) + value).astype(BF16)
            for buf in bufs:
                buf[:, to] = x
    for k, buf in enumerate(bufs):
        buf[:, width:] = cot[:, pl.ds(pl.multiple_of((mine ^ k) * 2 * cols, 2 * cols), 2 * cols)]


def place_rows(full, parts, n, start):
    z = lax.axis_index("sub")
    rows, cols = parts[0].shape[0], full.shape[1]
    full[pl.ds(pl.multiple_of(z * rows, rows), rows), :] = parts[0][:, start : start + cols]
    full[pl.ds(pl.multiple_of((z ^ 1) * rows, rows), rows), :] = parts[1][:, start : start + cols]
    far = parts[2:]
    halves = len(far) // (n - 2)
    size = rows // halves
    for i, part in enumerate(far):
        k = 2 + i // halves
        where = (z ^ k) * rows
        if halves == 2:
            mine = lax.axis_index("grp") * size
            where = where + (size - mine if i % 2 else mine)
        full[pl.ds(pl.multiple_of(where, size), size), :] = part[...]


def features(act, om, h, i, feat, sig):
    hd, m = om.shape[1], om.shape[2]
    rows = act.shape[0]
    soft, s = soft_and_sigmoid(dot(act[:, h * hd : (h + 1) * hd], om[h]))
    soft = soft.astype(BF16)
    at = (slice(i * rows, (i + 1) * rows), slice(h * m, (h + 1) * m))
    feat[at] = soft
    sig[at] = s
    return soft


def put_total(own, send, base, extra, total):
    hd = own.shape[1]
    n = total.shape[1] // hd
    for j in range(n):
        piece = total[:, j * hd : (j + 1) * hd]
        high = piece.astype(BF16)
        own[base + j : base + j + 1, :] = piece
        send[base + j : base + j + 1, :] = high
        own[base + extra + j : base + extra + j + 1, :] = jnp.zeros_like(piece)
        send[base + extra + j : base + extra + j + 1, :] = (piece - high.astype(F32)).astype(BF16)


def get_total(tail, extra, h, m):
    hd = tail.shape[1]
    n = m // hd
    rows = [
        tail[h * n + j : h * n + j + 1, :] + tail[extra + h * n + j : extra + h * n + j + 1, :]
        for j in range(n)
    ]
    return jnp.concatenate(rows, axis=1)


def summed(parts, lo, hi):
    out = parts[0][lo:hi, :]
    for part in parts[1:]:
        out = out + part[lo:hi, :].astype(F32)
    return out


def key_value_kernel(g, n, nw, hp, width, *refs):
    xs, ws, om = refs[:g], refs[g : g + nw], refs[g + nw]
    w_full, feat, sig, val, own, send = refs[g + nw + 1 :]
    hd, m = om.shape[1], om.shape[2]
    cols = hp * hd
    place_rows(w_full, ws, n, 0)
    rows = xs[0].shape[0]
    sums = [jnp.zeros((1, m), F32) for _ in range(hp)]
    for i, x in enumerate(xs):
        act = dot(x[:, :width], w_full[...]).astype(BF16)
        val[i * rows : (i + 1) * rows, :] = act[:, cols:]
        for h in range(hp):
            soft = features(act, om, h, i, feat, sig)
            sums[h] = sums[h] + jnp.sum(soft.astype(F32), axis=0, keepdims=True)
    base = hp * m
    own[base:, :] = jnp.zeros_like(own[base:, :])
    send[base:, :] = jnp.zeros_like(send[base:, :])
    for h in range(hp):
        s = dot(feat[:, h * m : (h + 1) * m], val[:, h * hd : (h + 1) * hd], 0, 0)
        own[h * m : (h + 1) * m, :] = s
        send[h * m : (h + 1) * m, :] = s.astype(BF16)
    put_total(own, send, base, hp * m // hd, jnp.concatenate(sums, axis=1))


def query_kernel(g, n, nw, hp, width, *refs):
    xs, ws, om = refs[:g], refs[g : g + nw], refs[g + nw]
    w_full, feat, sig = refs[g + nw + 1 :]
    place_rows(w_full, ws, n, 2 * w_full.shape[1])
    for i, x in enumerate(xs):
        act = dot(x[:, :width], w_full[...]).astype(BF16)
        for h in range(hp):
            features(act, om, h, i, feat, sig)


def query_side_kernel(g, p, hp, m, width, loss_scale, *refs):
    parts, xs, feat = refs[:p], refs[p : p + g], refs[p + g]
    total_half, summary_half, scaled_half, norm, own, send = refs[p + g + 1 :]
    hd = summary_half.shape[1]
    cols = hp * hd
    base = hp * m
    extra = base // hd
    summary_half[...] = summed(parts, 0, base).astype(BF16)
    tail = summed(parts, base, parts[0].shape[0])
    core = lax.axis_index("seq") % 2
    rows = xs[0].shape[0]
    own[base:, :] = jnp.zeros_like(own[base:, :])
    send[base:, :] = jnp.zeros_like(send[base:, :])
    sums = []
    for h in range(hp):
        row = get_total(tail, extra, h, m).astype(BF16)
        total_half[:, h * m : (h + 1) * m] = row
        spread = jnp.broadcast_to(row.astype(F32), (hd, m)).astype(BF16)
        acc = jnp.zeros((1, m), F32)
        for i in range(g):
            tok = slice(i * rows, (i + 1) * rows)
            qf = feat[tok, h * m : (h + 1) * m]
            at = pl.multiple_of(width + core * cols + h * hd, hd)
            denom = dot(qf, spread, 1, 1)
            numer = dot(qf, summary_half[h * m : (h + 1) * m, :])
            scaled = xs[i][:, pl.ds(at, hd)].astype(F32) * loss_scale / denom
            scaled_half[tok, h * hd : (h + 1) * hd] = scaled.astype(BF16)
            ng = -jnp.sum(scaled * (numer / denom), axis=1, keepdims=True)
            norm[tok, h : h + 1] = ng
            acc = acc + jnp.sum(qf.astype(F32) * ng.astype(BF16).astype(F32), axis=0, keepdims=True)
        s = dot(feat[:, h * m : (h + 1) * m], scaled_half[:, h * hd : (h + 1) * hd], 0, 0)
        own[h * m : (h + 1) * m, :] = s
        send[h * m : (h + 1) * m, :] = s.astype(BF16)
        sums.append(acc)
    put_total(own, send, base, extra, jnp.concatenate(sums, axis=1))


def query_grad_kernel(hp, scaled_half, summary_half, norm, total_half, sig, om, out):
    hd, m = om.shape[1], om.shape[2]
    for h in range(hp):
        fg = dot(scaled_half[:, h * hd : (h + 1) * hd], summary_half[h * m : (h + 1) * m, :], 1, 1)
        fg = fg + norm[:, h : h + 1] * total_half[:, h * m : (h + 1) * m].astype(F32)
        pg = (fg * sig[:, h * m : (h + 1) * m]).astype(BF16)
        out[:, h * hd : (h + 1) * hd] = dot(pg, om[h], 1, 1).astype(BF16)


def products(g, blocks, qg, kvg, wq, wkv, out):
    rows = qg.shape[0] // g
    for j, i in enumerate(blocks):
        tok = slice(i * rows, (i + 1) * rows)
        o = dot(qg[tok, :], wq[...], 1, 1) + dot(kvg[tok, :], wkv[...], 1, 1)
        out[j * rows : (j + 1) * rows, :] = o.astype(out.dtype)


def key_side_kernel(g, p, hp, *refs):
    parts = refs[:p]
    val, feat, sig, om, qg, wq, wkv = refs[p : p + 7]
    odd, one, kvg = refs[p + 7 :]
    hd, m = om.shape[1], om.shape[2]
    base = hp * m
    cols = hp * hd
    tail = summed(parts, base, parts[0].shape[0])
    for h in range(hp):
        gh = summed(parts, h * m, (h + 1) * m).astype(BF16)
        col = slice(h * hd, (h + 1) * hd)
        fg = dot(val[:, col], gh, 1, 1) + get_total(tail, base // hd, h, m)
        kvg[:, cols + h * hd : cols + (h + 1) * hd] = dot(feat[:, h * m : (h + 1) * m], gh).astype(BF16)
        pg = (fg * sig[:, h * m : (h + 1) * m]).astype(BF16)
        kvg[:, col] = dot(pg, om[h], 1, 1).astype(BF16)
    products(g, range(3, g, 2), qg, kvg, wq, wkv, odd)
    products(g, [1], qg, kvg, wq, wkv, one)


def even_kernel(g, blocks, qg, kvg, wq, wkv, even):
    products(g, blocks, qg, kvg, wq, wkv, even)


def local(events, offsets, cotangent, query_weight, key_weight, value_weight, omega):
    heads, hd, m = omega.shape
    n_seq, n_sub = lax.axis_size("seq"), lax.axis_size("sub")
    rows, width = events.shape
    loss_scale = math.sqrt(rows * n_seq * n_sub)
    g = math.gcd(heads, n_seq)
    r = n_seq // g
    hp = heads // g
    p = r * n_sub
    t = g * rows
    cols = hp * hd
    srows = hp * m + -(-2 * hp * m // hd // 16) * 16

    def over_seq(x, k):
        return lax.ppermute(x, "seq", [(i, i ^ k) for i in range(n_seq)])

    def over_sub(x, k):
        return lax.ppermute(x, "sub", [(i, i ^ k) for i in range(n_sub)])

    def to_all(own, send):
        parts = [own]
        for j in range(r):
            for k in range(n_sub):
                if j or k:
                    perm = [
                        (a * n_sub + b, (a ^ (j * g)) * n_sub + (b ^ k))
                        for a in range(n_seq)
                        for b in range(n_sub)
                    ]
                    parts.append(lax.ppermute(send, ("seq", "sub"), perm))
        return parts

    wrows = key_weight.shape[0]
    split = lax.axis_size("grp") == 2 and wrows % 32 == 0
    size = wrows // 2 if split else wrows
    wouts = [((wrows, 3 * cols), BF16), ((size, 2 * cols), BF16), ((size, cols), BF16)]
    frequency = jnp.exp(jnp.arange(width // 2, dtype=F32) * (-2.0 * math.log(10000.0) / width))
    near, far, far_query = call(
        functools.partial(weight_kernel, g, cols),
        wouts,
        [key_weight, value_weight, query_weight],
        0,
        vmem=53,
        in_specs=[HBM] * 3,
        scratch_shapes=[pltpu.SemaphoreType.DMA((6,))],
    )
    offsets, _ = lax.optimization_barrier((offsets, near))
    bufs = call(
        functools.partial(input_kernel, g, cols),
        [((rows, width + 2 * cols), BF16)] * (g // 2),
        [events, offsets[None], frequency[None], cotangent],
        0,
    )

    def swapped(parts):
        if not split:
            return parts
        return [x for part in parts for x in (part, lax.ppermute(part, "grp", [(0, 1), (1, 0)]))]

    nearest = over_sub(near, 1)
    arrived = [over_sub(far, k) for k in range(2, n_sub)]
    kvs = [near, nearest] + swapped(arrived)
    xs = [bufs[0]] * g
    for k in range(2, g, 2):
        xs[k] = over_seq(bufs[k // 2], k)
    xs[1] = over_seq(bufs[0], 1)
    xs[2:], _ = lax.optimization_barrier((xs[2:], arrived))
    for k in range(3, g, 2):
        xs[k] = over_seq(xs[k ^ 1], 1)
    far_query, _ = lax.optimization_barrier((far_query, arrived + xs[1:2]))
    query_rows = [over_sub(far_query, k) for k in range(2, n_sub)]
    kvs, _ = lax.optimization_barrier((kvs, query_rows))
    om = lax.dynamic_slice_in_dim(omega, (lax.axis_index("seq") % g) * hp, hp, 0)

    flop = 2 * t * width * cols
    summary_out = [((srows, hd), F32), ((srows, hd), BF16)]
    wkv_full, key_feat, key_sig, val, own, send = call(
        functools.partial(key_value_kernel, g, n_sub, len(kvs), hp, width),
        [((width, 2 * cols), BF16), ((t, hp * m), BF16), ((t, hp * m), F32), ((t, cols), BF16)] + summary_out,
        [*xs, *kvs, om],
        8 * flop,
    )
    summary = to_all(own, send)
    query_rows, _ = lax.optimization_barrier((query_rows, val))
    qs = [near, nearest] + swapped(query_rows)
    wq_full, query_feat, query_sig = call(
        functools.partial(query_kernel, g, n_sub, len(qs), hp, width),
        [((width, cols), BF16), ((t, hp * m), BF16), ((t, hp * m), F32)],
        [*xs, *qs, om],
        0,
    )
    total_half, summary_half, scaled_half, norm, own, send = call(
        functools.partial(query_side_kernel, g, p, hp, m, width, loss_scale),
        [((1, hp * m), BF16), ((hp * m, hd), BF16), ((t, cols), BF16), ((t, hp), F32)] + summary_out,
        [*summary, *xs, query_feat],
        8 * flop,
    )
    summary_grad = to_all(own, send)
    (query_grad,) = call(
        functools.partial(query_grad_kernel, hp),
        [((t, cols), BF16)],
        [scaled_half, summary_half, norm, total_half, query_sig, om],
        4 * flop,
    )
    others = g // 2 - 1
    odd, one, key_value_grad = call(
        functools.partial(key_side_kernel, g, p, hp),
        [((others * rows, width), BF16), ((rows, width), BF16), ((t, 2 * cols), BF16)],
        [*summary_grad, val, key_feat, key_sig, om, query_grad, wq_full, wkv_full],
        8 * flop,
    )
    got = over_seq(odd, 1)
    got_one = over_seq(one, 1)

    def even_blocks(blocks):
        return call(
            functools.partial(even_kernel, g, blocks),
            [((len(blocks) * rows, width), F32)],
            [query_grad, key_value_grad, wq_full, wkv_full],
            8 * flop,
        )[0]

    both = (even_blocks(range(2, g, 2)) + got.astype(F32)).astype(BF16)
    out = even_blocks([0]) + got_one.astype(F32)
    for k in range(2, g, 2):
        at = (k // 2 - 1) * rows
        out = out + over_seq(both[at : at + rows], k).astype(F32)
    return out.astype(BF16)


def solution(mesh):
    in_specs = (
        P(("grp", "seq", "sub"), None),
        P(("grp", "seq", "sub")),
        P(("grp", "seq", "sub"), None),
        P("sub", None),
        P("sub", None),
        P("sub", None),
        P(),
    )
    out_specs = P(("grp", "seq", "sub"), None)
    return jax.shard_map(local, mesh=mesh, in_specs=in_specs, out_specs=out_specs, check_vma=False)
```

```python
import functools
import math

import jax
import jax.numpy as jnp
from jax import lax
from jax.experimental import pallas as pl
from jax.experimental.pallas import tpu as pltpu
from jax.sharding import PartitionSpec as P

F32 = jnp.float32
BF16 = jnp.bfloat16
HBM = pl.BlockSpec(memory_space=pltpu.HBM)


def dot(a, b, ca=1, cb=0):
    return lax.dot_general(a, b, (((ca,), (cb,)), ((), ())), preferred_element_type=F32)


def soft_and_sigmoid(u):
    e = jnp.exp(-jnp.abs(u))
    series = e * (1.0 + e * (-0.5 + e * (1.0 / 3.0)))
    soft = jnp.maximum(u, 0.0) + jnp.where(e < 1e-3, series, jnp.log(1.0 + e))
    r = 1.0 / (1.0 + e)
    return soft, jnp.where(u >= 0.0, r, e * r)


def call(body, outs, args, flops, vmem=24, **kw):
    nbytes = sum(a.size * a.dtype.itemsize for a in args) if flops else 0
    return pl.pallas_call(
        body,
        out_shape=[jax.ShapeDtypeStruct(s, d) for s, d in outs],
        compiler_params=pltpu.CompilerParams(vmem_limit_bytes=int(vmem * 2**20)),
        cost_estimate=pl.CostEstimate(flops=flops, bytes_accessed=nbytes, transcendentals=0),
        **kw,
    )(*args)


def weight_kernel(g, cols, *refs):
    ws, (near, far, far_query), sems = refs[:3], refs[3:6], refs[6]
    mine = lax.axis_index("seq") % g
    at = pl.ds(pl.multiple_of(mine * cols, cols), cols)
    size = far.shape[0]
    rows = slice(None)
    if size < near.shape[0]:
        rows = pl.ds(pl.multiple_of(lax.axis_index("grp") * size, size), size)
    copies = []
    for i, w in enumerate(ws):
        to = slice(i * cols, (i + 1) * cols)
        copies.append((w.at[:, at], near.at[:, to]))
        copies.append((w.at[rows, at], far.at[:, to] if i < 2 else far_query))
    copies = [pltpu.make_async_copy(a, b, sems.at[i]) for i, (a, b) in enumerate(copies)]
    for c in copies:
        c.start()
    for c in copies:
        c.wait()


def input_kernel(g, cols, events, offsets, frequency, cot, *bufs):
    mine = (lax.axis_index("seq") % g) // 2
    tokens, width = events.shape
    half = width // 2
    lanes = 128
    column = jnp.transpose(jnp.broadcast_to(offsets[...].astype(F32), (lanes, tokens)))
    for j in range(0, half, lanes):
        angle = column * frequency[:, j : j + lanes]
        for value, start in ((jnp.sin(angle), j), (jnp.cos(angle), half + j)):
            to = slice(start, start + lanes)
            x = (events[:, to].astype(F32) + value).astype(BF16)
            for buf in bufs:
                buf[:, to] = x
    for k, buf in enumerate(bufs):
        buf[:, width:] = cot[:, pl.ds(pl.multiple_of((mine ^ k) * 2 * cols, 2 * cols), 2 * cols)]


def place_rows(full, parts, n, start):
    z = lax.axis_index("sub")
    rows, cols = parts[0].shape[0], full.shape[1]
    full[pl.ds(pl.multiple_of(z * rows, rows), rows), :] = parts[0][:, start : start + cols]
    full[pl.ds(pl.multiple_of((z ^ 1) * rows, rows), rows), :] = parts[1][:, start : start + cols]
    far = parts[2:]
    halves = len(far) // (n - 2)
    size = rows // halves
    for i, part in enumerate(far):
        k = 2 + i // halves
        where = (z ^ k) * rows
        if halves == 2:
            mine = lax.axis_index("grp") * size
            where = where + (size - mine if i % 2 else mine)
        full[pl.ds(pl.multiple_of(where, size), size), :] = part[...]


def features(act, om, h, i, feat, sig):
    hd, m = om.shape[1], om.shape[2]
    rows = act.shape[0]
    soft, s = soft_and_sigmoid(dot(act[:, h * hd : (h + 1) * hd], om[h]))
    soft = soft.astype(BF16)
    at = (slice(i * rows, (i + 1) * rows), slice(h * m, (h + 1) * m))
    feat[at] = soft
    sig[at] = s
    return soft


def put_total(own, send, base, extra, total):
    hd = own.shape[1]
    n = total.shape[1] // hd
    for j in range(n):
        piece = total[:, j * hd : (j + 1) * hd]
        high = piece.astype(BF16)
        own[base + j : base + j + 1, :] = piece
        send[base + j : base + j + 1, :] = high
        own[base + extra + j : base + extra + j + 1, :] = jnp.zeros_like(piece)
        send[base + extra + j : base + extra + j + 1, :] = (piece - high.astype(F32)).astype(BF16)


def get_total(tail, extra, h, m):
    hd = tail.shape[1]
    n = m // hd
    rows = [
        tail[h * n + j : h * n + j + 1, :] + tail[extra + h * n + j : extra + h * n + j + 1, :]
        for j in range(n)
    ]
    return jnp.concatenate(rows, axis=1)


def summed(parts, lo, hi):
    out = parts[0][lo:hi, :]
    for part in parts[1:]:
        out = out + part[lo:hi, :].astype(F32)
    return out


def key_value_kernel(g, n, nw, hp, width, *refs):
    xs, ws, om = refs[:g], refs[g : g + nw], refs[g + nw]
    w_full, feat, sig, val, total = refs[g + nw + 1 :]
    hd, m = om.shape[1], om.shape[2]
    cols = hp * hd
    place_rows(w_full, ws, n, 0)
    rows = xs[0].shape[0]
    sums = [jnp.zeros((1, m), F32) for _ in range(hp)]
    for i, x in enumerate(xs):
        act = dot(x[:, :width], w_full[...]).astype(BF16)
        val[i * rows : (i + 1) * rows, :] = act[:, cols:]
        for h in range(hp):
            soft = features(act, om, h, i, feat, sig)
            sums[h] = sums[h] + jnp.sum(soft.astype(F32), axis=0, keepdims=True)
    total[...] = jnp.concatenate(sums, axis=1)


def summary_kernel(hp, feat, val, total, own, send):
    m, hd = feat.shape[1] // hp, val.shape[1] // hp
    base = hp * m
    own[base:, :] = jnp.zeros_like(own[base:, :])
    send[base:, :] = jnp.zeros_like(send[base:, :])
    for h in range(hp):
        s = dot(feat[:, h * m : (h + 1) * m], val[:, h * hd : (h + 1) * hd], 0, 0)
        own[h * m : (h + 1) * m, :] = s
        send[h * m : (h + 1) * m, :] = s.astype(BF16)
    put_total(own, send, base, hp * m // hd, total[...])


def query_kernel(g, n, nw, hp, width, *refs):
    xs, ws, om = refs[:g], refs[g : g + nw], refs[g + nw]
    w_full, feat, sig = refs[g + nw + 1 :]
    place_rows(w_full, ws, n, 2 * w_full.shape[1])
    for i, x in enumerate(xs):
        act = dot(x[:, :width], w_full[...]).astype(BF16)
        for h in range(hp):
            features(act, om, h, i, feat, sig)


def query_side_kernel(g, p, hp, m, width, loss_scale, *refs):
    parts, xs, feat = refs[:p], refs[p : p + g], refs[p + g]
    total_half, summary_half, scaled_half, norm, own, send = refs[p + g + 1 :]
    hd = summary_half.shape[1]
    cols = hp * hd
    base = hp * m
    extra = base // hd
    summary_half[...] = summed(parts, 0, base).astype(BF16)
    tail = summed(parts, base, parts[0].shape[0])
    core = lax.axis_index("seq") % 2
    rows = xs[0].shape[0]
    own[base:, :] = jnp.zeros_like(own[base:, :])
    send[base:, :] = jnp.zeros_like(send[base:, :])
    sums = []
    for h in range(hp):
        row = get_total(tail, extra, h, m).astype(BF16)
        total_half[:, h * m : (h + 1) * m] = row
        spread = jnp.broadcast_to(row.astype(F32), (hd, m)).astype(BF16)
        acc = jnp.zeros((1, m), F32)
        for i in range(g):
            tok = slice(i * rows, (i + 1) * rows)
            qf = feat[tok, h * m : (h + 1) * m]
            at = pl.multiple_of(width + core * cols + h * hd, hd)
            denom = dot(qf, spread, 1, 1)
            numer = dot(qf, summary_half[h * m : (h + 1) * m, :])
            scaled = xs[i][:, pl.ds(at, hd)].astype(F32) * loss_scale / denom
            scaled_half[tok, h * hd : (h + 1) * hd] = scaled.astype(BF16)
            ng = -jnp.sum(scaled * (numer / denom), axis=1, keepdims=True)
            norm[tok, h : h + 1] = ng
            acc = acc + jnp.sum(qf.astype(F32) * ng.astype(BF16).astype(F32), axis=0, keepdims=True)
        s = dot(feat[:, h * m : (h + 1) * m], scaled_half[:, h * hd : (h + 1) * hd], 0, 0)
        own[h * m : (h + 1) * m, :] = s
        send[h * m : (h + 1) * m, :] = s.astype(BF16)
        sums.append(acc)
    put_total(own, send, base, extra, jnp.concatenate(sums, axis=1))


def query_grad_kernel(hp, scaled_half, summary_half, norm, total_half, sig, om, out):
    hd, m = om.shape[1], om.shape[2]
    for h in range(hp):
        fg = dot(scaled_half[:, h * hd : (h + 1) * hd], summary_half[h * m : (h + 1) * m, :], 1, 1)
        fg = fg + norm[:, h : h + 1] * total_half[:, h * m : (h + 1) * m].astype(F32)
        pg = (fg * sig[:, h * m : (h + 1) * m]).astype(BF16)
        out[:, h * hd : (h + 1) * hd] = dot(pg, om[h], 1, 1).astype(BF16)


def products(g, blocks, qg, kvg, wq, wkv, out):
    rows = qg.shape[0] // g
    for j, i in enumerate(blocks):
        tok = slice(i * rows, (i + 1) * rows)
        o = dot(qg[tok, :], wq[...], 1, 1) + dot(kvg[tok, :], wkv[...], 1, 1)
        out[j * rows : (j + 1) * rows, :] = o.astype(out.dtype)


def key_side_kernel(g, p, hp, *refs):
    parts = refs[:p]
    val, feat, sig, om, qg, wq, wkv = refs[p : p + 7]
    odd, one, kvg = refs[p + 7 :]
    hd, m = om.shape[1], om.shape[2]
    base = hp * m
    cols = hp * hd
    tail = summed(parts, base, parts[0].shape[0])
    for h in range(hp):
        gh = summed(parts, h * m, (h + 1) * m).astype(BF16)
        col = slice(h * hd, (h + 1) * hd)
        fg = dot(val[:, col], gh, 1, 1) + get_total(tail, base // hd, h, m)
        kvg[:, cols + h * hd : cols + (h + 1) * hd] = dot(feat[:, h * m : (h + 1) * m], gh).astype(BF16)
        pg = (fg * sig[:, h * m : (h + 1) * m]).astype(BF16)
        kvg[:, col] = dot(pg, om[h], 1, 1).astype(BF16)
    products(g, range(3, g, 2), qg, kvg, wq, wkv, odd)
    products(g, [1], qg, kvg, wq, wkv, one)


def even_kernel(g, blocks, qg, kvg, wq, wkv, even):
    products(g, blocks, qg, kvg, wq, wkv, even)


def local(events, offsets, cotangent, query_weight, key_weight, value_weight, omega):
    heads, hd, m = omega.shape
    n_seq, n_sub = lax.axis_size("seq"), lax.axis_size("sub")
    rows, width = events.shape
    loss_scale = math.sqrt(rows * n_seq * n_sub)
    g = math.gcd(heads, n_seq)
    r = n_seq // g
    hp = heads // g
    p = r * n_sub
    t = g * rows
    cols = hp * hd
    srows = hp * m + -(-2 * hp * m // hd // 16) * 16

    def over_seq(x, k):
        return lax.ppermute(x, "seq", [(i, i ^ k) for i in range(n_seq)])

    def over_sub(x, k):
        return lax.ppermute(x, "sub", [(i, i ^ k) for i in range(n_sub)])

    def to_all(own, send):
        parts = [own]
        for j in range(r):
            for k in range(n_sub):
                if j or k:
                    perm = [
                        (a * n_sub + b, (a ^ (j * g)) * n_sub + (b ^ k))
                        for a in range(n_seq)
                        for b in range(n_sub)
                    ]
                    parts.append(lax.ppermute(send, ("seq", "sub"), perm))
        return parts

    wrows = key_weight.shape[0]
    split = lax.axis_size("grp") == 2 and wrows % 32 == 0
    size = wrows // 2 if split else wrows
    wouts = [((wrows, 3 * cols), BF16), ((size, 2 * cols), BF16), ((size, cols), BF16)]
    frequency = jnp.exp(jnp.arange(width // 2, dtype=F32) * (-2.0 * math.log(10000.0) / width))
    near, far, far_query = call(
        functools.partial(weight_kernel, g, cols),
        wouts,
        [key_weight, value_weight, query_weight],
        0,
        vmem=53,
        in_specs=[HBM] * 3,
        scratch_shapes=[pltpu.SemaphoreType.DMA((6,))],
    )
    offsets, _ = lax.optimization_barrier((offsets, near))
    bufs = call(
        functools.partial(input_kernel, g, cols),
        [((rows, width + 2 * cols), BF16)] * (g // 2),
        [events, offsets[None], frequency[None], cotangent],
        0,
    )

    def swapped(parts):
        if not split:
            return parts
        return [x for part in parts for x in (part, lax.ppermute(part, "grp", [(0, 1), (1, 0)]))]

    nearest = over_sub(near, 1)
    arrived = [over_sub(far, k) for k in range(2, n_sub)]
    kvs = [near, nearest] + swapped(arrived)
    xs = [bufs[0]] * g
    for k in range(2, g, 2):
        xs[k] = over_seq(bufs[k // 2], k)
    xs[1] = over_seq(bufs[0], 1)
    xs[2:], _ = lax.optimization_barrier((xs[2:], arrived))
    for k in range(3, g, 2):
        xs[k] = over_seq(xs[k ^ 1], 1)
    far_query, _ = lax.optimization_barrier((far_query, arrived + xs[1:2]))
    query_rows = [over_sub(far_query, k) for k in range(2, n_sub)]
    om = lax.dynamic_slice_in_dim(omega, (lax.axis_index("seq") % g) * hp, hp, 0)

    flop = 2 * t * width * cols
    summary_out = [((srows, hd), F32), ((srows, hd), BF16)]
    wkv_full, key_feat, key_sig, val, total = call(
        functools.partial(key_value_kernel, g, n_sub, len(kvs), hp, width),
        [((width, 2 * cols), BF16), ((t, hp * m), BF16), ((t, hp * m), F32), ((t, cols), BF16), ((1, hp * m), F32)],
        [*xs, *kvs, om],
        8 * flop,
    )
    total, _ = lax.optimization_barrier((total, query_rows))
    own, send = call(functools.partial(summary_kernel, hp), summary_out, [key_feat, val, total], 0)
    summary = to_all(own, send)
    query_rows, _ = lax.optimization_barrier((query_rows, val))
    qs = [near, nearest] + swapped(query_rows)
    wq_full, query_feat, query_sig = call(
        functools.partial(query_kernel, g, n_sub, len(qs), hp, width),
        [((width, cols), BF16), ((t, hp * m), BF16), ((t, hp * m), F32)],
        [*xs, *qs, om],
        0,
    )
    total_half, summary_half, scaled_half, norm, own, send = call(
        functools.partial(query_side_kernel, g, p, hp, m, width, loss_scale),
        [((1, hp * m), BF16), ((hp * m, hd), BF16), ((t, cols), BF16), ((t, hp), F32)] + summary_out,
        [*summary, *xs, query_feat],
        8 * flop,
    )
    summary_grad = to_all(own, send)
    (query_grad,) = call(
        functools.partial(query_grad_kernel, hp),
        [((t, cols), BF16)],
        [scaled_half, summary_half, norm, total_half, query_sig, om],
        4 * flop,
    )
    others = g // 2 - 1
    odd, one, key_value_grad = call(
        functools.partial(key_side_kernel, g, p, hp),
        [((others * rows, width), BF16), ((rows, width), BF16), ((t, 2 * cols), BF16)],
        [*summary_grad, val, key_feat, key_sig, om, query_grad, wq_full, wkv_full],
        8 * flop,
    )
    got = over_seq(odd, 1)
    got_one = over_seq(one, 1)

    def even_blocks(blocks):
        return call(
            functools.partial(even_kernel, g, blocks),
            [((len(blocks) * rows, width), F32)],
            [query_grad, key_value_grad, wq_full, wkv_full],
            8 * flop,
        )[0]

    both = (even_blocks(range(2, g, 2)) + got.astype(F32)).astype(BF16)
    out = even_blocks([0]) + got_one.astype(F32)
    for k in range(2, g, 2):
        at = (k // 2 - 1) * rows
        out = out + over_seq(both[at : at + rows], k).astype(F32)
    return out.astype(BF16)


def solution(mesh):
    in_specs = (
        P(("grp", "seq", "sub"), None),
        P(("grp", "seq", "sub")),
        P(("grp", "seq", "sub"), None),
        P("sub", None),
        P("sub", None),
        P("sub", None),
        P(),
    )
    out_specs = P(("grp", "seq", "sub"), None)
    return jax.shard_map(local, mesh=mesh, in_specs=in_specs, out_specs=out_specs, check_vma=False)
```

```python
import functools
import math

import jax
import jax.numpy as jnp
from jax import lax
from jax.experimental import pallas as pl
from jax.experimental.pallas import tpu as pltpu
from jax.sharding import PartitionSpec as P

F32 = jnp.float32
BF16 = jnp.bfloat16
HBM = pl.BlockSpec(memory_space=pltpu.HBM)


def dot(a, b, ca=1, cb=0):
    return lax.dot_general(a, b, (((ca,), (cb,)), ((), ())), preferred_element_type=F32)


def soft_and_sigmoid(u):
    e = jnp.exp(-jnp.abs(u))
    series = e * (1.0 + e * (-0.5 + e * (1.0 / 3.0)))
    soft = jnp.maximum(u, 0.0) + jnp.where(e < 1e-3, series, jnp.log(1.0 + e))
    r = 1.0 / (1.0 + e)
    return soft, jnp.where(u >= 0.0, r, e * r)


def call(body, outs, args, flops, vmem=24, **kw):
    nbytes = sum(a.size * a.dtype.itemsize for a in args) if flops else 0
    return pl.pallas_call(
        body,
        out_shape=[jax.ShapeDtypeStruct(s, d) for s, d in outs],
        compiler_params=pltpu.CompilerParams(vmem_limit_bytes=int(vmem * 2**20)),
        cost_estimate=pl.CostEstimate(flops=flops, bytes_accessed=nbytes, transcendentals=0),
        **kw,
    )(*args)


def weight_kernel(g, cols, *refs):
    ws, (near, far, far_query), sems = refs[:3], refs[3:6], refs[6]
    mine = lax.axis_index("seq") % g
    at = pl.ds(pl.multiple_of(mine * cols, cols), cols)
    size = far.shape[0]
    rows = slice(None)
    if size < near.shape[0]:
        rows = pl.ds(pl.multiple_of(lax.axis_index("grp") * size, size), size)
    copies = []
    for i, w in enumerate(ws):
        to = slice(i * cols, (i + 1) * cols)
        copies.append((w.at[:, at], near.at[:, to]))
        copies.append((w.at[rows, at], far.at[:, to] if i < 2 else far_query))
    copies = [pltpu.make_async_copy(a, b, sems.at[i]) for i, (a, b) in enumerate(copies)]
    for c in copies:
        c.start()
    for c in copies:
        c.wait()


def input_kernel(g, cols, events, offsets, frequency, cot, *bufs):
    mine = (lax.axis_index("seq") % g) // 2
    tokens, width = events.shape
    half = width // 2
    lanes = 128
    column = jnp.transpose(jnp.broadcast_to(offsets[...].astype(F32), (lanes, tokens)))
    for j in range(0, half, lanes):
        angle = column * frequency[:, j : j + lanes]
        for value, start in ((jnp.sin(angle), j), (jnp.cos(angle), half + j)):
            to = slice(start, start + lanes)
            x = (events[:, to].astype(F32) + value).astype(BF16)
            for buf in bufs:
                buf[:, to] = x
    for k, buf in enumerate(bufs):
        buf[:, width:] = cot[:, pl.ds(pl.multiple_of((mine ^ k) * 2 * cols, 2 * cols), 2 * cols)]


def place_rows(full, parts, n, start):
    z = lax.axis_index("sub")
    rows, cols = parts[0].shape[0], full.shape[1]
    full[pl.ds(pl.multiple_of(z * rows, rows), rows), :] = parts[0][:, start : start + cols]
    full[pl.ds(pl.multiple_of((z ^ 1) * rows, rows), rows), :] = parts[1][:, start : start + cols]
    far = parts[2:]
    halves = len(far) // (n - 2)
    size = rows // halves
    for i, part in enumerate(far):
        k = 2 + i // halves
        where = (z ^ k) * rows
        if halves == 2:
            mine = lax.axis_index("grp") * size
            where = where + (size - mine if i % 2 else mine)
        full[pl.ds(pl.multiple_of(where, size), size), :] = part[...]


def features(act, om, h, i, feat, sig):
    hd, m = om.shape[1], om.shape[2]
    rows = act.shape[0]
    soft, s = soft_and_sigmoid(dot(act[:, h * hd : (h + 1) * hd], om[h]))
    soft = soft.astype(BF16)
    at = (slice(i * rows, (i + 1) * rows), slice(h * m, (h + 1) * m))
    feat[at] = soft
    sig[at] = s
    return soft


def put_total(own, send, base, extra, total):
    hd = own.shape[1]
    n = total.shape[1] // hd
    for j in range(n):
        piece = total[:, j * hd : (j + 1) * hd]
        high = piece.astype(BF16)
        own[base + j : base + j + 1, :] = piece
        send[base + j : base + j + 1, :] = high
        own[base + extra + j : base + extra + j + 1, :] = jnp.zeros_like(piece)
        send[base + extra + j : base + extra + j + 1, :] = (piece - high.astype(F32)).astype(BF16)


def get_total(tail, extra, h, m):
    hd = tail.shape[1]
    n = m // hd
    rows = [
        tail[h * n + j : h * n + j + 1, :] + tail[extra + h * n + j : extra + h * n + j + 1, :]
        for j in range(n)
    ]
    return jnp.concatenate(rows, axis=1)


def summed(parts, lo, hi):
    out = parts[0][lo:hi, :]
    for part in parts[1:]:
        out = out + part[lo:hi, :].astype(F32)
    return out


def key_value_kernel(g, n, nw, hp, width, *refs):
    xs, ws, om = refs[:g], refs[g : g + nw], refs[g + nw]
    w_full, feat, sig, val, total = refs[g + nw + 1 :]
    hd, m = om.shape[1], om.shape[2]
    cols = hp * hd
    place_rows(w_full, ws, n, 0)
    rows = xs[0].shape[0]
    sums = [jnp.zeros((1, m), F32) for _ in range(hp)]
    for i, x in enumerate(xs):
        act = dot(x[:, :width], w_full[...]).astype(BF16)
        val[i * rows : (i + 1) * rows, :] = act[:, cols:]
        for h in range(hp):
            soft = features(act, om, h, i, feat, sig)
            sums[h] = sums[h] + jnp.sum(soft.astype(F32), axis=0, keepdims=True)
    total[...] = jnp.concatenate(sums, axis=1)


def summary_kernel(hp, feat, val, total, own, send):
    m, hd = feat.shape[1] // hp, val.shape[1] // hp
    base = hp * m
    own[base:, :] = jnp.zeros_like(own[base:, :])
    send[base:, :] = jnp.zeros_like(send[base:, :])
    for h in range(hp):
        s = dot(feat[:, h * m : (h + 1) * m], val[:, h * hd : (h + 1) * hd], 0, 0)
        own[h * m : (h + 1) * m, :] = s
        send[h * m : (h + 1) * m, :] = s.astype(BF16)
    put_total(own, send, base, hp * m // hd, total[...])


def query_kernel(g, n, nw, hp, width, *refs):
    xs, ws, om = refs[:g], refs[g : g + nw], refs[g + nw]
    w_full, feat, sig = refs[g + nw + 1 :]
    place_rows(w_full, ws, n, 2 * w_full.shape[1])
    for i, x in enumerate(xs):
        act = dot(x[:, :width], w_full[...]).astype(BF16)
        for h in range(hp):
            features(act, om, h, i, feat, sig)


def query_side_kernel(g, p, hp, m, width, loss_scale, *refs):
    parts, xs, feat = refs[:p], refs[p : p + g], refs[p + g]
    total_half, summary_half, scaled_half, norm, own, send = refs[p + g + 1 :]
    hd = summary_half.shape[1]
    cols = hp * hd
    base = hp * m
    extra = base // hd
    summary_half[...] = summed(parts, 0, base).astype(BF16)
    tail = summed(parts, base, parts[0].shape[0])
    core = lax.axis_index("seq") % 2
    rows = xs[0].shape[0]
    own[base:, :] = jnp.zeros_like(own[base:, :])
    send[base:, :] = jnp.zeros_like(send[base:, :])
    sums = []
    for h in range(hp):
        row = get_total(tail, extra, h, m).astype(BF16)
        total_half[:, h * m : (h + 1) * m] = row
        spread = jnp.broadcast_to(row.astype(F32), (hd, m)).astype(BF16)
        acc = jnp.zeros((1, m), F32)
        for i in range(g):
            tok = slice(i * rows, (i + 1) * rows)
            qf = feat[tok, h * m : (h + 1) * m]
            at = pl.multiple_of(width + core * cols + h * hd, hd)
            denom = dot(qf, spread, 1, 1)
            numer = dot(qf, summary_half[h * m : (h + 1) * m, :])
            scaled = xs[i][:, pl.ds(at, hd)].astype(F32) * loss_scale / denom
            scaled_half[tok, h * hd : (h + 1) * hd] = scaled.astype(BF16)
            ng = -jnp.sum(scaled * (numer / denom), axis=1, keepdims=True)
            norm[tok, h : h + 1] = ng
            acc = acc + jnp.sum(qf.astype(F32) * ng.astype(BF16).astype(F32), axis=0, keepdims=True)
        s = dot(feat[:, h * m : (h + 1) * m], scaled_half[:, h * hd : (h + 1) * hd], 0, 0)
        own[h * m : (h + 1) * m, :] = s
        send[h * m : (h + 1) * m, :] = s.astype(BF16)
        sums.append(acc)
    put_total(own, send, base, extra, jnp.concatenate(sums, axis=1))


def query_grad_kernel(hp, scaled_half, summary_half, norm, total_half, sig, om, out):
    hd, m = om.shape[1], om.shape[2]
    for h in range(hp):
        fg = dot(scaled_half[:, h * hd : (h + 1) * hd], summary_half[h * m : (h + 1) * m, :], 1, 1)
        fg = fg + norm[:, h : h + 1] * total_half[:, h * m : (h + 1) * m].astype(F32)
        pg = (fg * sig[:, h * m : (h + 1) * m]).astype(BF16)
        out[:, h * hd : (h + 1) * hd] = dot(pg, om[h], 1, 1).astype(BF16)


def products(g, blocks, qg, kvg, wq, wkv, out):
    rows = qg.shape[0] // g
    for j, i in enumerate(blocks):
        tok = slice(i * rows, (i + 1) * rows)
        o = dot(qg[tok, :], wq[...], 1, 1) + dot(kvg[tok, :], wkv[...], 1, 1)
        out[j * rows : (j + 1) * rows, :] = o.astype(out.dtype)


def key_side_kernel(g, p, hp, *refs):
    parts = refs[:p]
    val, feat, sig, om, qg, wq, wkv = refs[p : p + 7]
    odd, kvg = refs[p + 7 :]
    hd, m = om.shape[1], om.shape[2]
    base = hp * m
    cols = hp * hd
    tail = summed(parts, base, parts[0].shape[0])
    for h in range(hp):
        gh = summed(parts, h * m, (h + 1) * m).astype(BF16)
        col = slice(h * hd, (h + 1) * hd)
        fg = dot(val[:, col], gh, 1, 1) + get_total(tail, base // hd, h, m)
        kvg[:, cols + h * hd : cols + (h + 1) * hd] = dot(feat[:, h * m : (h + 1) * m], gh).astype(BF16)
        pg = (fg * sig[:, h * m : (h + 1) * m]).astype(BF16)
        kvg[:, col] = dot(pg, om[h], 1, 1).astype(BF16)
    products(g, range(3, g, 2), qg, kvg, wq, wkv, odd)


def even_kernel(g, qg, kvg, wq, wkv, even):
    products(g, range(2, g, 2), qg, kvg, wq, wkv, even)


def near_kernel(g, qg, kvg, wq, wkv, top, bottom, zero):
    rows = zero.shape[0]
    half = rows // 2
    for start, out in ((rows, top), (rows + half, bottom)):
        tok = slice(start, start + half)
        o = dot(qg[tok, :], wq[...], 1, 1) + dot(kvg[tok, :], wkv[...], 1, 1)
        out[...] = o.astype(out.dtype)
    products(g, [0], qg, kvg, wq, wkv, zero)


def local(events, offsets, cotangent, query_weight, key_weight, value_weight, omega):
    heads, hd, m = omega.shape
    n_seq, n_sub = lax.axis_size("seq"), lax.axis_size("sub")
    rows, width = events.shape
    loss_scale = math.sqrt(rows * n_seq * n_sub)
    g = math.gcd(heads, n_seq)
    r = n_seq // g
    hp = heads // g
    p = r * n_sub
    t = g * rows
    cols = hp * hd
    srows = hp * m + -(-2 * hp * m // hd // 16) * 16

    def over_seq(x, k):
        return lax.ppermute(x, "seq", [(i, i ^ k) for i in range(n_seq)])

    def over_sub(x, k):
        return lax.ppermute(x, "sub", [(i, i ^ k) for i in range(n_sub)])

    def to_all(own, send):
        parts = [own]
        for j in range(r):
            for k in range(n_sub):
                if j or k:
                    perm = [
                        (a * n_sub + b, (a ^ (j * g)) * n_sub + (b ^ k))
                        for a in range(n_seq)
                        for b in range(n_sub)
                    ]
                    parts.append(lax.ppermute(send, ("seq", "sub"), perm))
        return parts

    wrows = key_weight.shape[0]
    split = lax.axis_size("grp") == 2 and wrows % 32 == 0
    size = wrows // 2 if split else wrows
    wouts = [((wrows, 3 * cols), BF16), ((size, 2 * cols), BF16), ((size, cols), BF16)]
    frequency = jnp.exp(jnp.arange(width // 2, dtype=F32) * (-2.0 * math.log(10000.0) / width))
    near, far, far_query = call(
        functools.partial(weight_kernel, g, cols),
        wouts,
        [key_weight, value_weight, query_weight],
        0,
        vmem=53,
        in_specs=[HBM] * 3,
        scratch_shapes=[pltpu.SemaphoreType.DMA((6,))],
    )
    frequency, _ = lax.optimization_barrier((frequency, near))
    bufs = call(
        functools.partial(input_kernel, g, cols),
        [((rows, width + 2 * cols), BF16)] * (g // 2),
        [events, offsets[None], frequency[None], cotangent],
        0,
    )

    def swapped(parts):
        if not split:
            return parts
        return [x for part in parts for x in (part, lax.ppermute(part, "grp", [(0, 1), (1, 0)]))]

    nearest = over_sub(near, 1)
    arrived = [over_sub(far, k) for k in range(2, n_sub)]
    kvs = [near, nearest] + swapped(arrived)
    xs = [bufs[0]] * g
    for k in range(2, g, 2):
        xs[k] = over_seq(bufs[k // 2], k)
    xs[1] = over_seq(bufs[0], 1)
    xs[2:], _ = lax.optimization_barrier((xs[2:], arrived))
    for k in range(3, g, 2):
        xs[k] = over_seq(xs[k ^ 1], 1)
    far_query, _ = lax.optimization_barrier((far_query, arrived + xs[1:2]))
    query_rows = [over_sub(far_query, k) for k in range(2, n_sub)]
    om = lax.dynamic_slice_in_dim(omega, (lax.axis_index("seq") % g) * hp, hp, 0)

    flop = 2 * t * width * cols
    summary_out = [((srows, hd), F32), ((srows, hd), BF16)]
    wkv_full, key_feat, key_sig, val, total = call(
        functools.partial(key_value_kernel, g, n_sub, len(kvs), hp, width),
        [((width, 2 * cols), BF16), ((t, hp * m), BF16), ((t, hp * m), F32), ((t, cols), BF16), ((1, hp * m), F32)],
        [*xs, *kvs, om],
        8 * flop,
    )
    total, _ = lax.optimization_barrier((total, query_rows))
    own, send = call(functools.partial(summary_kernel, hp), summary_out, [key_feat, val, total], 0)
    summary = to_all(own, send)
    query_rows, _ = lax.optimization_barrier((query_rows, val))
    qs = [near, nearest] + swapped(query_rows)
    wq_full, query_feat, query_sig = call(
        functools.partial(query_kernel, g, n_sub, len(qs), hp, width),
        [((width, cols), BF16), ((t, hp * m), BF16), ((t, hp * m), F32)],
        [*xs, *qs, om],
        0,
    )
    total_half, summary_half, scaled_half, norm, own, send = call(
        functools.partial(query_side_kernel, g, p, hp, m, width, loss_scale),
        [((1, hp * m), BF16), ((hp * m, hd), BF16), ((t, cols), BF16), ((t, hp), F32)] + summary_out,
        [*summary, *xs, query_feat],
        8 * flop,
    )
    summary_grad = to_all(own, send)
    (query_grad,) = call(
        functools.partial(query_grad_kernel, hp),
        [((t, cols), BF16)],
        [scaled_half, summary_half, norm, total_half, query_sig, om],
        4 * flop,
    )
    others = g // 2 - 1
    odd, key_value_grad = call(
        functools.partial(key_side_kernel, g, p, hp),
        [((others * rows, width), BF16), ((t, 2 * cols), BF16)],
        [*summary_grad, val, key_feat, key_sig, om, query_grad, wq_full, wkv_full],
        8 * flop,
    )
    got = over_seq(odd, 1)
    grads = [query_grad, key_value_grad, wq_full, wkv_full]
    (even,) = call(functools.partial(even_kernel, g), [((others * rows, width), F32)], grads, 8 * flop)
    both = (even + got.astype(F32)).astype(BF16)
    top, bottom, zero = call(
        functools.partial(near_kernel, g),
        [((rows // 2, width), BF16), ((rows // 2, width), BF16), ((rows, width), F32)],
        grads,
        0,
    )
    near_sum = jnp.concatenate([over_seq(top, 1), over_seq(bottom, 1)], axis=0)
    out = zero + near_sum.astype(F32)
    for k in range(2, g, 2):
        at = (k // 2 - 1) * rows
        out = out + over_seq(both[at : at + rows], k).astype(F32)
    return out.astype(BF16)


def solution(mesh):
    in_specs = (
        P(("grp", "seq", "sub"), None),
        P(("grp", "seq", "sub")),
        P(("grp", "seq", "sub"), None),
        P("sub", None),
        P("sub", None),
        P("sub", None),
        P(),
    )
    out_specs = P(("grp", "seq", "sub"), None)
    return jax.shard_map(local, mesh=mesh, in_specs=in_specs, out_specs=out_specs, check_vma=False)
```

```python
import functools
import math

import jax
import jax.numpy as jnp
from jax import lax
from jax.experimental import pallas as pl
from jax.experimental.pallas import tpu as pltpu
from jax.sharding import PartitionSpec as P

F32 = jnp.float32
BF16 = jnp.bfloat16
HBM = pl.BlockSpec(memory_space=pltpu.HBM)


def dot(a, b, ca=1, cb=0):
    return lax.dot_general(a, b, (((ca,), (cb,)), ((), ())), preferred_element_type=F32)


def soft_and_sigmoid(u):
    e = jnp.exp(-jnp.abs(u))
    series = e * (1.0 + e * (-0.5 + e * (1.0 / 3.0)))
    soft = jnp.maximum(u, 0.0) + jnp.where(e < 1e-3, series, jnp.log(1.0 + e))
    r = 1.0 / (1.0 + e)
    return soft, jnp.where(u >= 0.0, r, e * r)


def call(body, outs, args, flops, vmem=24, **kw):
    nbytes = sum(a.size * a.dtype.itemsize for a in args) if flops else 0
    return pl.pallas_call(
        body,
        out_shape=[jax.ShapeDtypeStruct(s, d) for s, d in outs],
        compiler_params=pltpu.CompilerParams(vmem_limit_bytes=int(vmem * 2**20)),
        cost_estimate=pl.CostEstimate(flops=flops, bytes_accessed=nbytes, transcendentals=0),
        **kw,
    )(*args)


def weight_kernel(g, cols, *refs):
    ws, (near, far, far_query), sems = refs[:3], refs[3:6], refs[6]
    mine = lax.axis_index("seq") % g
    at = pl.ds(pl.multiple_of(mine * cols, cols), cols)
    size = far.shape[0]
    rows = slice(None)
    if size < near.shape[0]:
        rows = pl.ds(pl.multiple_of(lax.axis_index("grp") * size, size), size)
    copies = []
    for i, w in enumerate(ws):
        to = slice(i * cols, (i + 1) * cols)
        copies.append((w.at[:, at], near.at[:, to]))
        copies.append((w.at[rows, at], far.at[:, to] if i < 2 else far_query))
    copies = [pltpu.make_async_copy(a, b, sems.at[i]) for i, (a, b) in enumerate(copies)]
    for c in copies:
        c.start()
    for c in copies:
        c.wait()


def input_kernel(g, cols, events, offsets, frequency, cot, *bufs):
    mine = (lax.axis_index("seq") % g) // 2
    tokens, width = events.shape
    half = width // 2
    lanes = 128
    column = jnp.transpose(jnp.broadcast_to(offsets[...].astype(F32), (lanes, tokens)))
    for j in range(0, half, lanes):
        angle = column * frequency[:, j : j + lanes]
        for value, start in ((jnp.sin(angle), j), (jnp.cos(angle), half + j)):
            to = slice(start, start + lanes)
            x = (events[:, to].astype(F32) + value).astype(BF16)
            for buf in bufs:
                buf[:, to] = x
    for k, buf in enumerate(bufs):
        buf[:, width:] = cot[:, pl.ds(pl.multiple_of((mine ^ k) * 2 * cols, 2 * cols), 2 * cols)]


def place_rows(full, parts, n, start):
    z = lax.axis_index("sub")
    rows, cols = parts[0].shape[0], full.shape[1]
    full[pl.ds(pl.multiple_of(z * rows, rows), rows), :] = parts[0][:, start : start + cols]
    full[pl.ds(pl.multiple_of((z ^ 1) * rows, rows), rows), :] = parts[1][:, start : start + cols]
    far = parts[2:]
    halves = len(far) // (n - 2)
    size = rows // halves
    for i, part in enumerate(far):
        k = 2 + i // halves
        where = (z ^ k) * rows
        if halves == 2:
            mine = lax.axis_index("grp") * size
            where = where + (size - mine if i % 2 else mine)
        full[pl.ds(pl.multiple_of(where, size), size), :] = part[...]


def features(act, om, h, i, feat, sig):
    hd, m = om.shape[1], om.shape[2]
    rows = act.shape[0]
    soft, s = soft_and_sigmoid(dot(act[:, h * hd : (h + 1) * hd], om[h]))
    soft = soft.astype(BF16)
    at = (slice(i * rows, (i + 1) * rows), slice(h * m, (h + 1) * m))
    feat[at] = soft
    sig[at] = s
    return soft


def put_total(own, send, base, extra, total):
    hd = own.shape[1]
    n = total.shape[1] // hd
    for j in range(n):
        piece = total[:, j * hd : (j + 1) * hd]
        high = piece.astype(BF16)
        own[base + j : base + j + 1, :] = piece
        send[base + j : base + j + 1, :] = high
        own[base + extra + j : base + extra + j + 1, :] = jnp.zeros_like(piece)
        send[base + extra + j : base + extra + j + 1, :] = (piece - high.astype(F32)).astype(BF16)


def get_total(tail, extra, h, m):
    hd = tail.shape[1]
    n = m // hd
    rows = [
        tail[h * n + j : h * n + j + 1, :] + tail[extra + h * n + j : extra + h * n + j + 1, :]
        for j in range(n)
    ]
    return jnp.concatenate(rows, axis=1)


def summed(parts, lo, hi):
    out = parts[0][lo:hi, :]
    for part in parts[1:]:
        out = out + part[lo:hi, :].astype(F32)
    return out


def key_value_kernel(g, n, nw, hp, width, *refs):
    xs, ws, om = refs[:g], refs[g : g + nw], refs[g + nw]
    w_full, feat, sig, val, total = refs[g + nw + 1 :]
    hd, m = om.shape[1], om.shape[2]
    cols = hp * hd
    place_rows(w_full, ws, n, 0)
    rows = xs[0].shape[0]
    sums = [jnp.zeros((1, m), F32) for _ in range(hp)]
    for i, x in enumerate(xs):
        act = dot(x[:, :width], w_full[...]).astype(BF16)
        val[i * rows : (i + 1) * rows, :] = act[:, cols:]
        for h in range(hp):
            soft = features(act, om, h, i, feat, sig)
            sums[h] = sums[h] + jnp.sum(soft.astype(F32), axis=0, keepdims=True)
    total[...] = jnp.concatenate(sums, axis=1)


def summary_kernel(hp, feat, val, total, own, send):
    m, hd = feat.shape[1] // hp, val.shape[1] // hp
    base = hp * m
    own[base:, :] = jnp.zeros_like(own[base:, :])
    send[base:, :] = jnp.zeros_like(send[base:, :])
    for h in range(hp):
        s = dot(feat[:, h * m : (h + 1) * m], val[:, h * hd : (h + 1) * hd], 0, 0)
        own[h * m : (h + 1) * m, :] = s
        send[h * m : (h + 1) * m, :] = s.astype(BF16)
    put_total(own, send, base, hp * m // hd, total[...])


def query_kernel(g, n, nw, hp, width, *refs):
    xs, ws, om = refs[:g], refs[g : g + nw], refs[g + nw]
    w_full, feat, sig = refs[g + nw + 1 :]
    place_rows(w_full, ws, n, 2 * w_full.shape[1])
    for i, x in enumerate(xs):
        act = dot(x[:, :width], w_full[...]).astype(BF16)
        for h in range(hp):
            features(act, om, h, i, feat, sig)


def query_side_kernel(g, p, hp, m, width, loss_scale, *refs):
    parts, xs, feat = refs[:p], refs[p : p + g], refs[p + g]
    total_half, summary_half, scaled_half, norm, own, send = refs[p + g + 1 :]
    hd = summary_half.shape[1]
    cols = hp * hd
    base = hp * m
    extra = base // hd
    summary_half[...] = summed(parts, 0, base).astype(BF16)
    tail = summed(parts, base, parts[0].shape[0])
    core = lax.axis_index("seq") % 2
    rows = xs[0].shape[0]
    own[base:, :] = jnp.zeros_like(own[base:, :])
    send[base:, :] = jnp.zeros_like(send[base:, :])
    sums = []
    for h in range(hp):
        row = get_total(tail, extra, h, m).astype(BF16)
        total_half[:, h * m : (h + 1) * m] = row
        spread = jnp.broadcast_to(row.astype(F32), (hd, m)).astype(BF16)
        acc = jnp.zeros((1, m), F32)
        for i in range(g):
            tok = slice(i * rows, (i + 1) * rows)
            qf = feat[tok, h * m : (h + 1) * m]
            at = pl.multiple_of(width + core * cols + h * hd, hd)
            denom = dot(qf, spread, 1, 1)
            numer = dot(qf, summary_half[h * m : (h + 1) * m, :])
            scaled = xs[i][:, pl.ds(at, hd)].astype(F32) * loss_scale / denom
            scaled_half[tok, h * hd : (h + 1) * hd] = scaled.astype(BF16)
            ng = -jnp.sum(scaled * (numer / denom), axis=1, keepdims=True)
            norm[tok, h : h + 1] = ng
            acc = acc + jnp.sum(qf.astype(F32) * ng.astype(BF16).astype(F32), axis=0, keepdims=True)
        s = dot(feat[:, h * m : (h + 1) * m], scaled_half[:, h * hd : (h + 1) * hd], 0, 0)
        own[h * m : (h + 1) * m, :] = s
        send[h * m : (h + 1) * m, :] = s.astype(BF16)
        sums.append(acc)
    put_total(own, send, base, extra, jnp.concatenate(sums, axis=1))


def query_grad_kernel(hp, scaled_half, summary_half, norm, total_half, sig, om, out):
    hd, m = om.shape[1], om.shape[2]
    for h in range(hp):
        fg = dot(scaled_half[:, h * hd : (h + 1) * hd], summary_half[h * m : (h + 1) * m, :], 1, 1)
        fg = fg + norm[:, h : h + 1] * total_half[:, h * m : (h + 1) * m].astype(F32)
        pg = (fg * sig[:, h * m : (h + 1) * m]).astype(BF16)
        out[:, h * hd : (h + 1) * hd] = dot(pg, om[h], 1, 1).astype(BF16)


def products(g, blocks, qg, kvg, wq, wkv, out):
    rows = qg.shape[0] // g
    for j, i in enumerate(blocks):
        tok = slice(i * rows, (i + 1) * rows)
        o = dot(qg[tok, :], wq[...], 1, 1) + dot(kvg[tok, :], wkv[...], 1, 1)
        out[j * rows : (j + 1) * rows, :] = o.astype(out.dtype)


def key_side_kernel(g, p, hp, *refs):
    parts = refs[:p]
    val, feat, sig, om, qg, wq, wkv = refs[p : p + 7]
    odd, kvg = refs[p + 7 :]
    hd, m = om.shape[1], om.shape[2]
    base = hp * m
    cols = hp * hd
    tail = summed(parts, base, parts[0].shape[0])
    for h in range(hp):
        gh = summed(parts, h * m, (h + 1) * m).astype(BF16)
        col = slice(h * hd, (h + 1) * hd)
        fg = dot(val[:, col], gh, 1, 1) + get_total(tail, base // hd, h, m)
        kvg[:, cols + h * hd : cols + (h + 1) * hd] = dot(feat[:, h * m : (h + 1) * m], gh).astype(BF16)
        pg = (fg * sig[:, h * m : (h + 1) * m]).astype(BF16)
        kvg[:, col] = dot(pg, om[h], 1, 1).astype(BF16)
    products(g, range(3, g, 2), qg, kvg, wq, wkv, odd)


def even_kernel(g, qg, kvg, wq, wkv, even):
    products(g, range(2, g, 2), qg, kvg, wq, wkv, even)


def near_kernel(g, qg, kvg, wq, wkv, top, bottom, zero):
    rows = zero.shape[0]
    half = rows // 2
    for start, out in ((rows, top), (rows + half, bottom)):
        tok = slice(start, start + half)
        o = dot(qg[tok, :], wq[...], 1, 1) + dot(kvg[tok, :], wkv[...], 1, 1)
        out[...] = o.astype(out.dtype)
    products(g, [0], qg, kvg, wq, wkv, zero)


def local(events, offsets, cotangent, query_weight, key_weight, value_weight, omega):
    heads, hd, m = omega.shape
    n_seq, n_sub = lax.axis_size("seq"), lax.axis_size("sub")
    rows, width = events.shape
    loss_scale = math.sqrt(rows * n_seq * n_sub)
    g = math.gcd(heads, n_seq)
    r = n_seq // g
    hp = heads // g
    p = r * n_sub
    t = g * rows
    cols = hp * hd
    srows = hp * m + -(-2 * hp * m // hd // 16) * 16

    def over_seq(x, k):
        return lax.ppermute(x, "seq", [(i, i ^ k) for i in range(n_seq)])

    def over_sub(x, k):
        return lax.ppermute(x, "sub", [(i, i ^ k) for i in range(n_sub)])

    def to_all(own, send):
        order = [*range(n_sub - 2, -1, -1), n_sub - 1]
        parts = [own]
        for j in range(r):
            for k in order:
                if j or k:
                    perm = [
                        (a * n_sub + b, (a ^ (j * g)) * n_sub + (b ^ k))
                        for a in range(n_seq)
                        for b in range(n_sub)
                    ]
                    parts.append(lax.ppermute(send, ("seq", "sub"), perm))
        return parts

    wrows = key_weight.shape[0]
    split = lax.axis_size("grp") == 2 and wrows % 32 == 0
    size = wrows // 2 if split else wrows
    wouts = [((wrows, 3 * cols), BF16), ((size, 2 * cols), BF16), ((size, cols), BF16)]
    frequency = jnp.exp(jnp.arange(width // 2, dtype=F32) * (-2.0 * math.log(10000.0) / width))
    near, far, far_query = call(
        functools.partial(weight_kernel, g, cols),
        wouts,
        [key_weight, value_weight, query_weight],
        0,
        vmem=53,
        in_specs=[HBM] * 3,
        scratch_shapes=[pltpu.SemaphoreType.DMA((6,))],
    )
    frequency, _ = lax.optimization_barrier((frequency, near))
    bufs = call(
        functools.partial(input_kernel, g, cols),
        [((rows, width + 2 * cols), BF16)] * (g // 2),
        [events, offsets[None], frequency[None], cotangent],
        0,
    )

    def swapped(parts):
        if not split:
            return parts
        return [x for part in parts for x in (part, lax.ppermute(part, "grp", [(0, 1), (1, 0)]))]

    nearest = over_sub(near, 1)
    arrived = [over_sub(far, k) for k in range(2, n_sub)]
    kvs = [near, nearest] + swapped(arrived)
    xs = [bufs[0]] * g
    for k in range(2, g, 2):
        xs[k] = over_seq(bufs[k // 2], k)
    xs[1] = over_seq(bufs[0], 1)
    xs[2:], _ = lax.optimization_barrier((xs[2:], arrived))
    for k in range(3, g, 2):
        xs[k] = over_seq(xs[k ^ 1], 1)
    far_query, _ = lax.optimization_barrier((far_query, arrived + xs[1:2]))
    query_rows = [over_sub(far_query, k) for k in range(2, n_sub)]
    om = lax.dynamic_slice_in_dim(omega, (lax.axis_index("seq") % g) * hp, hp, 0)

    flop = 2 * t * width * cols
    summary_out = [((srows, hd), F32), ((srows, hd), BF16)]
    wkv_full, key_feat, key_sig, val, total = call(
        functools.partial(key_value_kernel, g, n_sub, len(kvs), hp, width),
        [((width, 2 * cols), BF16), ((t, hp * m), BF16), ((t, hp * m), F32), ((t, cols), BF16), ((1, hp * m), F32)],
        [*xs, *kvs, om],
        8 * flop,
    )
    total, _ = lax.optimization_barrier((total, query_rows))
    own, send = call(functools.partial(summary_kernel, hp), summary_out, [key_feat, val, total], 0)
    summary = to_all(own, send)
    query_rows, _ = lax.optimization_barrier((query_rows, val))
    qs = [near, nearest] + swapped(query_rows)
    wq_full, query_feat, query_sig = call(
        functools.partial(query_kernel, g, n_sub, len(qs), hp, width),
        [((width, cols), BF16), ((t, hp * m), BF16), ((t, hp * m), F32)],
        [*xs, *qs, om],
        0,
    )
    total_half, summary_half, scaled_half, norm, own, send = call(
        functools.partial(query_side_kernel, g, p, hp, m, width, loss_scale),
        [((1, hp * m), BF16), ((hp * m, hd), BF16), ((t, cols), BF16), ((t, hp), F32)] + summary_out,
        [*summary, *xs, query_feat],
        8 * flop,
    )
    summary_grad = to_all(own, send)
    (query_grad,) = call(
        functools.partial(query_grad_kernel, hp),
        [((t, cols), BF16)],
        [scaled_half, summary_half, norm, total_half, query_sig, om],
        4 * flop,
    )
    others = g // 2 - 1
    odd, key_value_grad = call(
        functools.partial(key_side_kernel, g, p, hp),
        [((others * rows, width), BF16), ((t, 2 * cols), BF16)],
        [*summary_grad, val, key_feat, key_sig, om, query_grad, wq_full, wkv_full],
        8 * flop,
    )
    got = over_seq(odd, 1)
    grads = [query_grad, key_value_grad, wq_full, wkv_full]
    (even,) = call(functools.partial(even_kernel, g), [((others * rows, width), F32)], grads, 8 * flop)
    both = (even + got.astype(F32)).astype(BF16)
    top, bottom, zero = call(
        functools.partial(near_kernel, g),
        [((rows // 2, width), BF16), ((rows // 2, width), BF16), ((rows, width), F32)],
        grads,
        0,
    )
    near_sum = jnp.concatenate([over_seq(top, 1), over_seq(bottom, 1)], axis=0)
    out = zero + near_sum.astype(F32)
    for k in range(2, g, 2):
        at = (k // 2 - 1) * rows
        out = out + over_seq(both[at : at + rows], k).astype(F32)
    return out.astype(BF16)


def solution(mesh):
    in_specs = (
        P(("grp", "seq", "sub"), None),
        P(("grp", "seq", "sub")),
        P(("grp", "seq", "sub"), None),
        P("sub", None),
        P("sub", None),
        P("sub", None),
        P(),
    )
    out_specs = P(("grp", "seq", "sub"), None)
    return jax.shard_map(local, mesh=mesh, in_specs=in_specs, out_specs=out_specs, check_vma=False)
```

```python
import functools
import math

import jax
import jax.numpy as jnp
from jax import lax
from jax.experimental import pallas as pl
from jax.experimental.pallas import tpu as pltpu
from jax.sharding import PartitionSpec as P

F32 = jnp.float32
BF16 = jnp.bfloat16
HBM = pl.BlockSpec(memory_space=pltpu.HBM)


def dot(a, b, ca=1, cb=0):
    return lax.dot_general(a, b, (((ca,), (cb,)), ((), ())), preferred_element_type=F32)


def soft_and_sigmoid(u):
    e = jnp.exp(-jnp.abs(u))
    series = e * (1.0 + e * (-0.5 + e * (1.0 / 3.0)))
    soft = jnp.maximum(u, 0.0) + jnp.where(e < 1e-3, series, jnp.log(1.0 + e))
    r = 1.0 / (1.0 + e)
    return soft, jnp.where(u >= 0.0, r, e * r)


def call(body, outs, args, flops, vmem=24, **kw):
    nbytes = sum(a.size * a.dtype.itemsize for a in args) if flops else 0
    return pl.pallas_call(
        body,
        out_shape=[jax.ShapeDtypeStruct(s, d) for s, d in outs],
        compiler_params=pltpu.CompilerParams(vmem_limit_bytes=int(vmem * 2**20)),
        cost_estimate=pl.CostEstimate(flops=flops, bytes_accessed=nbytes, transcendentals=0),
        **kw,
    )(*args)


def weight_kernel(g, cols, *refs):
    ws, (near, far, far_query), sems = refs[:3], refs[3:6], refs[6]
    mine = lax.axis_index("seq") % g
    at = pl.ds(pl.multiple_of(mine * cols, cols), cols)
    size = far.shape[0]
    rows = slice(None)
    if size < near.shape[0]:
        rows = pl.ds(pl.multiple_of(lax.axis_index("grp") * size, size), size)
    copies = []
    for i, w in enumerate(ws):
        to = slice(i * cols, (i + 1) * cols)
        copies.append((w.at[:, at], near.at[:, to]))
        copies.append((w.at[rows, at], far.at[:, to] if i < 2 else far_query))
    copies = [pltpu.make_async_copy(a, b, sems.at[i]) for i, (a, b) in enumerate(copies)]
    for c in copies:
        c.start()
    for c in copies:
        c.wait()


def input_kernel(g, cols, events, offsets, frequency, cot, *bufs):
    mine = (lax.axis_index("seq") % g) // 2
    tokens, width = events.shape
    half = width // 2
    lanes = 128
    column = jnp.transpose(jnp.broadcast_to(offsets[...].astype(F32), (lanes, tokens)))
    for j in range(0, half, lanes):
        angle = column * frequency[:, j : j + lanes]
        for value, start in ((jnp.sin(angle), j), (jnp.cos(angle), half + j)):
            to = slice(start, start + lanes)
            x = (events[:, to].astype(F32) + value).astype(BF16)
            for buf in bufs:
                buf[:, to] = x
    for k, buf in enumerate(bufs):
        buf[:, width:] = cot[:, pl.ds(pl.multiple_of((mine ^ k) * 2 * cols, 2 * cols), 2 * cols)]


def place_rows(full, parts, n, start):
    z = lax.axis_index("sub")
    rows, cols = parts[0].shape[0], full.shape[1]
    full[pl.ds(pl.multiple_of(z * rows, rows), rows), :] = parts[0][:, start : start + cols]
    full[pl.ds(pl.multiple_of((z ^ 1) * rows, rows), rows), :] = parts[1][:, start : start + cols]
    far = parts[2:]
    halves = len(far) // (n - 2)
    size = rows // halves
    for i, part in enumerate(far):
        k = 2 + i // halves
        where = (z ^ k) * rows
        if halves == 2:
            mine = lax.axis_index("grp") * size
            where = where + (size - mine if i % 2 else mine)
        full[pl.ds(pl.multiple_of(where, size), size), :] = part[...]


def features(act, om, h, i, feat, sig):
    hd, m = om.shape[1], om.shape[2]
    rows = act.shape[0]
    soft, s = soft_and_sigmoid(dot(act[:, h * hd : (h + 1) * hd], om[h]))
    soft = soft.astype(BF16)
    at = (slice(i * rows, (i + 1) * rows), slice(h * m, (h + 1) * m))
    feat[at] = soft
    sig[at] = s
    return soft


def put_total(own, send, base, extra, total):
    hd = own.shape[1]
    n = total.shape[1] // hd
    for j in range(n):
        piece = total[:, j * hd : (j + 1) * hd]
        high = piece.astype(BF16)
        own[base + j : base + j + 1, :] = piece
        send[base + j : base + j + 1, :] = high
        own[base + extra + j : base + extra + j + 1, :] = jnp.zeros_like(piece)
        send[base + extra + j : base + extra + j + 1, :] = (piece - high.astype(F32)).astype(BF16)


def get_total(tail, extra, h, m):
    hd = tail.shape[1]
    n = m // hd
    rows = [
        tail[h * n + j : h * n + j + 1, :] + tail[extra + h * n + j : extra + h * n + j + 1, :]
        for j in range(n)
    ]
    return jnp.concatenate(rows, axis=1)


def summed(parts, lo, hi):
    out = parts[0][lo:hi, :]
    for part in parts[1:]:
        out = out + part[lo:hi, :].astype(F32)
    return out


def key_value_kernel(g, n, nw, hp, width, *refs):
    xs, ws, om = refs[:g], refs[g : g + nw], refs[g + nw]
    w_full, feat, sig, val, total = refs[g + nw + 1 :]
    hd, m = om.shape[1], om.shape[2]
    cols = hp * hd
    place_rows(w_full, ws, n, 0)
    rows = xs[0].shape[0]
    sums = [jnp.zeros((1, m), F32) for _ in range(hp)]
    for i, x in enumerate(xs):
        act = dot(x[:, :width], w_full[...]).astype(BF16)
        val[i * rows : (i + 1) * rows, :] = act[:, cols:]
        for h in range(hp):
            soft = features(act, om, h, i, feat, sig)
            sums[h] = sums[h] + jnp.sum(soft.astype(F32), axis=0, keepdims=True)
    total[...] = jnp.concatenate(sums, axis=1)


def summary_kernel(hp, feat, val, total, own, send):
    m, hd = feat.shape[1] // hp, val.shape[1] // hp
    base = hp * m
    own[base:, :] = jnp.zeros_like(own[base:, :])
    send[base:, :] = jnp.zeros_like(send[base:, :])
    for h in range(hp):
        s = dot(feat[:, h * m : (h + 1) * m], val[:, h * hd : (h + 1) * hd], 0, 0)
        own[h * m : (h + 1) * m, :] = s
        send[h * m : (h + 1) * m, :] = s.astype(BF16)
    put_total(own, send, base, hp * m // hd, total[...])


def query_kernel(g, n, nw, hp, width, *refs):
    xs, ws, om = refs[:g], refs[g : g + nw], refs[g + nw]
    w_full, feat, sig = refs[g + nw + 1 :]
    place_rows(w_full, ws, n, 2 * w_full.shape[1])
    for i, x in enumerate(xs):
        act = dot(x[:, :width], w_full[...]).astype(BF16)
        for h in range(hp):
            features(act, om, h, i, feat, sig)


def query_side_kernel(g, p, hp, m, width, loss_scale, *refs):
    parts, xs, feat = refs[:p], refs[p : p + g], refs[p + g]
    total_half, summary_half, scaled_half, norm, own, send = refs[p + g + 1 :]
    hd = summary_half.shape[1]
    cols = hp * hd
    base = hp * m
    extra = base // hd
    summary_half[...] = summed(parts, 0, base).astype(BF16)
    tail = summed(parts, base, parts[0].shape[0])
    core = lax.axis_index("seq") % 2
    rows = xs[0].shape[0]
    own[base:, :] = jnp.zeros_like(own[base:, :])
    send[base:, :] = jnp.zeros_like(send[base:, :])
    sums = []
    for h in range(hp):
        row = get_total(tail, extra, h, m).astype(BF16)
        total_half[:, h * m : (h + 1) * m] = row
        spread = jnp.broadcast_to(row.astype(F32), (hd, m)).astype(BF16)
        acc = jnp.zeros((1, m), F32)
        for i in range(g):
            tok = slice(i * rows, (i + 1) * rows)
            qf = feat[tok, h * m : (h + 1) * m]
            at = pl.multiple_of(width + core * cols + h * hd, hd)
            denom = dot(qf, spread, 1, 1)
            numer = dot(qf, summary_half[h * m : (h + 1) * m, :])
            scaled = xs[i][:, pl.ds(at, hd)].astype(F32) * loss_scale / denom
            scaled_half[tok, h * hd : (h + 1) * hd] = scaled.astype(BF16)
            ng = -jnp.sum(scaled * (numer / denom), axis=1, keepdims=True)
            norm[tok, h : h + 1] = ng
            acc = acc + jnp.sum(qf.astype(F32) * ng.astype(BF16).astype(F32), axis=0, keepdims=True)
        s = dot(feat[:, h * m : (h + 1) * m], scaled_half[:, h * hd : (h + 1) * hd], 0, 0)
        own[h * m : (h + 1) * m, :] = s
        send[h * m : (h + 1) * m, :] = s.astype(BF16)
        sums.append(acc)
    put_total(own, send, base, extra, jnp.concatenate(sums, axis=1))


def query_grad_kernel(hp, scaled_half, summary_half, norm, total_half, sig, om, out):
    hd, m = om.shape[1], om.shape[2]
    for h in range(hp):
        fg = dot(scaled_half[:, h * hd : (h + 1) * hd], summary_half[h * m : (h + 1) * m, :], 1, 1)
        fg = fg + norm[:, h : h + 1] * total_half[:, h * m : (h + 1) * m].astype(F32)
        pg = (fg * sig[:, h * m : (h + 1) * m]).astype(BF16)
        out[:, h * hd : (h + 1) * hd] = dot(pg, om[h], 1, 1).astype(BF16)


def products(g, blocks, qg, kvg, wq, wkv, out):
    rows = qg.shape[0] // g
    for j, i in enumerate(blocks):
        tok = slice(i * rows, (i + 1) * rows)
        o = dot(qg[tok, :], wq[...], 1, 1) + dot(kvg[tok, :], wkv[...], 1, 1)
        out[j * rows : (j + 1) * rows, :] = o.astype(out.dtype)


def key_side_kernel(g, p, hp, *refs):
    parts = refs[:p]
    val, feat, sig, om, qg, wq, wkv = refs[p : p + 7]
    odd, kvg = refs[p + 7 :]
    hd, m = om.shape[1], om.shape[2]
    base = hp * m
    cols = hp * hd
    tail = summed(parts, base, parts[0].shape[0])
    for h in range(hp):
        gh = summed(parts, h * m, (h + 1) * m).astype(BF16)
        col = slice(h * hd, (h + 1) * hd)
        fg = dot(val[:, col], gh, 1, 1) + get_total(tail, base // hd, h, m)
        kvg[:, cols + h * hd : cols + (h + 1) * hd] = dot(feat[:, h * m : (h + 1) * m], gh).astype(BF16)
        pg = (fg * sig[:, h * m : (h + 1) * m]).astype(BF16)
        kvg[:, col] = dot(pg, om[h], 1, 1).astype(BF16)
    products(g, range(3, g, 2), qg, kvg, wq, wkv, odd)


def even_kernel(g, qg, kvg, wq, wkv, even):
    products(g, range(2, g, 2), qg, kvg, wq, wkv, even)


def near_kernel(g, qg, kvg, wq, wkv, top, bottom, zero):
    rows = zero.shape[0]
    half = rows // 2
    for start, out in ((rows, top), (rows + half, bottom)):
        tok = slice(start, start + half)
        o = dot(qg[tok, :], wq[...], 1, 1) + dot(kvg[tok, :], wkv[...], 1, 1)
        out[...] = o.astype(out.dtype)
    products(g, [0], qg, kvg, wq, wkv, zero)


def local(events, offsets, cotangent, query_weight, key_weight, value_weight, omega):
    heads, hd, m = omega.shape
    n_seq, n_sub = lax.axis_size("seq"), lax.axis_size("sub")
    rows, width = events.shape
    loss_scale = math.sqrt(rows * n_seq * n_sub)
    g = math.gcd(heads, n_seq)
    r = n_seq // g
    hp = heads // g
    p = r * n_sub
    t = g * rows
    cols = hp * hd
    srows = hp * m + -(-2 * hp * m // hd // 16) * 16

    def over_seq(x, k):
        return lax.ppermute(x, "seq", [(i, i ^ k) for i in range(n_seq)])

    def over_sub(x, k):
        return lax.ppermute(x, "sub", [(i, i ^ k) for i in range(n_sub)])

    far_first = [*range(n_sub - 2, -1, -1), n_sub - 1]
    far_last = [n_sub - 1, *range(n_sub - 1)]

    def to_all(own, send, order):
        parts = [own]
        for j in range(r):
            for k in order:
                if j or k:
                    perm = [
                        (a * n_sub + b, (a ^ (j * g)) * n_sub + (b ^ k))
                        for a in range(n_seq)
                        for b in range(n_sub)
                    ]
                    parts.append(lax.ppermute(send, ("seq", "sub"), perm))
        return parts

    wrows = key_weight.shape[0]
    split = lax.axis_size("grp") == 2 and wrows % 32 == 0
    size = wrows // 2 if split else wrows
    wouts = [((wrows, 3 * cols), BF16), ((size, 2 * cols), BF16), ((size, cols), BF16)]
    frequency = jnp.exp(jnp.arange(width // 2, dtype=F32) * (-2.0 * math.log(10000.0) / width))
    near, far, far_query = call(
        functools.partial(weight_kernel, g, cols),
        wouts,
        [key_weight, value_weight, query_weight],
        0,
        vmem=53,
        in_specs=[HBM] * 3,
        scratch_shapes=[pltpu.SemaphoreType.DMA((6,))],
    )
    frequency, _ = lax.optimization_barrier((frequency, near))
    bufs = call(
        functools.partial(input_kernel, g, cols),
        [((rows, width + 2 * cols), BF16)] * (g // 2),
        [events, offsets[None], frequency[None], cotangent],
        0,
    )

    def swapped(parts):
        if not split:
            return parts
        return [x for part in parts for x in (part, lax.ppermute(part, "grp", [(0, 1), (1, 0)]))]

    nearest = over_sub(near, 1)
    arrived = [over_sub(far, k) for k in range(2, n_sub)]
    kvs = [near, nearest] + swapped(arrived)
    xs = [bufs[0]] * g
    for k in range(2, g, 2):
        xs[k] = over_seq(bufs[k // 2], k)
    xs[1] = over_seq(bufs[0], 1)
    xs[2:], _ = lax.optimization_barrier((xs[2:], arrived))
    for k in range(3, g, 2):
        xs[k] = over_seq(xs[k ^ 1], 1)
    far_query, _ = lax.optimization_barrier((far_query, arrived + xs[1:2]))
    query_rows = [over_sub(far_query, k) for k in range(2, n_sub)]
    om = lax.dynamic_slice_in_dim(omega, (lax.axis_index("seq") % g) * hp, hp, 0)

    flop = 2 * t * width * cols
    summary_out = [((srows, hd), F32), ((srows, hd), BF16)]
    wkv_full, key_feat, key_sig, val, total = call(
        functools.partial(key_value_kernel, g, n_sub, len(kvs), hp, width),
        [((width, 2 * cols), BF16), ((t, hp * m), BF16), ((t, hp * m), F32), ((t, cols), BF16), ((1, hp * m), F32)],
        [*xs, *kvs, om],
        8 * flop,
    )
    total, _ = lax.optimization_barrier((total, query_rows))
    own, send = call(functools.partial(summary_kernel, hp), summary_out, [key_feat, val, total], 0)
    summary = to_all(own, send, far_first)
    query_rows, _ = lax.optimization_barrier((query_rows, val))
    qs = [near, nearest] + swapped(query_rows)
    wq_full, query_feat, query_sig = call(
        functools.partial(query_kernel, g, n_sub, len(qs), hp, width),
        [((width, cols), BF16), ((t, hp * m), BF16), ((t, hp * m), F32)],
        [*xs, *qs, om],
        0,
    )
    total_half, summary_half, scaled_half, norm, own, send = call(
        functools.partial(query_side_kernel, g, p, hp, m, width, loss_scale),
        [((1, hp * m), BF16), ((hp * m, hd), BF16), ((t, cols), BF16), ((t, hp), F32)] + summary_out,
        [*summary, *xs, query_feat],
        8 * flop,
    )
    summary_grad = to_all(own, send, far_last)
    (query_grad,) = call(
        functools.partial(query_grad_kernel, hp),
        [((t, cols), BF16)],
        [scaled_half, summary_half, norm, total_half, query_sig, om],
        4 * flop,
    )
    others = g // 2 - 1
    odd, key_value_grad = call(
        functools.partial(key_side_kernel, g, p, hp),
        [((others * rows, width), BF16), ((t, 2 * cols), BF16)],
        [*summary_grad, val, key_feat, key_sig, om, query_grad, wq_full, wkv_full],
        8 * flop,
    )
    got = over_seq(odd, 1)
    grads = [query_grad, key_value_grad, wq_full, wkv_full]
    (even,) = call(functools.partial(even_kernel, g), [((others * rows, width), F32)], grads, 8 * flop)
    both = (even + got.astype(F32)).astype(BF16)
    top, bottom, zero = call(
        functools.partial(near_kernel, g),
        [((rows // 2, width), BF16), ((rows // 2, width), BF16), ((rows, width), F32)],
        grads,
        0,
    )
    near_sum = jnp.concatenate([over_seq(top, 1), over_seq(bottom, 1)], axis=0)
    out = zero + near_sum.astype(F32)
    for k in range(2, g, 2):
        at = (k // 2 - 1) * rows
        out = out + over_seq(both[at : at + rows], k).astype(F32)
    return out.astype(BF16)


def solution(mesh):
    in_specs = (
        P(("grp", "seq", "sub"), None),
        P(("grp", "seq", "sub")),
        P(("grp", "seq", "sub"), None),
        P("sub", None),
        P("sub", None),
        P("sub", None),
        P(),
    )
    out_specs = P(("grp", "seq", "sub"), None)
    return jax.shard_map(local, mesh=mesh, in_specs=in_specs, out_specs=out_specs, check_vma=False)
```

```python
import functools
import math

import jax
import jax.numpy as jnp
from jax import lax
from jax.experimental import pallas as pl
from jax.experimental.pallas import tpu as pltpu
from jax.sharding import PartitionSpec as P

F32 = jnp.float32
BF16 = jnp.bfloat16
HBM = pl.BlockSpec(memory_space=pltpu.HBM)


def dot(a, b, ca=1, cb=0):
    return lax.dot_general(a, b, (((ca,), (cb,)), ((), ())), preferred_element_type=F32)


def soft_and_sigmoid(u):
    e = jnp.exp(-jnp.abs(u))
    series = e * (1.0 + e * (-0.5 + e * (1.0 / 3.0)))
    soft = jnp.maximum(u, 0.0) + jnp.where(e < 1e-3, series, jnp.log(1.0 + e))
    r = 1.0 / (1.0 + e)
    return soft, jnp.where(u >= 0.0, r, e * r)


def call(body, outs, args, flops, vmem=24, **kw):
    nbytes = sum(a.size * a.dtype.itemsize for a in args) if flops else 0
    return pl.pallas_call(
        body,
        out_shape=[jax.ShapeDtypeStruct(s, d) for s, d in outs],
        compiler_params=pltpu.CompilerParams(vmem_limit_bytes=int(vmem * 2**20)),
        cost_estimate=pl.CostEstimate(flops=flops, bytes_accessed=nbytes, transcendentals=0),
        **kw,
    )(*args)


def weight_kernel(g, cols, *refs):
    ws, (near, far, far_query), sems = refs[:3], refs[3:6], refs[6]
    mine = lax.axis_index("seq") % g
    at = pl.ds(pl.multiple_of(mine * cols, cols), cols)
    size = far.shape[0]
    rows = slice(None)
    if size < near.shape[0]:
        rows = pl.ds(pl.multiple_of(lax.axis_index("grp") * size, size), size)
    copies = []
    for i, w in enumerate(ws):
        to = slice(i * cols, (i + 1) * cols)
        copies.append((w.at[:, at], near.at[:, to]))
        copies.append((w.at[rows, at], far.at[:, to] if i < 2 else far_query))
    copies = [pltpu.make_async_copy(a, b, sems.at[i]) for i, (a, b) in enumerate(copies)]
    for c in copies:
        c.start()
    for c in copies:
        c.wait()


def input_kernel(g, cols, events, offsets, frequency, cot, *bufs):
    mine = (lax.axis_index("seq") % g) // 2
    tokens, width = events.shape
    half = width // 2
    lanes = 128
    column = jnp.transpose(jnp.broadcast_to(offsets[...].astype(F32), (lanes, tokens)))
    for j in range(0, half, lanes):
        angle = column * frequency[:, j : j + lanes]
        for value, start in ((jnp.sin(angle), j), (jnp.cos(angle), half + j)):
            to = slice(start, start + lanes)
            x = (events[:, to].astype(F32) + value).astype(BF16)
            for buf in bufs:
                buf[:, to] = x
    for k, buf in enumerate(bufs):
        buf[:, width:] = cot[:, pl.ds(pl.multiple_of((mine ^ k) * 2 * cols, 2 * cols), 2 * cols)]


def place_rows(full, parts, n, start):
    z = lax.axis_index("sub")
    rows, cols = parts[0].shape[0], full.shape[1]
    full[pl.ds(pl.multiple_of(z * rows, rows), rows), :] = parts[0][:, start : start + cols]
    full[pl.ds(pl.multiple_of((z ^ 1) * rows, rows), rows), :] = parts[1][:, start : start + cols]
    far = parts[2:]
    halves = len(far) // (n - 2)
    size = rows // halves
    for i, part in enumerate(far):
        k = 2 + i // halves
        where = (z ^ k) * rows
        if halves == 2:
            mine = lax.axis_index("grp") * size
            where = where + (size - mine if i % 2 else mine)
        full[pl.ds(pl.multiple_of(where, size), size), :] = part[...]


def features(act, om, h, i, feat, sig):
    hd, m = om.shape[1], om.shape[2]
    rows = act.shape[0]
    soft, s = soft_and_sigmoid(dot(act[:, h * hd : (h + 1) * hd], om[h]))
    soft = soft.astype(BF16)
    at = (slice(i * rows, (i + 1) * rows), slice(h * m, (h + 1) * m))
    feat[at] = soft
    sig[at] = s
    return soft


def put_total(own, send, base, extra, total):
    hd = own.shape[1]
    n = total.shape[1] // hd
    for j in range(n):
        piece = total[:, j * hd : (j + 1) * hd]
        high = piece.astype(BF16)
        own[base + j : base + j + 1, :] = piece
        send[base + j : base + j + 1, :] = high
        own[base + extra + j : base + extra + j + 1, :] = jnp.zeros_like(piece)
        send[base + extra + j : base + extra + j + 1, :] = (piece - high.astype(F32)).astype(BF16)


def get_total(tail, extra, h, m):
    hd = tail.shape[1]
    n = m // hd
    rows = [
        tail[h * n + j : h * n + j + 1, :] + tail[extra + h * n + j : extra + h * n + j + 1, :]
        for j in range(n)
    ]
    return jnp.concatenate(rows, axis=1)


def summed(parts, lo, hi):
    out = parts[0][lo:hi, :]
    for part in parts[1:]:
        out = out + part[lo:hi, :].astype(F32)
    return out


def key_value_kernel(g, n, nw, hp, width, *refs):
    xs, ws, om = refs[:g], refs[g : g + nw], refs[g + nw]
    w_full, feat, sig, val, total = refs[g + nw + 1 :]
    hd, m = om.shape[1], om.shape[2]
    cols = hp * hd
    place_rows(w_full, ws, n, 0)
    rows = xs[0].shape[0]
    sums = [jnp.zeros((1, m), F32) for _ in range(hp)]
    for i, x in enumerate(xs):
        act = dot(x[:, :width], w_full[...]).astype(BF16)
        val[i * rows : (i + 1) * rows, :] = act[:, cols:]
        for h in range(hp):
            soft = features(act, om, h, i, feat, sig)
            sums[h] = sums[h] + jnp.sum(soft.astype(F32), axis=0, keepdims=True)
    total[...] = jnp.concatenate(sums, axis=1)


def summary_kernel(hp, feat, val, total, own, send):
    m, hd = feat.shape[1] // hp, val.shape[1] // hp
    base = hp * m
    own[base:, :] = jnp.zeros_like(own[base:, :])
    send[base:, :] = jnp.zeros_like(send[base:, :])
    for h in range(hp):
        s = dot(feat[:, h * m : (h + 1) * m], val[:, h * hd : (h + 1) * hd], 0, 0)
        own[h * m : (h + 1) * m, :] = s
        send[h * m : (h + 1) * m, :] = s.astype(BF16)
    put_total(own, send, base, hp * m // hd, total[...])


def query_kernel(g, n, nw, hp, width, *refs):
    xs, ws, om = refs[:g], refs[g : g + nw], refs[g + nw]
    w_full, feat, sig = refs[g + nw + 1 :]
    place_rows(w_full, ws, n, 2 * w_full.shape[1])
    for i, x in enumerate(xs):
        act = dot(x[:, :width], w_full[...]).astype(BF16)
        for h in range(hp):
            features(act, om, h, i, feat, sig)


def query_side_kernel(g, p, hp, m, width, loss_scale, *refs):
    parts, xs, feat = refs[:p], refs[p : p + g], refs[p + g]
    total_half, summary_half, scaled_half, norm, own, send = refs[p + g + 1 :]
    hd = summary_half.shape[1]
    cols = hp * hd
    base = hp * m
    extra = base // hd
    summary_half[...] = summed(parts, 0, base).astype(BF16)
    tail = summed(parts, base, parts[0].shape[0])
    core = lax.axis_index("seq") % 2
    rows = xs[0].shape[0]
    own[base:, :] = jnp.zeros_like(own[base:, :])
    send[base:, :] = jnp.zeros_like(send[base:, :])
    sums = []
    for h in range(hp):
        row = get_total(tail, extra, h, m).astype(BF16)
        total_half[:, h * m : (h + 1) * m] = row
        spread = jnp.broadcast_to(row.astype(F32), (hd, m)).astype(BF16)
        acc = jnp.zeros((1, m), F32)
        for i in range(g):
            tok = slice(i * rows, (i + 1) * rows)
            qf = feat[tok, h * m : (h + 1) * m]
            at = pl.multiple_of(width + core * cols + h * hd, hd)
            denom = dot(qf, spread, 1, 1)
            numer = dot(qf, summary_half[h * m : (h + 1) * m, :])
            scaled = xs[i][:, pl.ds(at, hd)].astype(F32) * loss_scale / denom
            scaled_half[tok, h * hd : (h + 1) * hd] = scaled.astype(BF16)
            ng = -jnp.sum(scaled * (numer / denom), axis=1, keepdims=True)
            norm[tok, h : h + 1] = ng
            acc = acc + jnp.sum(qf.astype(F32) * ng.astype(BF16).astype(F32), axis=0, keepdims=True)
        s = dot(feat[:, h * m : (h + 1) * m], scaled_half[:, h * hd : (h + 1) * hd], 0, 0)
        own[h * m : (h + 1) * m, :] = s
        send[h * m : (h + 1) * m, :] = s.astype(BF16)
        sums.append(acc)
    put_total(own, send, base, extra, jnp.concatenate(sums, axis=1))


def query_grad_kernel(g, hp, scaled_half, summary_half, norm, total_half, sig, om, wq, out, part):
    hd, m = om.shape[1], om.shape[2]
    for h in range(hp):
        fg = dot(scaled_half[:, h * hd : (h + 1) * hd], summary_half[h * m : (h + 1) * m, :], 1, 1)
        fg = fg + norm[:, h : h + 1] * total_half[:, h * m : (h + 1) * m].astype(F32)
        pg = (fg * sig[:, h * m : (h + 1) * m]).astype(BF16)
        out[:, h * hd : (h + 1) * hd] = dot(pg, om[h], 1, 1).astype(BF16)
    part[...] = dot(out[out.shape[0] // g * 2 :, :], wq[...], 1, 1)


def products(g, blocks, qg, kvg, wq, wkv, out):
    rows = qg.shape[0] // g
    for j, i in enumerate(blocks):
        tok = slice(i * rows, (i + 1) * rows)
        o = dot(qg[tok, :], wq[...], 1, 1) + dot(kvg[tok, :], wkv[...], 1, 1)
        out[j * rows : (j + 1) * rows, :] = o.astype(out.dtype)


def far_products(g, blocks, part, kvg, wkv, out):
    rows = kvg.shape[0] // g
    for j, i in enumerate(blocks):
        o = part[(i - 2) * rows : (i - 1) * rows, :] + dot(kvg[i * rows : (i + 1) * rows, :], wkv[...], 1, 1)
        out[j * rows : (j + 1) * rows, :] = o.astype(out.dtype)


def key_side_kernel(g, p, hp, *refs):
    parts = refs[:p]
    val, feat, sig, om, part, wkv = refs[p : p + 6]
    odd, kvg = refs[p + 6 :]
    hd, m = om.shape[1], om.shape[2]
    base = hp * m
    cols = hp * hd
    tail = summed(parts, base, parts[0].shape[0])
    for h in range(hp):
        gh = summed(parts, h * m, (h + 1) * m).astype(BF16)
        col = slice(h * hd, (h + 1) * hd)
        fg = dot(val[:, col], gh, 1, 1) + get_total(tail, base // hd, h, m)
        kvg[:, cols + h * hd : cols + (h + 1) * hd] = dot(feat[:, h * m : (h + 1) * m], gh).astype(BF16)
        pg = (fg * sig[:, h * m : (h + 1) * m]).astype(BF16)
        kvg[:, col] = dot(pg, om[h], 1, 1).astype(BF16)
    far_products(g, range(3, g, 2), part, kvg, wkv, odd)


def even_kernel(g, part, kvg, wkv, even):
    far_products(g, range(2, g, 2), part, kvg, wkv, even)


def near_kernel(g, qg, kvg, wq, wkv, top, bottom, zero):
    rows = zero.shape[0]
    half = rows // 2
    for start, out in ((rows, top), (rows + half, bottom)):
        tok = slice(start, start + half)
        o = dot(qg[tok, :], wq[...], 1, 1) + dot(kvg[tok, :], wkv[...], 1, 1)
        out[...] = o.astype(out.dtype)
    products(g, [0], qg, kvg, wq, wkv, zero)


def local(events, offsets, cotangent, query_weight, key_weight, value_weight, omega):
    heads, hd, m = omega.shape
    n_seq, n_sub = lax.axis_size("seq"), lax.axis_size("sub")
    rows, width = events.shape
    loss_scale = math.sqrt(rows * n_seq * n_sub)
    g = math.gcd(heads, n_seq)
    r = n_seq // g
    hp = heads // g
    p = r * n_sub
    t = g * rows
    cols = hp * hd
    srows = hp * m + -(-2 * hp * m // hd // 16) * 16

    def over_seq(x, k):
        return lax.ppermute(x, "seq", [(i, i ^ k) for i in range(n_seq)])

    def over_sub(x, k):
        return lax.ppermute(x, "sub", [(i, i ^ k) for i in range(n_sub)])

    far_first = [*range(n_sub - 2, -1, -1), n_sub - 1]
    far_last = [n_sub - 1, *range(n_sub - 1)]

    def to_all(own, send, order):
        parts = [own]
        for j in range(r):
            for k in order:
                if j or k:
                    perm = [
                        (a * n_sub + b, (a ^ (j * g)) * n_sub + (b ^ k))
                        for a in range(n_seq)
                        for b in range(n_sub)
                    ]
                    parts.append(lax.ppermute(send, ("seq", "sub"), perm))
        return parts

    wrows = key_weight.shape[0]
    split = lax.axis_size("grp") == 2 and wrows % 32 == 0
    size = wrows // 2 if split else wrows
    wouts = [((wrows, 3 * cols), BF16), ((size, 2 * cols), BF16), ((size, cols), BF16)]
    frequency = jnp.exp(jnp.arange(width // 2, dtype=F32) * (-2.0 * math.log(10000.0) / width))
    near, far, far_query = call(
        functools.partial(weight_kernel, g, cols),
        wouts,
        [key_weight, value_weight, query_weight],
        0,
        vmem=53,
        in_specs=[HBM] * 3,
        scratch_shapes=[pltpu.SemaphoreType.DMA((6,))],
    )
    frequency, _ = lax.optimization_barrier((frequency, near))
    bufs = call(
        functools.partial(input_kernel, g, cols),
        [((rows, width + 2 * cols), BF16)] * (g // 2),
        [events, offsets[None], frequency[None], cotangent],
        0,
    )

    def swapped(parts):
        if not split:
            return parts
        return [x for part in parts for x in (part, lax.ppermute(part, "grp", [(0, 1), (1, 0)]))]

    nearest = over_sub(near, 1)
    arrived = [over_sub(far, k) for k in range(2, n_sub)]
    kvs = [near, nearest] + swapped(arrived)
    xs = [bufs[0]] * g
    for k in range(2, g, 2):
        xs[k] = over_seq(bufs[k // 2], k)
    xs[1] = over_seq(bufs[0], 1)
    xs[2:], _ = lax.optimization_barrier((xs[2:], arrived))
    for k in range(3, g, 2):
        xs[k] = over_seq(xs[k ^ 1], 1)
    far_query, _ = lax.optimization_barrier((far_query, arrived + xs[1:2]))
    query_rows = [over_sub(far_query, k) for k in range(2, n_sub)]
    om = lax.dynamic_slice_in_dim(omega, (lax.axis_index("seq") % g) * hp, hp, 0)

    flop = 2 * t * width * cols
    summary_out = [((srows, hd), F32), ((srows, hd), BF16)]
    wkv_full, key_feat, key_sig, val, total = call(
        functools.partial(key_value_kernel, g, n_sub, len(kvs), hp, width),
        [((width, 2 * cols), BF16), ((t, hp * m), BF16), ((t, hp * m), F32), ((t, cols), BF16), ((1, hp * m), F32)],
        [*xs, *kvs, om],
        8 * flop,
    )
    total, _ = lax.optimization_barrier((total, query_rows))
    own, send = call(functools.partial(summary_kernel, hp), summary_out, [key_feat, val, total], 0)
    summary = to_all(own, send, far_first)
    query_rows, _ = lax.optimization_barrier((query_rows, val))
    qs = [near, nearest] + swapped(query_rows)
    wq_full, query_feat, query_sig = call(
        functools.partial(query_kernel, g, n_sub, len(qs), hp, width),
        [((width, cols), BF16), ((t, hp * m), BF16), ((t, hp * m), F32)],
        [*xs, *qs, om],
        0,
    )
    total_half, summary_half, scaled_half, norm, own, send = call(
        functools.partial(query_side_kernel, g, p, hp, m, width, loss_scale),
        [((1, hp * m), BF16), ((hp * m, hd), BF16), ((t, cols), BF16), ((t, hp), F32)] + summary_out,
        [*summary, *xs, query_feat],
        8 * flop,
    )
    summary_grad = to_all(own, send, far_last)
    query_grad, query_part = call(
        functools.partial(query_grad_kernel, g, hp),
        [((t, cols), BF16), ((t - 2 * rows, width), F32)],
        [scaled_half, summary_half, norm, total_half, query_sig, om, wq_full],
        4 * flop,
    )
    others = g // 2 - 1
    odd, key_value_grad = call(
        functools.partial(key_side_kernel, g, p, hp),
        [((others * rows, width), BF16), ((t, 2 * cols), BF16)],
        [*summary_grad, val, key_feat, key_sig, om, query_part, wkv_full],
        8 * flop,
    )
    got = over_seq(odd, 1)
    grads = [query_grad, key_value_grad, wq_full, wkv_full]
    (even,) = call(
        functools.partial(even_kernel, g),
        [((others * rows, width), F32)],
        [query_part, key_value_grad, wkv_full],
        8 * flop,
    )
    both = (even + got.astype(F32)).astype(BF16)
    top, bottom, zero = call(
        functools.partial(near_kernel, g),
        [((rows // 2, width), BF16), ((rows // 2, width), BF16), ((rows, width), F32)],
        grads,
        0,
    )
    near_sum = jnp.concatenate([over_seq(top, 1), over_seq(bottom, 1)], axis=0)
    out = zero + near_sum.astype(F32)
    for k in range(2, g, 2):
        at = (k // 2 - 1) * rows
        out = out + over_seq(both[at : at + rows], k).astype(F32)
    return out.astype(BF16)


def solution(mesh):
    in_specs = (
        P(("grp", "seq", "sub"), None),
        P(("grp", "seq", "sub")),
        P(("grp", "seq", "sub"), None),
        P("sub", None),
        P("sub", None),
        P("sub", None),
        P(),
    )
    out_specs = P(("grp", "seq", "sub"), None)
    return jax.shard_map(local, mesh=mesh, in_specs=in_specs, out_specs=out_specs, check_vma=False)
```
